32 devices in a mesh: groups: 2 (over y), seq: 16 (over z, x, core).
Axes of the slice: x: 2, y: 2, z: 4, core: 2. Of those that a mesh axis runs over, the one named last changes fastest.
Arguments:
- xbc: bfloat16 [16384, 2304], P(('groups', 'seq')), parts along dimension 0, may hold values from -24 to 24
- conv_weight: float32 [4, 2304], replicated, may hold values from -3 to 3
- log_decay: float32 [16, 16384], P(None, ('groups', 'seq')), parts along dimension 1, may hold values from -1 to 0, as said below
- level_weights: float32 [16, 14, 16384], P(None, None, ('groups', 'seq')), parts along dimension 2, may hold values from 0.1 to 1
- gain: float32 [2048], replicated, may hold values from 0.25 to 1.75
Outputs:
- mixed: bfloat16 [16384, 2048], P(('groups', 'seq')), parts along dimension 0
The draws below stay inside these ranges and needn't reach their ends.
There are 2 independent parts, one for each index of `groups`. The reference program is written for one: setup_inputs(seed, part) draws one part's arguments, and reference() takes and returns one part's arrays. A program takes and returns all parts, laid end to end along the dimension named above; an argument that names none is the same for every part. Nothing has to cross between parts.
Inputs may be any that keep to these rules, and one draw needn't show every extreme that they name: `log_decay`: every entry is negative.
All inputs are finite; a program needn't handle non-finite values.
Results may differ from the reference program's by a relative error of at most 0.0034.
Values may be sent and summed in bfloat16 or wider, within the bound.
No kernel may reach another device: no remote copies, remote signals or barrier semaphores. Data moves between devices by JAX's collectives and lax.ppermute only.
A program may use at most 128 MiB of HBM per device.

```python
import math
import jax
import jax.numpy as jnp
from jax import lax

PAIRED_MIXER_NUM = 16
HEAD_DIM = 128
STATE = 128
KERNEL = 4
TOK_DEV = 512
INNER = 2048
WIDTH = 2304
STEP_AMOUNT = 8192
LOG_TOK = 9
LOG_SEQ = 4
LEVELS = 14


def draw_xbc(key, part):
    key_base, key_cols, key_rows = jax.random.split(key, 3)
    col_scale = jnp.exp(jax.random.uniform(key_cols, (1, WIDTH), jnp.float32, math.log(0.4), math.log(4.0)))
    row_scale = jnp.exp(jax.random.uniform(key_rows, (STEP_AMOUNT, 1), jnp.float32, math.log(0.5), math.log(2.0)))
    entries = jax.random.normal(key_base, (STEP_AMOUNT, WIDTH), jnp.float32) * col_scale * row_scale
    return jnp.clip(entries, -24.0, 24.0).astype(jnp.bfloat16)


def draw_log_decay(key, part):
    lookup_vectors = jax.random.split(key, 9)
    head_kind = jax.random.randint(lookup_vectors[0], (PAIRED_MIXER_NUM, 1), 0, 4)
    fast_rate = jnp.exp(jax.random.uniform(lookup_vectors[2], (PAIRED_MIXER_NUM, 1), jnp.float32, math.log(1.0 / 50.0), math.log(1.0 / 30.0)))
    medium_rate = jnp.exp(jax.random.uniform(lookup_vectors[3], (PAIRED_MIXER_NUM, 1), jnp.float32, math.log(0.5), math.log(2.0))) / TOK_DEV
    slow_rate = jnp.exp(jax.random.uniform(lookup_vectors[4], (PAIRED_MIXER_NUM, 1), jnp.float32, math.log(0.1), math.log(0.4))) / STEP_AMOUNT
    channel_forget_factor = jnp.where(head_kind == 0, fast_rate, jnp.where(head_kind == 1, medium_rate, slow_rate))
    segment_factor = jnp.exp(jax.random.uniform(lookup_vectors[5], (PAIRED_MIXER_NUM, STEP_AMOUNT // TOK_DEV), jnp.float32, math.log(0.5), math.log(2.0)))
    segment_factor = jnp.repeat(segment_factor, TOK_DEV, axis=1)
    element_factor = jnp.exp(jax.random.uniform(lookup_vectors[6], (PAIRED_MIXER_NUM, STEP_AMOUNT), jnp.float32, math.log(0.5), math.log(2.0)))
    segment_offset = jax.random.randint(lookup_vectors[7], (PAIRED_MIXER_NUM, 3, 1), 0, STEP_AMOUNT)
    segment_size = jax.random.uniform(lookup_vectors[8], (PAIRED_MIXER_NUM, 3, 1), jnp.float32, 0.22, 0.5)
    element_index = lax.iota(jnp.int32, STEP_AMOUNT)[None, None, :]
    segment_list = jnp.sum(jnp.where(element_index == segment_offset, segment_size, 0.0), axis=1)
    return -(channel_forget_factor * segment_factor * element_factor + segment_list)


def steps_of(key, shape, cuts, least, largest):
    loudness, own = 1.0, jax.random.fold_in(key, 6)
    for dim, parts in cuts:
        heights = jnp.exp(jax.random.uniform(jax.random.fold_in(own, dim), (parts,), jnp.float32, least / len(cuts), largest / len(cuts)))
        loudness = loudness * jnp.repeat(heights, shape[dim] // parts).reshape([-1 if axis == dim else 1 for axis in range(len(shape))])
    return loudness


def gaussian(rng, extent, spread, most, held_as=jnp.bfloat16):
    drawn = jax.random.normal(rng, extent, jnp.float32) * spread
    return jnp.minimum(jnp.maximum(drawn, -most), most).astype(held_as)


def setup_inputs(seed: int = 0, part: int = 0) -> dict:
    keys = jax.random.split(jax.random.key(seed), 6)
    own_keys = jax.random.split(jax.random.fold_in(keys[5], part), 6)
    return {
        "xbc": draw_xbc(jax.random.fold_in(jax.random.fold_in(keys[5], part), 71), part),
        "conv_weight": gaussian(keys[1], (KERNEL, WIDTH), KERNEL ** -0.5, 3.0, jnp.float32),
        "log_decay": draw_log_decay(jax.random.fold_in(jax.random.fold_in(keys[5], part), 71), part),
        "level_weights": jnp.clip(jnp.exp(math.log(1.0) - 2.3025851 * jax.random.uniform(own_keys[3], (PAIRED_MIXER_NUM, LEVELS, STEP_AMOUNT), jnp.float32) ** steps_of(own_keys[3], (PAIRED_MIXER_NUM, LEVELS, STEP_AMOUNT), ((2, 16),), -0.2, 0.2)), 0.1, 1.0),
        "gain": jnp.clip(1.0 + 0.15 * jax.random.normal(keys[4], (INNER,), jnp.float32), 0.25, 1.75),
    }


def bit_length(numbers, limit):
    counted = jnp.zeros(numbers.shape, jnp.int32)
    for power_index in range(limit):
        counted = counted + (numbers >= 1 << power_index).astype(jnp.int32)
    return counted

def compute_near(values_rows, in_map, out_map, local_log, level_gain, head_count):
    row_count = values_rows.shape[0]
    head_dim = values_rows.shape[1] // head_count
    local_bits = row_count.bit_length() - 1
    scores = jnp.dot(out_map, in_map.T, preferred_element_type=jnp.float32)
    element_index = lax.iota(jnp.int32, row_count)
    level_index = bit_length(jnp.bitwise_xor(element_index[:, None], element_index[None, :]), local_bits)
    causal = element_index[None, :] <= element_index[:, None]
    chosen = jnp.zeros((head_count, row_count, row_count), jnp.float32)
    for level_step in range(local_bits + 1):
        chosen = jnp.where((level_index == level_step)[None], level_gain[:, level_step, :, None], chosen)
    gap_log = jnp.where(causal[None], local_log[:, :, None] - local_log[:, None, :], -1e+30)
    weight = (chosen * jnp.exp(gap_log) * scores[None]).astype(jnp.bfloat16)
    shaped = values_rows.reshape(row_count, head_count, head_dim).astype(jnp.float32)
    near_heads = jnp.einsum('hts,shp->thp', weight.astype(jnp.float32), shaped)
    return near_heads.reshape(row_count, head_count * head_dim)

def reference(xbc, conv_weight, log_decay, level_weights, gain):
    inner_width = PAIRED_MIXER_NUM * HEAD_DIM
    blocks = STEP_AMOUNT // TOK_DEV
    padded = jnp.concatenate([jnp.zeros((KERNEL - 1, xbc.shape[1]), jnp.float32), xbc.astype(jnp.float32)], axis=0)
    convolved = padded[0:STEP_AMOUNT] * conv_weight[0]
    for offset in range(1, KERNEL):
        convolved = convolved + padded[offset:offset + STEP_AMOUNT] * conv_weight[offset]
    activated = jax.nn.silu(convolved).astype(jnp.bfloat16)
    values_all = activated[:, :inner_width].reshape(blocks, TOK_DEV, inner_width)
    in_all = activated[:, inner_width:inner_width + STATE].reshape(blocks, TOK_DEV, STATE)
    out_all = activated[:, inner_width + STATE:].reshape(blocks, TOK_DEV, STATE)
    local_log = jnp.cumsum(log_decay.reshape(PAIRED_MIXER_NUM, blocks, TOK_DEV), axis=2)
    block_total = local_log[:, :, TOK_DEV - 1]
    inclusive = jnp.cumsum(block_total, axis=1)
    before = inclusive - block_total

    def state_of(pieces):
        values_block, in_block, log_block, total_block = pieces
        tail_decay = jnp.exp(total_block[:, None] - log_block)
        decayed = (values_block.reshape(TOK_DEV, PAIRED_MIXER_NUM, HEAD_DIM) * tail_decay.T[:, :, None]).reshape(TOK_DEV, inner_width).astype(jnp.bfloat16)
        return jnp.dot(in_block.T, decayed, preferred_element_type=jnp.float32)
    states = lax.map(state_of, (values_all, in_all, local_log.transpose(1, 0, 2), block_total.T))
    group_list = []
    for level_index in range(1, LOG_SEQ + 1):
        group_span = 2 ** (level_index - 1)
        group_count = blocks // group_span
        grouped = states.reshape(group_count, group_span, STATE, PAIRED_MIXER_NUM, HEAD_DIM)
        ends_log = inclusive.reshape(PAIRED_MIXER_NUM, group_count, group_span)
        weight = jnp.exp(ends_log[:, :, group_span - 1:group_span] - ends_log)
        level_node = jnp.einsum('hgm,gmnhp->gnhp', weight, grouped, precision=lax.Precision.HIGHEST)
        group_list.append((level_node.reshape(group_count, STATE, inner_width), ends_log[:, :, group_span - 1]))

    def output_of(pieces):
        block_index, values_block, in_block, out_block, log_block, gain_block, start_log = pieces
        near_term = compute_near(values_block, in_block, out_block, log_block, gain_block, PAIRED_MIXER_NUM)
        far_term = jnp.zeros((TOK_DEV, inner_width), jnp.float32)
        queries_wide = out_block.astype(jnp.float32)
        for level_index in range(1, LOG_SEQ + 1):
            node_all, group_ends = group_list[level_index - 1]
            is_upper = block_index >> level_index - 1 & 1 == 1
            group_slot = jnp.maximum((block_index >> level_index - 1) - 1, 0).astype(jnp.int32)
            level_node = node_all[group_slot]
            gap_log = start_log - group_ends[:, group_slot]
            exponent = jnp.where(is_upper, log_block + gap_log[:, None], -1e+30)
            factor = gain_block[:, LOG_TOK + level_index, :] * jnp.exp(exponent)
            product = jnp.dot(queries_wide, level_node, precision=lax.Precision.HIGHEST)
            far_term = far_term + (product.reshape(TOK_DEV, PAIRED_MIXER_NUM, HEAD_DIM) * factor.T[:, :, None]).reshape(TOK_DEV, inner_width)
        mixed_sum = (near_term + far_term).reshape(TOK_DEV, PAIRED_MIXER_NUM, HEAD_DIM)
        inv_rms = lax.rsqrt(lax.optimization_barrier(jnp.mean(mixed_sum * mixed_sum, axis=2, keepdims=True)) + 1e-05)
        return ((mixed_sum * inv_rms).reshape(TOK_DEV, inner_width) * gain).astype(jnp.bfloat16)
    gains_blocks = level_weights.reshape(PAIRED_MIXER_NUM, LEVELS, blocks, TOK_DEV).transpose(2, 0, 1, 3)
    result = lax.map(output_of, (jnp.arange(blocks, dtype=jnp.int32), values_all, in_all, out_all, local_log.transpose(1, 0, 2), gains_blocks, before.T))
    return result.reshape(STEP_AMOUNT, inner_width)
```

```python
import functools

import jax
import jax.numpy as jnp
from jax import lax
from jax.experimental import pallas as pl
from jax.experimental.pallas import tpu as pltpu
from jax.sharding import PartitionSpec as P

F32 = jnp.float32
BF16 = jnp.bfloat16
LANES = 128
GROUP = 8
PARTS = 3
VMEM_LIMIT = 24 << 20
HBM_SPEC = pl.BlockSpec(memory_space=pltpu.HBM)
VMEM_SPEC = pl.BlockSpec(memory_space=pltpu.VMEM)


def in_vmem(*arrays):
    return [pltpu.with_memory_space_constraint(array, pltpu.VMEM) for array in arrays]


def in_hbm(*arrays):
    return [pltpu.with_memory_space_constraint(array, pltpu.HBM) for array in arrays]


def params():
    return pltpu.CompilerParams(vmem_limit_bytes=VMEM_LIMIT)


def product(left, right):
    return jnp.dot(left, right, preferred_element_type=F32)


def write_spans(message_ref, first_row, spans):
    head_count = spans.shape[0]
    for part in range(PARTS):
        rounded = spans.astype(BF16)
        start = first_row + part * head_count
        message_ref[start : start + head_count, :] = rounded
        spans = spans - rounded.astype(F32)


def read_spans(message_ref, first_row, head_count):
    total = None
    for part in range(PARTS):
        start = first_row + part * head_count
        piece = message_ref[start : start + head_count, :].astype(F32)
        total = piece if total is None else total + piece
    return total


def running_sum(logs):
    column = lax.broadcasted_iota(jnp.int32, logs.shape, 1)
    shift = 1
    while shift < logs.shape[1]:
        logs = logs + jnp.where(column >= shift, pltpu.roll(logs, shift, 1), 0.0)
        shift *= 2
    return logs


def front_kernel(
    xbc_hbm, edge_ref, taps_hbm, decay_hbm, acts_ref, maps_ref, state_ref, message_ref, log_ref,
    xbc_buf, taps_buf, decay_buf, padded, sems, small_sems, chunk
):
    rows, width = xbc_buf.shape
    taps = taps_buf.shape[0]
    head_count = decay_buf.shape[0]
    state_size = maps_ref.shape[1]
    steps = width // chunk
    small = [
        pltpu.make_async_copy(decay_hbm, decay_buf, small_sems.at[0]),
        pltpu.make_async_copy(taps_hbm, taps_buf, small_sems.at[1]),
    ]
    copies = []
    for step in range(steps):
        part = pl.ds(step * chunk, chunk)
        copies.append(
            pltpu.make_async_copy(xbc_hbm.at[:, part], xbc_buf.at[:, part], sems.at[step])
        )
    for copy in small + copies[-1:] + copies[:-1]:
        copy.start()

    def activated(start):
        part = pl.ds(start, chunk)
        weights = taps_buf[:, part]
        values = xbc_buf[:, part].astype(F32)
        padded[GROUP : GROUP + rows, :] = values
        padded[GROUP - taps + 1 : GROUP, :] = edge_ref[:, part].astype(F32)
        total = None
        for tap in range(taps):
            first = GROUP - taps + 1 + tap
            shifted = values if tap == taps - 1 else padded[first : first + rows, :]
            term = shifted * weights[tap : tap + 1]
            total = term if total is None else total + term
        return (total / (1.0 + jnp.exp(-total))).astype(BF16)

    small[0].wait()
    local_log = running_sum(decay_buf[...])
    log_ref[...] = local_log
    totals = jnp.broadcast_to(local_log[:, rows - 1 : rows], (head_count, LANES))
    write_spans(message_ref, state_ref.shape[0], totals)
    small[1].wait()
    copies[-1].wait()
    last = activated(width - chunk)
    maps_ref[...] = last[:, :state_size]
    acts_ref[width - chunk :, :] = last.T
    per_chunk = chunk // state_size

    for step in range(steps - 1):
        copies[step].wait()
        turned = activated(step * chunk).T
        acts_ref[step * chunk : (step + 1) * chunk, :] = turned
        for part in range(per_chunk):
            head = step * per_chunk + part
            logs = log_ref[head : head + 1, :]
            tail = jnp.exp(logs[:, rows - 1 : rows] - logs)
            own = turned[part * LANES : (part + 1) * LANES].astype(F32)
            decayed = (own * tail).astype(BF16)
            state = product(decayed, maps_ref[...])
            state_ref[head * LANES : (head + 1) * LANES, :] = state
            message_ref[head * LANES : (head + 1) * LANES, :] = state.astype(BF16)


def front(xbc, edge, conv_weight, log_decay):
    rows, width = xbc.shape
    taps = conv_weight.shape[0]
    head_count = log_decay.shape[0]
    inner = head_count * LANES
    state_size = (width - inner) // 2
    chunk = 2 * state_size
    return pl.pallas_call(
        functools.partial(front_kernel, chunk=chunk),
        in_specs=[HBM_SPEC, VMEM_SPEC, HBM_SPEC, HBM_SPEC],
        out_specs=[VMEM_SPEC] * 5,
        out_shape=[
            pltpu.VMEM((width, rows), BF16),
            pltpu.VMEM((rows, state_size), BF16),
            pltpu.VMEM((inner, state_size), F32),
            pltpu.VMEM((inner + PARTS * head_count, state_size), BF16),
            pltpu.VMEM((head_count, rows), F32),
        ],
        scratch_shapes=[
            pltpu.VMEM((rows, width), BF16),
            pltpu.VMEM((taps, width), F32),
            pltpu.VMEM((head_count, rows), F32),
            pltpu.VMEM((rows + GROUP, chunk), F32),
            pltpu.SemaphoreType.DMA((width // chunk,)),
            pltpu.SemaphoreType.DMA((2,)),
        ],
        compiler_params=params(),
        name="front",
    )(*in_hbm(xbc), *in_vmem(edge), *in_hbm(conv_weight, log_decay))


def pair_kernel(state_ref, log_ref, got_ref, own_ref, stats_ref, send_ref, rest_ref, shards):
    head_count, rows = log_ref.shape
    inner = state_ref.shape[0]
    index = lax.axis_index("seq")
    is_upper = index % 2 == 1
    mine = jnp.broadcast_to(log_ref[:, rows - 1 : rows], (head_count, LANES))
    theirs = read_spans(got_ref, inner, head_count)
    stats_ref[0] = mine + theirs
    stats_ref[1] = jnp.where(is_upper, theirs, 0.0)
    write_spans(send_ref, inner // shards, mine + theirs)
    write_spans(rest_ref, inner // shards, mine + theirs)
    stats_ref[2] = jnp.exp(mine)
    stats_ref[3] = jnp.exp(theirs)
    shard = index % shards
    share = head_count // shards

    def joined(head):
        at = pl.ds(pl.multiple_of(head * LANES, LANES), LANES)
        own = state_ref[at, :]
        got = got_ref[at, :].astype(F32)
        late = jnp.where(is_upper, own, got)
        early = jnp.where(is_upper, got, own)
        late_row = jnp.where(is_upper, 2, 3)
        return early * stats_ref[late_row, pl.ds(head, 1), :] + late

    for local in range(share):
        place = slice(local * LANES, (local + 1) * LANES)
        send_ref[place, :] = joined((shard ^ 2) * share + local).astype(BF16)
        kept = joined(shard * share + local)
        own_ref[place, :] = kept
        rest_ref[place, :] = kept.astype(BF16)


def pair(state, log, got, shards):
    head_count, _ = log.shape
    inner, state_size = state.shape
    part = inner // shards
    spans = PARTS * head_count
    return pl.pallas_call(
        functools.partial(pair_kernel, shards=shards),
        in_specs=[VMEM_SPEC] * 3,
        out_specs=[VMEM_SPEC] * 4,
        out_shape=[
            pltpu.VMEM((part, state_size), F32),
            pltpu.VMEM((4, head_count, LANES), F32),
            pltpu.VMEM((part + spans, state_size), BF16),
            pltpu.VMEM((part + spans, state_size), BF16),
        ],
        compiler_params=params(),
        name="pair",
    )(*in_vmem(state, log, got))


def join_kernel(own_ref, stats_ref, got_ref, _, *refs, bit, shards, gathered):
    sources = refs[:gathered]
    if gathered:
        next_stats_ref, send_ref, across_ref = refs[gathered:]
    else:
        next_stats_ref, send_ref, next_ref = refs
    part = own_ref.shape[0]
    head_count = stats_ref.shape[1]
    share = head_count // shards
    index = lax.axis_index("seq")
    is_upper = (index >> bit) % 2 == 1
    mine = stats_ref[0]
    theirs = read_spans(got_ref, part, head_count)
    next_stats_ref[0] = mine + theirs
    next_stats_ref[1] = stats_ref[1] + jnp.where(is_upper, theirs, 0.0)
    next_stats_ref[2] = jnp.exp(jnp.where(is_upper, mine, theirs))
    next_stats_ref[3] = jnp.zeros_like(mine)
    write_spans(send_ref, part, mine + theirs)
    for local in range(share):
        place = slice(local * LANES, (local + 1) * LANES)
        head = (index % shards) * share + local
        own = own_ref[place, :]
        got = got_ref[place, :].astype(F32)
        late = jnp.where(is_upper, own, got)
        early = jnp.where(is_upper, got, own)
        total = early * next_stats_ref[2, pl.ds(head, 1), :] + late
        send_ref[place, :] = total.astype(BF16)
        if not gathered:
            next_ref[place, :] = total
    for slot in range(gathered):
        across_ref[slot * part : (slot + 1) * part, :] = sources[slot][:part, :]


def join(own, stats, got, after, bit, shards, sources):
    operands = [own, stats, got, after, *sources]
    out_shape = [pltpu.VMEM(stats.shape, F32), pltpu.VMEM(got.shape, BF16)]
    if sources:
        out_shape.append(pltpu.VMEM((len(sources) * own.shape[0], own.shape[1]), BF16))
    else:
        out_shape.append(pltpu.VMEM(own.shape, F32))
    return pl.pallas_call(
        functools.partial(join_kernel, bit=bit, shards=shards, gathered=len(sources)),
        in_specs=[VMEM_SPEC] * len(operands),
        out_specs=[VMEM_SPEC] * 3,
        out_shape=out_shape,
        compiler_params=params(),
        name="join",
    )(*in_vmem(*operands))


def bit_length(numbers, limit):
    counted = jnp.zeros(numbers.shape, jnp.int32)
    for power in range(limit):
        counted = counted + (numbers >= 1 << power).astype(jnp.int32)
    return counted


def near_kernel(*refs, first, wide, heads):
    if first:
        acts_ref, maps_ref, log_ref, gains_ref, node_ref, _ = refs[:6]
        near_ref, scores, tails, turned, weights = refs[6:]
    else:
        acts_ref, maps_ref, log_ref, gains_ref, node_ref, _, scores, tails, _ = refs[:9]
        near_ref, turned, weights = refs[9:]
    head_count, rows = log_ref.shape
    inner = head_count * LANES
    state_size = maps_ref.shape[1]
    tiles = rows // LANES
    tile_bits = tiles.bit_length() - 1
    groups = LANES // GROUP
    low_bits = GROUP.bit_length() - 1
    tile_levels = LANES.bit_length() - 1
    queries = acts_ref[inner + state_size :, :]
    middle = LANES // 2 - 1
    if first:
        for start in range(0, rows, wide):
            upto = start + wide
            scores[:upto, start:upto] = product(maps_ref[:upto, :], queries[:, start:upto])
        turned[head_count:, :] = jnp.zeros((LANES - head_count, rows), F32)
        turned[:head_count, :] = log_ref[...]
        columns = [turned[:, tile * LANES : (tile + 1) * LANES].T for tile in range(tiles)]
        for tile in range(tiles):
            place = slice(tile * LANES, (tile + 1) * LANES)
            tails[0, place, :] = jnp.exp(columns[tile][middle : middle + 1] - columns[tile])
            for bit in range(tile_bits):
                if tile >> bit & 1 == 0:
                    edge = ((tile >> bit) + 1 << bit) - 1
                    tails[1 + bit, place, :] = jnp.exp(columns[edge][LANES - 1 :] - columns[tile])
    for late in range(tiles):
        for early in range(tiles):
            if early > late:
                weights[
                    :, early * LANES : (early + 1) * LANES, late * LANES : (late + 1) * LANES
                ] = jnp.zeros((weights.shape[0], LANES, LANES), BF16)
    lane = lax.broadcasted_iota(jnp.int32, (GROUP, LANES), 1)
    row = lax.broadcasted_iota(jnp.int32, (GROUP, LANES), 0)
    inside = bit_length((lane % GROUP) ^ row, low_bits)
    ahead = row <= lane % GROUP
    lane_group = lax.broadcasted_iota(jnp.int32, (groups, LANES), 1) // GROUP
    row_group = lax.broadcasted_iota(jnp.int32, (groups, LANES), 0)
    between = bit_length(lane_group ^ row_group, groups.bit_length() - 1)
    before = row_group < lane_group
    same = (
        lax.broadcasted_iota(jnp.int32, (groups, 1, LANES), 2) // GROUP
        == lax.broadcasted_iota(jnp.int32, (groups, 1, LANES), 0)
    )
    is_upper = lax.axis_index("seq") % 2 == 1

    def spread(kind, place, head):
        chosen = jnp.full((LANES, LANES), head, jnp.int32)
        return jnp.take_along_axis(
            tails[kind, place, :], chosen, axis=1, mode="promise_in_bounds"
        )

    def one_head(head, slot):
        logs = log_ref[pl.ds(head, 1), :]
        gain_rows = [
            gains_ref[pl.ds(level * head_count + head, 1), :]
            for level in range(tile_levels + tile_bits + 2)
        ]
        for late in range(tiles):
            span = slice(late * LANES, (late + 1) * LANES)
            own = logs[:, span]
            start = late * LANES + middle
            grown = jnp.exp(own - logs[:, start : start + 1])
            corner = jnp.zeros((GROUP, LANES), F32)
            for level in range(low_bits + 1):
                gain = gain_rows[level][:, span] * grown
                corner = jnp.where(ahead & (inside == level), gain, corner)
            rest = jnp.zeros((groups, LANES), F32)
            for level in range(low_bits + 1, tile_levels + 1):
                gain = gain_rows[level][:, span] * grown
                rest = jnp.where(before & (between == level - low_bits), gain, rest)
            chosen = jnp.where(same, corner[None], rest[:, None, :]).reshape(LANES, LANES)
            weight = chosen * spread(0, span, head) * scores[span, span]
            weights[slot, span, span] = weight.astype(BF16)
            for bit in range(tile_bits):
                if late >> bit & 1 == 0:
                    continue
                edge = (late >> bit << bit) * LANES - 1
                level = tile_levels + 1 + bit
                factor = gain_rows[level][:, span] * jnp.exp(
                    own - logs[:, edge : edge + 1]
                )
                for early in range(((late >> bit) - 1) << bit, (late >> bit) << bit):
                    place = slice(early * LANES, (early + 1) * LANES)
                    weight = spread(1 + bit, place, head) * factor * scores[place, span]
                    weights[slot, place, span] = weight.astype(BF16)
        at = pl.ds(pl.multiple_of(head * LANES, LANES), LANES)
        level = tile_levels + tile_bits + 1
        factor = gain_rows[level] * jnp.exp(jnp.where(is_upper, logs, -1e30))
        far = product(node_ref[at, :], queries) * factor
        for start in range(0, rows, wide):
            upto = start + wide
            near_ref[at, start:upto] = far[:, start:upto] + product(
                acts_ref[at, :upto], weights[slot, :upto, start:upto]
            )

    def some_heads(step, carry):
        for slot in range(weights.shape[0]):
            one_head(step * weights.shape[0] + slot, slot)
        return carry

    lax.fori_loop(heads[0] // weights.shape[0], heads[1] // weights.shape[0], some_heads, 0)


def near(acts, maps, log, gains, node, after, earlier, heads):
    head_count, rows = log.shape
    wide = min(rows, 2 * LANES)
    tile_bits = (rows // LANES).bit_length() - 1
    first = earlier is None
    out_shape = [pltpu.VMEM((head_count * LANES, rows), F32)]
    operands = [acts, maps, log, gains, node, after]
    aliases = {}
    if first:
        out_shape.append(pltpu.VMEM((rows, rows), F32))
        out_shape.append(pltpu.VMEM((1 + tile_bits, rows, LANES), F32))
    else:
        near_term, scores, tails = earlier
        operands += [scores, tails, near_term]
        aliases = {len(operands) - 1: 0}
    made = pl.pallas_call(
        functools.partial(near_kernel, first=first, wide=wide, heads=heads),
        in_specs=[VMEM_SPEC] * len(operands),
        out_specs=[VMEM_SPEC] * len(out_shape),
        out_shape=out_shape,
        input_output_aliases=aliases,
        scratch_shapes=[
            pltpu.VMEM((LANES, rows), F32),
            pltpu.VMEM((2, rows, rows), BF16),
        ],
        compiler_params=params(),
        cost_estimate=pl.CostEstimate(
            flops=2 * head_count * rows * rows * LANES, bytes_accessed=10 << 20, transcendentals=0
        ),
        name="near",
    )(*in_vmem(*operands))
    return [made[0], *earlier[1:]] if not first else made


def far_product(node_ref, first_row, count, queries):
    return product(node_ref[first_row : first_row + count, :], queries)


def far_factor(gains_ref, log_ref, stats_ref, head, level, base):
    is_upper = (lax.axis_index("seq") >> level) % 2 == 1
    shift = stats_ref[1, pl.ds(head, 1), :][:, :1]
    exponent = jnp.where(is_upper, log_ref[pl.ds(head, 1), :] + shift, -1e30)
    row = (base + level) * log_ref.shape[0] + head
    return gains_ref[pl.ds(row, 1), :] * jnp.exp(exponent)


def middle_kernel(*refs, places, levels, shards):
    count = len(places)
    acts_ref, log_ref, gains_ref = refs[:3]
    stats = refs[3 : 3 + count]
    sources = refs[3 + count : -2]
    total_ref = refs[-1]
    head_count, _ = log_ref.shape
    part = head_count // shards * LANES
    inner = head_count * LANES
    state_size = acts_ref.shape[0] - inner >> 1
    shard = lax.axis_index("seq") % shards
    base = gains_ref.shape[0] // head_count - levels
    queries = acts_ref[inner + state_size :, :]
    for relative in range(shards):
        terms = []
        for slot in range(count):
            source, start = places[slot][relative]
            terms.append(far_product(sources[source], start, part, queries))
        for local in range(head_count // shards):
            head = (relative ^ shard) * (head_count // shards) + local
            at = pl.ds(pl.multiple_of(head * LANES, LANES), LANES)
            total = total_ref[at, :]
            for slot in range(count):
                factor = far_factor(gains_ref, log_ref, stats[slot], head, slot + 1, base)
                total = total + terms[slot][local * LANES : (local + 1) * LANES] * factor
            total_ref[at, :] = total


def middle(near_term, acts, log, gains, stats, sources, places, levels, shards):
    operands = [acts, log, gains, *stats, *sources, near_term]
    return pl.pallas_call(
        functools.partial(middle_kernel, places=places, levels=levels, shards=shards),
        in_specs=[VMEM_SPEC] * len(operands),
        out_specs=VMEM_SPEC,
        out_shape=pltpu.VMEM(near_term.shape, F32),
        input_output_aliases={len(operands) - 1: 0},
        compiler_params=params(),
        name="middle",
    )(*in_vmem(*operands))


def last_kernel(
    total_ref, acts_ref, log_ref, gains_ref, gain_ref, stats_ref, node_a, node_b, *rest,
    starts, level, relatives, shards, base
):
    out_hbm, turned, out_buf, out_sems = rest[-4:]
    head_count, rows = log_ref.shape
    share = head_count // shards
    part = share * LANES
    inner = head_count * LANES
    state_size = acts_ref.shape[0] - inner >> 1
    shard = lax.axis_index("seq") % shards
    turned[...] = jnp.zeros_like(turned)
    turned[:head_count, :] = gain_ref[...]
    gain_columns = turned[...].T
    queries = acts_ref[inner + state_size :, :]
    copies = []
    for relative, node_ref, start in zip(relatives, (node_a, node_b), starts):
        term = far_product(node_ref, start, part, queries)
        for local in range(share):
            head = (relative ^ shard) * share + local
            at = pl.ds(pl.multiple_of(head * LANES, LANES), LANES)
            factor = far_factor(gains_ref, log_ref, stats_ref, head, level, base)
            total = total_ref[at, :] + term[local * LANES : (local + 1) * LANES] * factor
            mean = jnp.mean(total * total, axis=0, keepdims=True)
            scale = lax.rsqrt(mean + 1e-05)
            chosen = jnp.full((LANES, LANES), head, jnp.int32)
            column = jnp.take_along_axis(gain_columns, chosen, axis=1, mode="promise_in_bounds")
            column = jnp.concatenate([column] * (rows // LANES), axis=1)
            slot = len(copies)
            out_buf[slot] = (total * scale * column).astype(BF16).T
            copy = pltpu.make_async_copy(out_buf.at[slot], out_hbm.at[:, at], out_sems.at[slot])
            copy.start()
            copies.append(copy)
    for copy in copies:
        copy.wait()


def last(
    total, acts, log, gains, gain, stats, nodes, starts, level, levels, relatives, shards, mixed
):
    head_count, rows = log.shape
    count = head_count // shards * len(relatives)
    operands = in_vmem(total, acts, log, gains, gain.reshape(head_count, LANES), stats, *nodes)
    specs = [VMEM_SPEC] * len(operands)
    aliases = {}
    if mixed is not None:
        aliases = {len(operands): 0}
        operands.append(mixed)
        specs.append(HBM_SPEC)
    return pl.pallas_call(
        functools.partial(
            last_kernel, starts=starts, level=level, relatives=relatives, shards=shards,
            base=gains.shape[0] // head_count - levels,
        ),
        in_specs=specs,
        out_specs=HBM_SPEC,
        out_shape=jax.ShapeDtypeStruct((rows, head_count * LANES), BF16),
        input_output_aliases=aliases,
        scratch_shapes=[
            pltpu.VMEM((LANES, LANES), F32),
            pltpu.VMEM((count, rows, LANES), BF16),
            pltpu.SemaphoreType.DMA((count,)),
        ],
        compiler_params=params(),
        name="last",
    )(*operands)


def moved(value, apart, chosen=lambda index: True):
    devices = range(lax.axis_size("seq"))
    return lax.ppermute(value, "seq", [(i, i ^ apart) for i in devices if chosen(i)])


def on_device(xbc, conv_weight, log_decay, level_weights, gain):
    taps = conv_weight.shape[0]
    rows = xbc.shape[0]
    head_count = log_decay.shape[0]
    devices = lax.axis_size("seq")
    levels = devices.bit_length() - 1
    shards = 4
    part = head_count * LANES // shards
    gains = level_weights.transpose(1, 0, 2).reshape(-1, rows)
    behind = [(i, i + 1) for i in range(devices - 1)]
    edge = lax.ppermute(xbc[rows - taps + 1 :], "seq", behind)
    acts, maps, state, message, log = front(xbc, edge, conv_weight, log_decay)
    first_node = moved(message, 1)
    own, stats, send, rest = pair(state, log, first_node, shards)
    near_made = None
    all_stats = [stats]
    got = []
    for bit in range(1, levels - 1):
        got.append(moved(send, 1 << bit))
        if bit <= 2:
            half = head_count // 2
            heads = (half * (bit - 1), half * bit)
            near_made = near(acts, maps, log, gains, first_node, stats, near_made, heads)
        sources = [rest, *got[1:]] if bit == levels - 2 else []
        stats, send, own = join(own, stats, got[-1], near_made[0], bit, shards, sources)
        all_stats.append(stats)
    top = levels - 1

    def is_upper(index):
        return index >> top & 1 == 1

    across = moved(own, 2)
    node = moved(send, 1 << top, lambda index: index >> top & 1 == 0)
    node_across = moved(node, 2, is_upper)
    beside = moved(jnp.concatenate([*[kept[:part] for kept in got], across, node[:part]]), 1)
    count = len(got)
    places = [
        [(slot, 0), (count + 1, slot * part), (count, slot * part),
         (count + 1, (count + slot) * part)]
        for slot in range(count)
    ]
    total = middle(
        near_made[0], acts, log, gains, all_stats[:count], [*got, across, beside], places, levels,
        shards,
    )

    common = (acts, log, gains, gain, all_stats[-1])
    mixed = last(
        total, *common, (node, beside), (0, 2 * count * part), top, levels, (0, 1), shards, None
    )
    node_corner = moved(node_across, 1, is_upper)
    return last(
        total, *common, (node_across, node_corner), (0, 0), top, levels, (2, 3), shards, mixed
    )


def solution(mesh):
    in_specs = (
        P(("groups", "seq"), None),
        P(),
        P(None, ("groups", "seq")),
        P(None, None, ("groups", "seq")),
        P(),
    )
    out_specs = P(("groups", "seq"), None)
    return jax.shard_map(
        on_device, mesh=mesh, in_specs=in_specs, out_specs=out_specs, check_vma=False
    )
```

```python
import functools

import jax
import jax.numpy as jnp
from jax import lax
from jax.experimental import pallas as pl
from jax.experimental.pallas import tpu as pltpu
from jax.sharding import PartitionSpec as P

F32 = jnp.float32
BF16 = jnp.bfloat16
LANES = 128
GROUP = 8
PARTS = 4
VMEM_LIMIT = 24 << 20
HBM_SPEC = pl.BlockSpec(memory_space=pltpu.HBM)
VMEM_SPEC = pl.BlockSpec(memory_space=pltpu.VMEM)


def in_vmem(*arrays):
    return [pltpu.with_memory_space_constraint(array, pltpu.VMEM) for array in arrays]


def in_hbm(*arrays):
    return [pltpu.with_memory_space_constraint(array, pltpu.HBM) for array in arrays]


def params():
    return pltpu.CompilerParams(vmem_limit_bytes=VMEM_LIMIT)


def small_cost():
    return pl.CostEstimate(flops=1024, bytes_accessed=1024, transcendentals=0)


def product(left, right):
    return jnp.dot(left, right, preferred_element_type=F32)


def write_spans(message_ref, first_row, spans):
    head_count = spans.shape[0]
    place = lax.broadcasted_iota(jnp.int32, spans.shape, 1) // (LANES // PARTS)
    packed = jnp.zeros(spans.shape, F32)
    for part in range(PARTS - 1):
        rounded = spans.astype(BF16).astype(F32)
        packed = jnp.where(place == part, rounded, packed)
        spans = spans - rounded
    message_ref[first_row : first_row + head_count, :] = packed.astype(BF16)


def read_spans(message_ref, first_row, head_count):
    total = message_ref[first_row : first_row + head_count, :].astype(F32)
    width = LANES // PARTS
    while width < LANES:
        total = total + pltpu.roll(total, width, 1)
        width *= 2
    return total


def running_sum(logs):
    column = lax.broadcasted_iota(jnp.int32, logs.shape, 1)
    shift = 1
    while shift < logs.shape[1]:
        logs = logs + jnp.where(column >= shift, pltpu.roll(logs, shift, 1), 0.0)
        shift *= 2
    return logs


def activated(values, edge, weights, padded):
    rows = values.shape[0]
    taps = weights.shape[0]
    padded[GROUP : GROUP + rows, :] = values
    if edge is not None:
        padded[GROUP - taps + 1 : GROUP, :] = edge
    total = None
    for tap in range(taps):
        first = GROUP - taps + 1 + tap
        shifted = values if tap == taps - 1 else padded[first : first + rows, :]
        term = shifted * weights[tap : tap + 1]
        total = term if total is None else total + term
    return (total * jax.nn.sigmoid(total)).astype(BF16)


def front_kernel(
    xbc_hbm, taps_hbm, decay_hbm, acts_ref, maps_ref, state_ref, log_ref, taps_ref, top_ref,
    head_ref, xbc_buf, decay_buf, padded, sems, small_sems, chunk
):
    rows, width = xbc_buf.shape
    steps = width // chunk
    small = [
        pltpu.make_async_copy(decay_hbm, decay_buf, small_sems.at[0]),
        pltpu.make_async_copy(taps_hbm, taps_ref, small_sems.at[1]),
    ]
    copies = []
    for step in range(steps):
        part = pl.ds(step * chunk, chunk)
        copies.append(
            pltpu.make_async_copy(xbc_hbm.at[:, part], xbc_buf.at[:, part], sems.at[step])
        )
    for copy in small + copies[-1:] + copies[:-1]:
        copy.start()
    small[0].wait()
    log_ref[...] = running_sum(decay_buf[...])
    small[1].wait()

    def some_columns(start, slot):
        part = slice(start, start + LANES)
        top_ref[:, part] = xbc_buf[: top_ref.shape[0], part]
        values = xbc_buf[:, part].astype(F32)
        result = activated(values, None, taps_ref[:, part], padded.at[slot])
        head_ref[:, part] = result[:LANES]
        turned = result[LANES:].T
        acts_ref[part, LANES:] = turned
        return result, turned

    copies[-1].wait()
    some_columns(width - LANES, 0)
    result, _ = some_columns(width - 2 * LANES, 1)
    maps_ref[...] = result
    for step in range(steps - 1):
        copies[step].wait()
        for slot in range(chunk // LANES):
            head = step * (chunk // LANES) + slot
            _, turned = some_columns(head * LANES, slot)
            logs = log_ref[head : head + 1, :]
            tail = jnp.exp(logs[:, rows - 1 : rows] - logs[:, LANES:])
            decayed = (turned.astype(F32) * tail).astype(BF16)
            state_ref[head * LANES : (head + 1) * LANES, :] = product(
                decayed, maps_ref[LANES:, :]
            )


def front(xbc, conv_weight, log_decay):
    rows, width = xbc.shape
    taps = conv_weight.shape[0]
    head_count = log_decay.shape[0]
    inner = head_count * LANES
    state_size = (width - inner) // 2
    chunk = 2 * LANES
    return pl.pallas_call(
        functools.partial(front_kernel, chunk=chunk),
        in_specs=[HBM_SPEC] * 3,
        out_specs=[VMEM_SPEC] * 7,
        out_shape=[
            pltpu.VMEM((width, rows), BF16),
            pltpu.VMEM((rows, state_size), BF16),
            pltpu.VMEM((inner, state_size), F32),
            pltpu.VMEM((head_count, rows), F32),
            pltpu.VMEM((taps, width), F32),
            pltpu.VMEM((2 * GROUP, width), BF16),
            pltpu.VMEM((LANES, width), BF16),
        ],
        scratch_shapes=[
            pltpu.VMEM((rows, width), BF16),
            pltpu.VMEM((head_count, rows), F32),
            pltpu.VMEM((chunk // LANES, rows + GROUP, LANES), F32),
            pltpu.SemaphoreType.DMA((width // chunk,)),
            pltpu.SemaphoreType.DMA((2,)),
        ],
        compiler_params=params(),
        name="front",
    )(*in_hbm(xbc, conv_weight, log_decay))


def edge_kernel(edge_ref, log_ref, taps_ref, top_ref, head_ref, *refs):
    acts_ref, maps_ref, state_ref, message_ref, padded = refs[-5:]
    head_count, rows = log_ref.shape
    width = head_ref.shape[1]
    inner = head_count * LANES
    few = top_ref.shape[0]
    is_first = lax.axis_index("seq") == 0

    def some_columns(start, slot):
        part = slice(start, start + LANES)
        edge = jnp.where(is_first, 0.0, edge_ref[:, part].astype(F32))
        values = top_ref[:, part].astype(F32)
        result = activated(values, edge, taps_ref[:, part], padded.at[slot])
        block = jnp.concatenate([result, head_ref[few:, part]], axis=0)
        turned = block.T
        acts_ref[part, :LANES] = turned
        return block, turned

    some_columns(width - LANES, 0)
    maps, _ = some_columns(width - 2 * LANES, 1)
    maps_ref[:LANES, :] = maps
    totals = jnp.broadcast_to(log_ref[:, rows - 1 : rows], (head_count, LANES))
    write_spans(message_ref, inner, totals)
    for head in range(head_count):
        part = slice(head * LANES, (head + 1) * LANES)
        _, turned = some_columns(head * LANES, head % padded.shape[0])
        logs = log_ref[head : head + 1, :]
        tail = jnp.exp(logs[:, rows - 1 : rows] - logs[:, :LANES])
        decayed = (turned.astype(F32) * tail).astype(BF16)
        state = state_ref[part, :] + product(decayed, maps)
        state_ref[part, :] = state
        message_ref[part, :] = state.astype(BF16)


def edge_rows(edge, log, taps, top, head, acts, maps, state):
    head_count, _ = log.shape
    inner, state_size = state.shape
    operands = [edge, log, taps, top, head, acts, maps, state]
    return pl.pallas_call(
        edge_kernel,
        in_specs=[VMEM_SPEC] * len(operands),
        out_specs=[VMEM_SPEC] * 4,
        out_shape=[
            pltpu.VMEM(acts.shape, BF16),
            pltpu.VMEM(maps.shape, BF16),
            pltpu.VMEM(state.shape, F32),
            pltpu.VMEM((inner + head_count, state_size), BF16),
        ],
        input_output_aliases={5: 0, 6: 1, 7: 2},
        scratch_shapes=[pltpu.VMEM((2, top.shape[0] + GROUP, LANES), F32)],
        compiler_params=params(),
        cost_estimate=small_cost(),
        name="edge",
    )(*in_vmem(*operands))


def pair_kernel(state_ref, log_ref, got_ref, own_ref, stats_ref, send_ref, rest_ref, shards):
    head_count, rows = log_ref.shape
    inner = state_ref.shape[0]
    index = lax.axis_index("seq")
    is_upper = index % 2 == 1
    mine = jnp.broadcast_to(log_ref[:, rows - 1 : rows], (head_count, LANES))
    theirs = read_spans(got_ref, inner, head_count)
    stats_ref[0] = mine + theirs
    stats_ref[1] = jnp.where(is_upper, theirs, 0.0)
    write_spans(send_ref, inner // shards, mine + theirs)
    write_spans(rest_ref, inner // shards, mine + theirs)
    stats_ref[2] = jnp.exp(mine)
    stats_ref[3] = jnp.exp(theirs)
    shard = index % shards
    share = head_count // shards

    def joined(head):
        at = pl.ds(pl.multiple_of(head * LANES, LANES), LANES)
        own = state_ref[at, :]
        got = got_ref[at, :].astype(F32)
        late = jnp.where(is_upper, own, got)
        early = jnp.where(is_upper, got, own)
        late_row = jnp.where(is_upper, 2, 3)
        return early * stats_ref[late_row, pl.ds(head, 1), :] + late

    for local in range(share):
        place = slice(local * LANES, (local + 1) * LANES)
        send_ref[place, :] = joined((shard ^ 2) * share + local).astype(BF16)
        kept = joined(shard * share + local)
        own_ref[place, :] = kept
        rest_ref[place, :] = kept.astype(BF16)


def pair(state, log, got, shards):
    head_count, _ = log.shape
    inner, state_size = state.shape
    part = inner // shards
    return pl.pallas_call(
        functools.partial(pair_kernel, shards=shards),
        in_specs=[VMEM_SPEC] * 3,
        out_specs=[VMEM_SPEC] * 4,
        out_shape=[
            pltpu.VMEM((part, state_size), F32),
            pltpu.VMEM((4, head_count, LANES), F32),
            pltpu.VMEM((part + head_count, state_size), BF16),
            pltpu.VMEM((part + head_count, state_size), BF16),
        ],
        compiler_params=params(),
        cost_estimate=small_cost(),
        name="pair",
    )(*in_vmem(state, log, got))


def join_kernel(own_ref, stats_ref, got_ref, _, *refs, bit, shards, gathered):
    sources = refs[:gathered]
    if gathered:
        next_stats_ref, send_ref, across_ref = refs[gathered:]
    else:
        next_stats_ref, send_ref, next_ref = refs
    part = own_ref.shape[0]
    head_count = stats_ref.shape[1]
    share = head_count // shards
    index = lax.axis_index("seq")
    is_upper = (index >> bit) % 2 == 1
    mine = stats_ref[0]
    theirs = read_spans(got_ref, part, head_count)
    next_stats_ref[0] = mine + theirs
    next_stats_ref[1] = stats_ref[1] + jnp.where(is_upper, theirs, 0.0)
    next_stats_ref[2] = jnp.exp(jnp.where(is_upper, mine, theirs))
    next_stats_ref[3] = jnp.zeros_like(mine)
    if not gathered:
        write_spans(send_ref, part, mine + theirs)
    for local in range(share):
        place = slice(local * LANES, (local + 1) * LANES)
        head = (index % shards) * share + local
        own = own_ref[place, :]
        got = got_ref[place, :].astype(F32)
        late = jnp.where(is_upper, own, got)
        early = jnp.where(is_upper, got, own)
        total = early * next_stats_ref[2, pl.ds(head, 1), :] + late
        send_ref[place, :] = total.astype(BF16)
        if not gathered:
            next_ref[place, :] = total
    for slot in range(gathered):
        across_ref[slot * part : (slot + 1) * part, :] = sources[slot][:part, :]


def join(own, stats, got, after, bit, shards, sources):
    operands = [own, stats, got, after, *sources]
    message = own.shape if sources else got.shape
    out_shape = [pltpu.VMEM(stats.shape, F32), pltpu.VMEM(message, BF16)]
    if sources:
        out_shape.append(pltpu.VMEM((len(sources) * own.shape[0], own.shape[1]), BF16))
    else:
        out_shape.append(pltpu.VMEM(own.shape, F32))
    return pl.pallas_call(
        functools.partial(join_kernel, bit=bit, shards=shards, gathered=len(sources)),
        in_specs=[VMEM_SPEC] * len(operands),
        out_specs=[VMEM_SPEC] * 3,
        out_shape=out_shape,
        compiler_params=params(),
        cost_estimate=small_cost(),
        name="join",
    )(*in_vmem(*operands))


def bit_length(numbers, limit):
    counted = jnp.zeros(numbers.shape, jnp.int32)
    for power in range(limit):
        counted = counted + (numbers >= 1 << power).astype(jnp.int32)
    return counted


def near_kernel(*refs, first, wide, heads):
    if first:
        acts_ref, maps_ref, log_ref, gains_ref, node_ref, _ = refs[:6]
        near_ref, scores, tails, turned, weights = refs[6:]
    else:
        acts_ref, maps_ref, log_ref, gains_ref, node_ref, _, scores, tails, _ = refs[:9]
        near_ref, turned, weights = refs[9:]
    head_count, rows = log_ref.shape
    inner = head_count * LANES
    state_size = maps_ref.shape[1]
    tiles = rows // LANES
    tile_bits = tiles.bit_length() - 1
    groups = LANES // GROUP
    low_bits = GROUP.bit_length() - 1
    tile_levels = LANES.bit_length() - 1
    queries = acts_ref[inner + state_size :, :]
    middle = LANES // 2 - 1
    if first:
        for start in range(0, rows, wide):
            upto = start + wide
            scores[:upto, start:upto] = product(maps_ref[:upto, :], queries[:, start:upto])
        turned[head_count:, :] = jnp.zeros((LANES - head_count, rows), F32)
        turned[:head_count, :] = log_ref[...]
        columns = [turned[:, tile * LANES : (tile + 1) * LANES].T for tile in range(tiles)]
        for tile in range(tiles):
            place = slice(tile * LANES, (tile + 1) * LANES)
            tails[0, place, :] = jnp.exp(columns[tile][middle : middle + 1] - columns[tile])
            for bit in range(tile_bits):
                if tile >> bit & 1 == 0:
                    edge = ((tile >> bit) + 1 << bit) - 1
                    tails[1 + bit, place, :] = jnp.exp(columns[edge][LANES - 1 :] - columns[tile])
    for late in range(tiles):
        for early in range(tiles):
            if early > late:
                weights[
                    :, early * LANES : (early + 1) * LANES, late * LANES : (late + 1) * LANES
                ] = jnp.zeros((weights.shape[0], LANES, LANES), BF16)
    lane = lax.broadcasted_iota(jnp.int32, (GROUP, LANES), 1)
    row = lax.broadcasted_iota(jnp.int32, (GROUP, LANES), 0)
    inside = bit_length((lane % GROUP) ^ row, low_bits)
    ahead = row <= lane % GROUP
    lane_group = lax.broadcasted_iota(jnp.int32, (groups, LANES), 1) // GROUP
    row_group = lax.broadcasted_iota(jnp.int32, (groups, LANES), 0)
    between = bit_length(lane_group ^ row_group, groups.bit_length() - 1)
    before = row_group < lane_group
    same = (
        lax.broadcasted_iota(jnp.int32, (groups, 1, LANES), 2) // GROUP
        == lax.broadcasted_iota(jnp.int32, (groups, 1, LANES), 0)
    )
    is_upper = lax.axis_index("seq") % 2 == 1

    def spread(kind, place, head):
        chosen = jnp.full((LANES, LANES), head, jnp.int32)
        return jnp.take_along_axis(
            tails[kind, place, :], chosen, axis=1, mode="promise_in_bounds"
        )

    def one_head(head, slot):
        logs = log_ref[pl.ds(head, 1), :]
        gain_rows = [
            gains_ref[pl.ds(level * head_count + head, 1), :]
            for level in range(tile_levels + tile_bits + 2)
        ]
        for late in range(tiles):
            span = slice(late * LANES, (late + 1) * LANES)
            own = logs[:, span]
            start = late * LANES + middle
            grown = jnp.exp(own - logs[:, start : start + 1])
            corner = jnp.zeros((GROUP, LANES), F32)
            for level in range(low_bits + 1):
                gain = gain_rows[level][:, span] * grown
                corner = jnp.where(ahead & (inside == level), gain, corner)
            rest = jnp.zeros((groups, LANES), F32)
            for level in range(low_bits + 1, tile_levels + 1):
                gain = gain_rows[level][:, span] * grown
                rest = jnp.where(before & (between == level - low_bits), gain, rest)
            chosen = jnp.where(same, corner[None], rest[:, None, :]).reshape(LANES, LANES)
            weight = chosen * spread(0, span, head) * scores[span, span]
            weights[slot, span, span] = weight.astype(BF16)
            for bit in range(tile_bits):
                if late >> bit & 1 == 0:
                    continue
                edge = (late >> bit << bit) * LANES - 1
                level = tile_levels + 1 + bit
                factor = gain_rows[level][:, span] * jnp.exp(
                    own - logs[:, edge : edge + 1]
                )
                for early in range(((late >> bit) - 1) << bit, (late >> bit) << bit):
                    place = slice(early * LANES, (early + 1) * LANES)
                    weight = spread(1 + bit, place, head) * factor * scores[place, span]
                    weights[slot, place, span] = weight.astype(BF16)
        at = pl.ds(pl.multiple_of(head * LANES, LANES), LANES)
        level = tile_levels + tile_bits + 1
        factor = gain_rows[level] * jnp.exp(jnp.where(is_upper, logs, -1e30))
        far = product(node_ref[at, :], queries) * factor
        for start in range(0, rows, wide):
            upto = start + wide
            near_ref[at, start:upto] = far[:, start:upto] + product(
                acts_ref[at, :upto], weights[slot, :upto, start:upto]
            )

    def some_heads(step, carry):
        for slot in range(weights.shape[0]):
            one_head(step * weights.shape[0] + slot, slot)
        return carry

    lax.fori_loop(heads[0] // weights.shape[0], heads[1] // weights.shape[0], some_heads, 0)


def near(acts, maps, log, gains, node, after, earlier, heads):
    head_count, rows = log.shape
    wide = min(rows, 2 * LANES)
    tile_bits = (rows // LANES).bit_length() - 1
    first = earlier is None
    out_shape = [pltpu.VMEM((head_count * LANES, rows), F32)]
    operands = [acts, maps, log, gains, node, after]
    aliases = {}
    if first:
        out_shape.append(pltpu.VMEM((rows, rows), F32))
        out_shape.append(pltpu.VMEM((1 + tile_bits, rows, LANES), F32))
    else:
        near_term, scores, tails = earlier
        operands += [scores, tails, near_term]
        aliases = {len(operands) - 1: 0}
    made = pl.pallas_call(
        functools.partial(near_kernel, first=first, wide=wide, heads=heads),
        in_specs=[VMEM_SPEC] * len(operands),
        out_specs=[VMEM_SPEC] * len(out_shape),
        out_shape=out_shape,
        input_output_aliases=aliases,
        scratch_shapes=[
            pltpu.VMEM((LANES, rows), F32),
            pltpu.VMEM((2, rows, rows), BF16),
        ],
        compiler_params=params(),
        cost_estimate=pl.CostEstimate(
            flops=2 * head_count * rows * rows * LANES, bytes_accessed=10 << 20, transcendentals=0
        ),
        name="near",
    )(*in_vmem(*operands))
    return [made[0], *earlier[1:]] if not first else made


def far_product(node_ref, first_row, count, queries):
    return product(node_ref[first_row : first_row + count, :], queries)


def far_factor(gains_ref, log_ref, stats_ref, head, level, base):
    is_upper = (lax.axis_index("seq") >> level) % 2 == 1
    shift = stats_ref[1, pl.ds(head, 1), :][:, :1]
    exponent = jnp.where(is_upper, log_ref[pl.ds(head, 1), :] + shift, -1e30)
    row = (base + level) * log_ref.shape[0] + head
    return gains_ref[pl.ds(row, 1), :] * jnp.exp(exponent)


def middle_kernel(*refs, places, relatives, levels, shards):
    count = len(places)
    acts_ref, log_ref, gains_ref = refs[:3]
    stats = refs[3 : 3 + count]
    sources = refs[3 + count : -2]
    total_ref = refs[-1]
    head_count, _ = log_ref.shape
    part = head_count // shards * LANES
    inner = head_count * LANES
    state_size = acts_ref.shape[0] - inner >> 1
    shard = lax.axis_index("seq") % shards
    base = gains_ref.shape[0] // head_count - levels
    queries = acts_ref[inner + state_size :, :]
    for relative in relatives:
        terms = []
        for slot in range(count):
            source, start = places[slot][relative]
            terms.append(far_product(sources[source], start, part, queries))
        for local in range(head_count // shards):
            head = (relative ^ shard) * (head_count // shards) + local
            at = pl.ds(pl.multiple_of(head * LANES, LANES), LANES)
            total = total_ref[at, :]
            for slot in range(count):
                factor = far_factor(gains_ref, log_ref, stats[slot], head, slot + 1, base)
                total = total + terms[slot][local * LANES : (local + 1) * LANES] * factor
            total_ref[at, :] = total


def middle(
    near_term, acts, log, gains, stats, sources, places, relatives, levels, shards
):
    operands = [acts, log, gains, *stats, *sources, near_term]
    return pl.pallas_call(
        functools.partial(
            middle_kernel, places=places, relatives=relatives, levels=levels, shards=shards
        ),
        in_specs=[VMEM_SPEC] * len(operands),
        out_specs=VMEM_SPEC,
        out_shape=pltpu.VMEM(near_term.shape, F32),
        input_output_aliases={len(operands) - 1: 0},
        compiler_params=params(),
        cost_estimate=small_cost(),
        name="middle",
    )(*in_vmem(*operands))


def last_kernel(
    total_ref, acts_ref, log_ref, gains_ref, gain_ref, stats_ref, node_ref, *rest,
    level, relatives, shards, base
):
    out_hbm, turned, out_buf, out_sems = rest[-4:]
    head_count, rows = log_ref.shape
    share = head_count // shards
    part = share * LANES
    inner = head_count * LANES
    state_size = acts_ref.shape[0] - inner >> 1
    shard = lax.axis_index("seq") % shards
    turned[...] = jnp.zeros_like(turned)
    turned[:head_count, :] = gain_ref[...]
    gain_columns = turned[...].T
    queries = acts_ref[inner + state_size :, :]
    copies = []
    for place, relative in enumerate(relatives):
        term = far_product(node_ref, place * part, part, queries)
        for local in range(share):
            head = (relative ^ shard) * share + local
            at = pl.ds(pl.multiple_of(head * LANES, LANES), LANES)
            factor = far_factor(gains_ref, log_ref, stats_ref, head, level, base)
            total = total_ref[at, :] + term[local * LANES : (local + 1) * LANES] * factor
            mean = jnp.mean(total * total, axis=0, keepdims=True)
            scale = lax.rsqrt(mean + 1e-05)
            chosen = jnp.full((LANES, LANES), head, jnp.int32)
            column = jnp.take_along_axis(gain_columns, chosen, axis=1, mode="promise_in_bounds")
            column = jnp.concatenate([column] * (rows // LANES), axis=1)
            slot = len(copies)
            out_buf[slot] = (total * scale * column).astype(BF16).T
            copy = pltpu.make_async_copy(out_buf.at[slot], out_hbm.at[:, at], out_sems.at[slot])
            copy.start()
            copies.append(copy)
    for copy in copies:
        copy.wait()


def last(
    total, acts, log, gains, gain, stats, node, level, levels, relatives, shards, mixed
):
    head_count, rows = log.shape
    count = head_count // shards * len(relatives)
    operands = in_vmem(total, acts, log, gains, gain.reshape(head_count, LANES), stats, node)
    specs = [VMEM_SPEC] * len(operands)
    aliases = {}
    if mixed is not None:
        aliases = {len(operands): 0}
        operands.append(mixed)
        specs.append(HBM_SPEC)
    return pl.pallas_call(
        functools.partial(
            last_kernel, level=level, relatives=relatives, shards=shards,
            base=gains.shape[0] // head_count - levels,
        ),
        in_specs=specs,
        out_specs=HBM_SPEC,
        out_shape=jax.ShapeDtypeStruct((rows, head_count * LANES), BF16),
        input_output_aliases=aliases,
        scratch_shapes=[
            pltpu.VMEM((LANES, LANES), F32),
            pltpu.VMEM((count, rows, LANES), BF16),
            pltpu.SemaphoreType.DMA((count,)),
        ],
        compiler_params=params(),
        cost_estimate=small_cost(),
        name="last",
    )(*operands)


def moved(value, apart):
    return lax.ppermute(value, "seq", [(i, i ^ apart) for i in range(lax.axis_size("seq"))])


def on_device(xbc, conv_weight, log_decay, level_weights, gain):
    taps = conv_weight.shape[0]
    rows = xbc.shape[0]
    head_count = log_decay.shape[0]
    devices = lax.axis_size("seq")
    levels = devices.bit_length() - 1
    shards = 4
    part = head_count * LANES // shards
    gains = level_weights.transpose(1, 0, 2).reshape(-1, rows)
    behind = [(i, (i + 1) % devices) for i in range(devices)]
    edge = lax.ppermute(xbc[rows - taps + 1 :], "seq", behind)
    acts, maps, state, log, *kept = front(xbc, conv_weight, log_decay)
    acts, maps, state, message = edge_rows(edge, log, *kept, acts, maps, state)
    first_node = moved(message, 1)
    own, stats, send, rest = pair(state, log, first_node, shards)
    near_made = None
    all_stats = [stats]
    got = []
    for bit in range(1, levels - 1):
        got.append(moved(send, 1 << bit))
        if bit <= 2:
            half = head_count // 2
            heads = (half * (bit - 1), half * bit)
            near_made = near(acts, maps, log, gains, first_node, stats, near_made, heads)
        sources = [rest, *got[1:]] if bit == levels - 2 else []
        stats, send, own = join(own, stats, got[-1], near_made[0], bit, shards, sources)
        all_stats.append(stats)
    top = levels - 1

    across = moved(own, 2)
    node = moved(send, 1 << top)
    beside = moved(jnp.concatenate([*[kept[:part] for kept in got], across]), 1)
    count = len(got)
    shared = (acts, log, gains, all_stats[:count])
    direct = [{0: (slot, 0), 2: (count, slot * part)} for slot in range(count)]
    relayed = [{1: (0, slot * part), 3: (0, (count + slot) * part)} for slot in range(count)]
    total = middle(near_made[0], *shared, [*got, across], direct, (0, 2), levels, shards)
    node, total = lax.optimization_barrier((node, total))
    common = (acts, log, gains, gain, all_stats[-1])
    node_across = moved(node, 2)
    mixed = last(total, *common, node, top, levels, (0,), shards, None)
    node_across, mixed, total = lax.optimization_barrier((node_across, mixed, total))
    node_beside = moved(jnp.concatenate([node, node_across]), 1)
    total = middle(total, *shared, [beside], relayed, (1, 3), levels, shards)
    mixed = last(total, *common, node_across, top, levels, (2,), shards, mixed)
    return last(total, *common, node_beside, top, levels, (1, 3), shards, mixed)


def solution(mesh):
    in_specs = (
        P(("groups", "seq"), None),
        P(),
        P(None, ("groups", "seq")),
        P(None, None, ("groups", "seq")),
        P(),
    )
    out_specs = P(("groups", "seq"), None)
    return jax.shard_map(
        on_device, mesh=mesh, in_specs=in_specs, out_specs=out_specs, check_vma=False
    )
```

```python
import functools

import jax
import jax.numpy as jnp
from jax import lax
from jax.experimental import pallas as pl
from jax.experimental.pallas import tpu as pltpu
from jax.sharding import PartitionSpec as P

F32 = jnp.float32
BF16 = jnp.bfloat16
LANES = 128
GROUP = 8
PARTS = 4
VMEM_LIMIT = 24 << 20
HBM_SPEC = pl.BlockSpec(memory_space=pltpu.HBM)
VMEM_SPEC = pl.BlockSpec(memory_space=pltpu.VMEM)


def in_vmem(*arrays):
    return [pltpu.with_memory_space_constraint(array, pltpu.VMEM) for array in arrays]


def in_hbm(*arrays):
    return [pltpu.with_memory_space_constraint(array, pltpu.HBM) for array in arrays]


def params():
    return pltpu.CompilerParams(vmem_limit_bytes=VMEM_LIMIT)


def small_cost():
    return pl.CostEstimate(flops=1024, bytes_accessed=1024, transcendentals=0)


def product(left, right):
    return jnp.dot(left, right, preferred_element_type=F32)


def write_spans(message_ref, first_row, spans):
    head_count = spans.shape[0]
    place = lax.broadcasted_iota(jnp.int32, spans.shape, 1) // (LANES // PARTS)
    packed = jnp.zeros(spans.shape, F32)
    for part in range(PARTS - 1):
        rounded = spans.astype(BF16).astype(F32)
        packed = jnp.where(place == part, rounded, packed)
        spans = spans - rounded
    message_ref[first_row : first_row + head_count, :] = packed.astype(BF16)


def read_spans(message_ref, first_row, head_count):
    total = message_ref[first_row : first_row + head_count, :].astype(F32)
    width = LANES // PARTS
    while width < LANES:
        total = total + pltpu.roll(total, width, 1)
        width *= 2
    return total


def running_sum(logs):
    column = lax.broadcasted_iota(jnp.int32, logs.shape, 1)
    shift = 1
    while shift < logs.shape[1]:
        logs = logs + jnp.where(column >= shift, pltpu.roll(logs, shift, 1), 0.0)
        shift *= 2
    return logs


def activated(values, edge, weights, padded):
    rows = values.shape[0]
    taps = weights.shape[0]
    padded[GROUP : GROUP + rows, :] = values
    if edge is not None:
        padded[GROUP - taps + 1 : GROUP, :] = edge
    total = None
    for tap in range(taps):
        first = GROUP - taps + 1 + tap
        shifted = values if tap == taps - 1 else padded[first : first + rows, :]
        term = shifted * weights[tap : tap + 1]
        total = term if total is None else total + term
    return (total * jax.nn.sigmoid(total)).astype(BF16)


def some_columns(xbc_ref, taps_ref, acts_ref, head_ref, padded, start):
    part = slice(start, start + LANES)
    values = xbc_ref[:, part].astype(F32)
    result = activated(values, None, taps_ref[:, part], padded)
    head_ref[:, part] = result[:LANES]
    turned = result[LANES:].T
    acts_ref[part, LANES:] = turned
    return result, turned


def load_kernel(
    xbc_hbm, taps_hbm, decay_hbm, xbc_ref, taps_ref, log_ref, edge_ref, acts_ref, head_ref,
    maps_ref, decay_buf, padded, sems
):
    rows, width = xbc_ref.shape
    pieces = sems.shape[0] - 2
    maps_width = 2 * maps_ref.shape[1]
    size = (width - maps_width) // (pieces - 1)
    starts = [width - maps_width] + [piece * size for piece in range(pieces - 1)]
    copies = [
        pltpu.make_async_copy(decay_hbm, decay_buf, sems.at[pieces]),
        pltpu.make_async_copy(taps_hbm, taps_ref, sems.at[pieces + 1]),
    ]
    for piece, start in enumerate(starts):
        part = pl.ds(start, size if piece else maps_width)
        copies.append(
            pltpu.make_async_copy(xbc_hbm.at[:, part], xbc_ref.at[:, part], sems.at[piece])
        )
    for copy in copies:
        copy.start()
    copies[0].wait()
    log_ref[...] = running_sum(decay_buf[...])
    copies[1].wait()
    copies[2].wait()
    for slot, start in enumerate(range(width - LANES, width - maps_width - 1, -LANES)):
        result, _ = some_columns(
            xbc_ref, taps_ref, acts_ref, head_ref, padded.at[slot % 2], start
        )
    maps_ref[...] = result
    for copy in copies[3:]:
        copy.wait()
    few = edge_ref.shape[0]
    tail = xbc_ref[rows - 2 * GROUP :, :].astype(F32)
    edge_ref[...] = tail[2 * GROUP - few :].astype(BF16)


def load(xbc, conv_weight, log_decay):
    rows, width = xbc.shape
    head_count = log_decay.shape[0]
    state_size = (width - head_count * LANES) // 2
    pieces = 5
    return pl.pallas_call(
        load_kernel,
        in_specs=[HBM_SPEC] * 3,
        out_specs=[VMEM_SPEC] * 7,
        out_shape=[
            pltpu.VMEM(xbc.shape, BF16),
            pltpu.VMEM(conv_weight.shape, F32),
            pltpu.VMEM(log_decay.shape, F32),
            pltpu.VMEM((conv_weight.shape[0] - 1, width), BF16),
            pltpu.VMEM((width, rows), BF16),
            pltpu.VMEM((LANES, width), BF16),
            pltpu.VMEM((rows, state_size), BF16),
        ],
        scratch_shapes=[
            pltpu.VMEM(log_decay.shape, F32),
            pltpu.VMEM((2, rows + GROUP, LANES), F32),
            pltpu.SemaphoreType.DMA((pieces + 2,)),
        ],
        compiler_params=params(),
        cost_estimate=small_cost(),
        name="load",
    )(*in_hbm(xbc, conv_weight, log_decay))


def front_kernel(
    xbc_ref, taps_ref, log_ref, maps_ref, acts_in, head_in, acts_ref, head_ref, state_ref, padded
):
    rows, _ = xbc_ref.shape
    for head in range(log_ref.shape[0]):
        place = slice(head * LANES, (head + 1) * LANES)
        _, turned = some_columns(
            xbc_ref, taps_ref, acts_ref, head_ref, padded.at[head % 2], head * LANES
        )
        logs = log_ref[head : head + 1, :]
        tail = jnp.exp(logs[:, rows - 1 : rows] - logs[:, LANES:])
        decayed = (turned.astype(F32) * tail).astype(BF16)
        state_ref[place, :] = product(decayed, maps_ref[LANES:, :])


def front(xbc, taps, log, maps, acts, head):
    rows, _ = xbc.shape
    operands = [xbc, taps, log, maps, acts, head]
    return pl.pallas_call(
        front_kernel,
        in_specs=[VMEM_SPEC] * len(operands),
        out_specs=[VMEM_SPEC] * 3,
        out_shape=[
            pltpu.VMEM(acts.shape, BF16),
            pltpu.VMEM(head.shape, BF16),
            pltpu.VMEM((log.shape[0] * LANES, maps.shape[1]), F32),
        ],
        input_output_aliases={4: 0, 5: 1},
        scratch_shapes=[pltpu.VMEM((2, rows + GROUP, LANES), F32)],
        compiler_params=params(),
        name="front",
    )(*in_vmem(*operands))


def edge_kernel(edge_ref, log_ref, taps_ref, xbc_ref, head_ref, *refs):
    acts_ref, maps_ref, state_ref, message_ref, padded = refs[-5:]
    head_count, rows = log_ref.shape
    width = head_ref.shape[1]
    inner = head_count * LANES
    few = 2 * GROUP
    is_first = lax.axis_index("seq") == 0

    def first_tile(start, slot):
        part = slice(start, start + LANES)
        edge = jnp.where(is_first, 0.0, edge_ref[:, part].astype(F32))
        values = xbc_ref[:few, part].astype(F32)
        result = activated(values, edge, taps_ref[:, part], padded.at[slot])
        block = jnp.concatenate([result, head_ref[few:, part]], axis=0)
        turned = block.T
        acts_ref[part, :LANES] = turned
        return block, turned

    first_tile(width - LANES, 0)
    maps, _ = first_tile(width - 2 * LANES, 1)
    maps_ref[:LANES, :] = maps
    totals = jnp.broadcast_to(log_ref[:, rows - 1 : rows], (head_count, LANES))
    write_spans(message_ref, inner, totals)
    for head in range(head_count):
        part = slice(head * LANES, (head + 1) * LANES)
        _, turned = first_tile(head * LANES, head % padded.shape[0])
        logs = log_ref[head : head + 1, :]
        tail = jnp.exp(logs[:, rows - 1 : rows] - logs[:, :LANES])
        decayed = (turned.astype(F32) * tail).astype(BF16)
        state = state_ref[part, :] + product(decayed, maps)
        state_ref[part, :] = state
        message_ref[part, :] = state.astype(BF16)


def edge_rows(edge, log, taps, xbc, head, acts, maps, state):
    head_count, _ = log.shape
    inner, state_size = state.shape
    operands = [edge, log, taps, xbc, head, acts, maps, state]
    return pl.pallas_call(
        edge_kernel,
        in_specs=[VMEM_SPEC] * len(operands),
        out_specs=[VMEM_SPEC] * 4,
        out_shape=[
            pltpu.VMEM(acts.shape, BF16),
            pltpu.VMEM(maps.shape, BF16),
            pltpu.VMEM(state.shape, F32),
            pltpu.VMEM((inner + head_count, state_size), BF16),
        ],
        input_output_aliases={5: 0, 6: 1, 7: 2},
        scratch_shapes=[pltpu.VMEM((2, 3 * GROUP, LANES), F32)],
        compiler_params=params(),
        cost_estimate=small_cost(),
        name="edge",
    )(*in_vmem(*operands))


def pair_kernel(state_ref, log_ref, got_ref, own_ref, stats_ref, send_ref, rest_ref, shards):
    head_count, rows = log_ref.shape
    inner = state_ref.shape[0]
    index = lax.axis_index("seq")
    is_upper = index % 2 == 1
    mine = jnp.broadcast_to(log_ref[:, rows - 1 : rows], (head_count, LANES))
    theirs = read_spans(got_ref, inner, head_count)
    stats_ref[0] = mine + theirs
    stats_ref[1] = jnp.where(is_upper, theirs, 0.0)
    write_spans(send_ref, inner // shards, mine + theirs)
    write_spans(rest_ref, inner // shards, mine + theirs)
    stats_ref[2] = jnp.exp(mine)
    stats_ref[3] = jnp.exp(theirs)
    shard = index % shards
    share = head_count // shards

    def joined(head):
        at = pl.ds(pl.multiple_of(head * LANES, LANES), LANES)
        own = state_ref[at, :]
        got = got_ref[at, :].astype(F32)
        late = jnp.where(is_upper, own, got)
        early = jnp.where(is_upper, got, own)
        late_row = jnp.where(is_upper, 2, 3)
        return early * stats_ref[late_row, pl.ds(head, 1), :] + late

    for local in range(share):
        place = slice(local * LANES, (local + 1) * LANES)
        send_ref[place, :] = joined((shard ^ 2) * share + local).astype(BF16)
        kept = joined(shard * share + local)
        own_ref[place, :] = kept
        rest_ref[place, :] = kept.astype(BF16)


def pair(state, log, got, shards):
    head_count, _ = log.shape
    inner, state_size = state.shape
    part = inner // shards
    return pl.pallas_call(
        functools.partial(pair_kernel, shards=shards),
        in_specs=[VMEM_SPEC] * 3,
        out_specs=[VMEM_SPEC] * 4,
        out_shape=[
            pltpu.VMEM((part, state_size), F32),
            pltpu.VMEM((4, head_count, LANES), F32),
            pltpu.VMEM((part + head_count, state_size), BF16),
            pltpu.VMEM((part + head_count, state_size), BF16),
        ],
        compiler_params=params(),
        cost_estimate=small_cost(),
        name="pair",
    )(*in_vmem(state, log, got))


def join_kernel(own_ref, stats_ref, got_ref, _, *refs, bit, shards, gathered):
    sources = refs[:gathered]
    if gathered:
        next_stats_ref, send_ref, across_ref = refs[gathered:]
    else:
        next_stats_ref, send_ref, next_ref = refs
    part = own_ref.shape[0]
    head_count = stats_ref.shape[1]
    share = head_count // shards
    index = lax.axis_index("seq")
    is_upper = (index >> bit) % 2 == 1
    mine = stats_ref[0]
    theirs = read_spans(got_ref, part, head_count)
    next_stats_ref[0] = mine + theirs
    next_stats_ref[1] = stats_ref[1] + jnp.where(is_upper, theirs, 0.0)
    next_stats_ref[2] = jnp.exp(jnp.where(is_upper, mine, theirs))
    next_stats_ref[3] = jnp.zeros_like(mine)
    if not gathered:
        write_spans(send_ref, part, mine + theirs)
    for local in range(share):
        place = slice(local * LANES, (local + 1) * LANES)
        head = (index % shards) * share + local
        own = own_ref[place, :]
        got = got_ref[place, :].astype(F32)
        late = jnp.where(is_upper, own, got)
        early = jnp.where(is_upper, got, own)
        total = early * next_stats_ref[2, pl.ds(head, 1), :] + late
        send_ref[place, :] = total.astype(BF16)
        if not gathered:
            next_ref[place, :] = total
    for slot in range(gathered):
        across_ref[slot * part : (slot + 1) * part, :] = sources[slot][:part, :]


def join(own, stats, got, after, bit, shards, sources):
    operands = [own, stats, got, after, *sources]
    message = own.shape if sources else got.shape
    out_shape = [pltpu.VMEM(stats.shape, F32), pltpu.VMEM(message, BF16)]
    if sources:
        out_shape.append(pltpu.VMEM((len(sources) * own.shape[0], own.shape[1]), BF16))
    else:
        out_shape.append(pltpu.VMEM(own.shape, F32))
    return pl.pallas_call(
        functools.partial(join_kernel, bit=bit, shards=shards, gathered=len(sources)),
        in_specs=[VMEM_SPEC] * len(operands),
        out_specs=[VMEM_SPEC] * 3,
        out_shape=out_shape,
        compiler_params=params(),
        cost_estimate=small_cost(),
        name="join",
    )(*in_vmem(*operands))


def bit_length(numbers, limit):
    counted = jnp.zeros(numbers.shape, jnp.int32)
    for power in range(limit):
        counted = counted + (numbers >= 1 << power).astype(jnp.int32)
    return counted


def near_kernel(*refs, first, wide, heads):
    if first:
        acts_ref, maps_ref, log_ref, gains_ref, node_ref, _, gain_ref = refs[:7]
        near_ref, scores, tails, columns_ref, turned, weights = refs[7:]
    else:
        acts_ref, maps_ref, log_ref, gains_ref, node_ref, _, scores, tails, _ = refs[:9]
        near_ref, turned, weights = refs[9:]
    head_count, rows = log_ref.shape
    inner = head_count * LANES
    state_size = maps_ref.shape[1]
    tiles = rows // LANES
    tile_bits = tiles.bit_length() - 1
    groups = LANES // GROUP
    low_bits = GROUP.bit_length() - 1
    tile_levels = LANES.bit_length() - 1
    queries = acts_ref[inner + state_size :, :]
    middle = LANES // 2 - 1
    if first:
        for start in range(0, rows, wide):
            upto = start + wide
            scores[:upto, start:upto] = product(maps_ref[:upto, :], queries[:, start:upto])
        turned[head_count:, :] = jnp.zeros((LANES - head_count, rows), F32)
        turned[:head_count, :LANES] = gain_ref[...]
        columns_ref[...] = turned[:, :LANES].T
        turned[:head_count, :] = log_ref[...]
        columns = [turned[:, tile * LANES : (tile + 1) * LANES].T for tile in range(tiles)]
        for tile in range(tiles):
            place = slice(tile * LANES, (tile + 1) * LANES)
            tails[0, place, :] = jnp.exp(columns[tile][middle : middle + 1] - columns[tile])
            for bit in range(tile_bits):
                if tile >> bit & 1 == 0:
                    edge = ((tile >> bit) + 1 << bit) - 1
                    tails[1 + bit, place, :] = jnp.exp(columns[edge][LANES - 1 :] - columns[tile])
    for late in range(tiles):
        for early in range(tiles):
            if early > late:
                weights[
                    :, early * LANES : (early + 1) * LANES, late * LANES : (late + 1) * LANES
                ] = jnp.zeros((weights.shape[0], LANES, LANES), BF16)
    lane = lax.broadcasted_iota(jnp.int32, (GROUP, LANES), 1)
    row = lax.broadcasted_iota(jnp.int32, (GROUP, LANES), 0)
    inside = bit_length((lane % GROUP) ^ row, low_bits)
    ahead = row <= lane % GROUP
    lane_group = lax.broadcasted_iota(jnp.int32, (groups, LANES), 1) // GROUP
    row_group = lax.broadcasted_iota(jnp.int32, (groups, LANES), 0)
    between = bit_length(lane_group ^ row_group, groups.bit_length() - 1)
    before = row_group < lane_group
    same = (
        lax.broadcasted_iota(jnp.int32, (groups, 1, LANES), 2) // GROUP
        == lax.broadcasted_iota(jnp.int32, (groups, 1, LANES), 0)
    )
    is_upper = lax.axis_index("seq") % 2 == 1

    def spread(kind, place, head):
        chosen = jnp.full((LANES, LANES), head, jnp.int32)
        return jnp.take_along_axis(
            tails[kind, place, :], chosen, axis=1, mode="promise_in_bounds"
        )

    def one_head(head, slot):
        logs = log_ref[pl.ds(head, 1), :]
        gain_rows = [
            gains_ref[pl.ds(level * head_count + head, 1), :]
            for level in range(tile_levels + tile_bits + 2)
        ]
        for late in range(tiles):
            span = slice(late * LANES, (late + 1) * LANES)
            own = logs[:, span]
            start = late * LANES + middle
            grown = jnp.exp(own - logs[:, start : start + 1])
            corner = jnp.zeros((GROUP, LANES), F32)
            for level in range(low_bits + 1):
                gain = gain_rows[level][:, span] * grown
                corner = jnp.where(ahead & (inside == level), gain, corner)
            rest = jnp.zeros((groups, LANES), F32)
            for level in range(low_bits + 1, tile_levels + 1):
                gain = gain_rows[level][:, span] * grown
                rest = jnp.where(before & (between == level - low_bits), gain, rest)
            chosen = jnp.where(same, corner[None], rest[:, None, :]).reshape(LANES, LANES)
            weight = chosen * spread(0, span, head) * scores[span, span]
            weights[slot, span, span] = weight.astype(BF16)
            for bit in range(tile_bits):
                if late >> bit & 1 == 0:
                    continue
                edge = (late >> bit << bit) * LANES - 1
                level = tile_levels + 1 + bit
                factor = gain_rows[level][:, span] * jnp.exp(
                    own - logs[:, edge : edge + 1]
                )
                for early in range(((late >> bit) - 1) << bit, (late >> bit) << bit):
                    place = slice(early * LANES, (early + 1) * LANES)
                    weight = spread(1 + bit, place, head) * factor * scores[place, span]
                    weights[slot, place, span] = weight.astype(BF16)
        at = pl.ds(pl.multiple_of(head * LANES, LANES), LANES)
        level = tile_levels + tile_bits + 1
        factor = gain_rows[level] * jnp.exp(jnp.where(is_upper, logs, -1e30))
        far = product(node_ref[at, :], queries) * factor
        for start in range(0, rows, wide):
            upto = start + wide
            near_ref[at, start:upto] = far[:, start:upto] + product(
                acts_ref[at, :upto], weights[slot, :upto, start:upto]
            )

    def some_heads(step, carry):
        for slot in range(weights.shape[0]):
            one_head(step * weights.shape[0] + slot, slot)
        return carry

    lax.fori_loop(heads[0] // weights.shape[0], heads[1] // weights.shape[0], some_heads, 0)


def near(acts, maps, log, gains, node, after, gain, earlier, heads):
    head_count, rows = log.shape
    wide = min(rows, 2 * LANES)
    tile_bits = (rows // LANES).bit_length() - 1
    first = earlier is None
    out_shape = [pltpu.VMEM((head_count * LANES, rows), F32)]
    operands = [acts, maps, log, gains, node, after]
    aliases = {}
    if first:
        out_shape.append(pltpu.VMEM((rows, rows), F32))
        out_shape.append(pltpu.VMEM((1 + tile_bits, rows, LANES), F32))
        out_shape.append(pltpu.VMEM((LANES, LANES), F32))
        operands.append(gain.reshape(head_count, LANES))
    else:
        near_term, scores, tails, _ = earlier
        operands += [scores, tails, near_term]
        aliases = {len(operands) - 1: 0}
    made = pl.pallas_call(
        functools.partial(near_kernel, first=first, wide=wide, heads=heads),
        in_specs=[VMEM_SPEC] * len(operands),
        out_specs=[VMEM_SPEC] * len(out_shape),
        out_shape=out_shape,
        input_output_aliases=aliases,
        scratch_shapes=[
            pltpu.VMEM((LANES, rows), F32),
            pltpu.VMEM((2, rows, rows), BF16),
        ],
        compiler_params=params(),
        cost_estimate=pl.CostEstimate(
            flops=2 * head_count * rows * rows * LANES, bytes_accessed=10 << 20, transcendentals=0
        ),
        name="near",
    )(*in_vmem(*operands))
    return made if first else [made[0], *earlier[1:]]


def far_product(node_ref, first_row, count, queries):
    return product(node_ref[first_row : first_row + count, :], queries)


def far_factor(gains_ref, log_ref, stats_ref, head, level, base):
    is_upper = (lax.axis_index("seq") >> level) % 2 == 1
    shift = stats_ref[1, pl.ds(head, 1), :][:, :1]
    exponent = jnp.where(is_upper, log_ref[pl.ds(head, 1), :] + shift, -1e30)
    row = (base + level) * log_ref.shape[0] + head
    return gains_ref[pl.ds(row, 1), :] * jnp.exp(exponent)


def middle_kernel(*refs, places, relatives, levels, shards):
    count = len(places)
    acts_ref, log_ref, gains_ref = refs[:3]
    stats = refs[3 : 3 + count]
    sources = refs[3 + count : -2]
    total_ref = refs[-1]
    head_count, _ = log_ref.shape
    part = head_count // shards * LANES
    inner = head_count * LANES
    state_size = acts_ref.shape[0] - inner >> 1
    shard = lax.axis_index("seq") % shards
    base = gains_ref.shape[0] // head_count - levels
    queries = acts_ref[inner + state_size :, :]
    for relative in relatives:
        terms = []
        for slot in range(count):
            source, start = places[slot][relative]
            terms.append(far_product(sources[source], start, part, queries))
        for local in range(head_count // shards):
            head = (relative ^ shard) * (head_count // shards) + local
            at = pl.ds(pl.multiple_of(head * LANES, LANES), LANES)
            total = total_ref[at, :]
            for slot in range(count):
                factor = far_factor(gains_ref, log_ref, stats[slot], head, slot + 1, base)
                total = total + terms[slot][local * LANES : (local + 1) * LANES] * factor
            total_ref[at, :] = total


def middle(
    near_term, acts, log, gains, stats, sources, places, relatives, levels, shards
):
    operands = [acts, log, gains, *stats, *sources, near_term]
    return pl.pallas_call(
        functools.partial(
            middle_kernel, places=places, relatives=relatives, levels=levels, shards=shards
        ),
        in_specs=[VMEM_SPEC] * len(operands),
        out_specs=VMEM_SPEC,
        out_shape=pltpu.VMEM(near_term.shape, F32),
        input_output_aliases={len(operands) - 1: 0},
        compiler_params=params(),
        cost_estimate=small_cost(),
        name="middle",
    )(*in_vmem(*operands))


def last_kernel(
    total_ref, acts_ref, log_ref, gains_ref, columns_ref, stats_ref, node_ref, *refs,
    level, relatives, done, shards, base
):
    head_count, rows = log_ref.shape
    share = head_count // shards
    part = share * LANES
    inner = head_count * LANES
    state_size = acts_ref.shape[0] - inner >> 1
    shard = lax.axis_index("seq") % shards
    queries = acts_ref[inner + state_size :, :]
    copies = []
    if done:
        out_hbm, mixed_ref, sems = refs[-3:]

    def send(source_ref, slot, relative, local):
        start = pl.multiple_of(((relative ^ shard) * share + local) * LANES, LANES)
        copies.append(
            pltpu.make_async_copy(
                source_ref.at[slot], out_hbm.at[:, pl.ds(start, LANES)], sems.at[len(copies)]
            )
        )
        copies[-1].start()

    if done:
        for relative, source_ref in zip(done, refs):
            for local in range(share):
                send(source_ref, local, relative, local)
    else:
        (mixed_ref,) = refs
    for place, relative in enumerate(relatives):
        term = far_product(node_ref, place * part, part, queries)
        for local in range(share):
            head = (relative ^ shard) * share + local
            at = pl.ds(pl.multiple_of(head * LANES, LANES), LANES)
            factor = far_factor(gains_ref, log_ref, stats_ref, head, level, base)
            total = total_ref[at, :] + term[local * LANES : (local + 1) * LANES] * factor
            mean = jnp.mean(total * total, axis=0, keepdims=True)
            scale = lax.rsqrt(mean + 1e-05)
            chosen = jnp.full((LANES, LANES), head, jnp.int32)
            column = jnp.take_along_axis(
                columns_ref[...], chosen, axis=1, mode="promise_in_bounds"
            )
            column = jnp.concatenate([column] * (rows // LANES), axis=1)
            slot = place * share + local
            mixed_ref[slot] = (total * scale * column).astype(BF16).T
            if done:
                send(mixed_ref, slot, relative, local)
    for copy in copies:
        copy.wait()


def last(total, acts, log, gains, columns, stats, node, level, levels, relatives, shards, done):
    head_count, rows = log.shape
    share = head_count // shards
    operands = [total, acts, log, gains, columns, stats, node, *done.values()]
    mixed = pltpu.VMEM((share * len(relatives), rows, LANES), BF16)
    whole = jax.ShapeDtypeStruct((rows, head_count * LANES), BF16)
    return pl.pallas_call(
        functools.partial(
            last_kernel, level=level, relatives=relatives, done=tuple(done), shards=shards,
            base=gains.shape[0] // head_count - levels,
        ),
        in_specs=[VMEM_SPEC] * len(operands),
        out_specs=HBM_SPEC if done else VMEM_SPEC,
        out_shape=whole if done else mixed,
        scratch_shapes=[mixed, pltpu.SemaphoreType.DMA((head_count,))] if done else [],
        compiler_params=params(),
        cost_estimate=small_cost(),
        name="last",
    )(*in_vmem(*operands))


def moved(value, apart):
    return lax.ppermute(value, "seq", [(i, i ^ apart) for i in range(lax.axis_size("seq"))])


def on_device(xbc, conv_weight, log_decay, level_weights, gain):
    rows = xbc.shape[0]
    head_count = log_decay.shape[0]
    devices = lax.axis_size("seq")
    levels = devices.bit_length() - 1
    shards = 4
    part = head_count * LANES // shards
    gains = level_weights.transpose(1, 0, 2).reshape(-1, rows)
    behind = [(i, (i + 1) % devices) for i in range(devices)]
    values, taps, log, edge, acts, head, maps = load(xbc, conv_weight, log_decay)
    edge = lax.ppermute(edge, "seq", behind)
    acts, head, state = front(values, taps, log, maps, acts, head)
    acts, maps, state, message = edge_rows(edge, log, taps, values, head, acts, maps, state)
    first_node = moved(message, 1)
    own, stats, send, rest = pair(state, log, first_node, shards)
    near_made = None
    all_stats = [stats]
    got = []
    for bit in range(1, levels - 1):
        got.append(moved(send, 1 << bit))
        if bit <= 2:
            half = head_count // 2
            heads = (half * (bit - 1), half * bit)
            near_made = near(
                acts, maps, log, gains, first_node, stats, gain, near_made, heads
            )
        sources = [rest, *got[1:]] if bit == levels - 2 else []
        stats, send, own = join(own, stats, got[-1], near_made[0], bit, shards, sources)
        all_stats.append(stats)
    top = levels - 1

    across = moved(own, 2)
    node = moved(send, 1 << top)
    beside = moved(jnp.concatenate([*[kept[:part] for kept in got], across]), 1)
    count = len(got)
    shared = (acts, log, gains, all_stats[:count])
    direct = [{0: (slot, 0), 2: (count, slot * part)} for slot in range(count)]
    relayed = [{1: (0, slot * part), 3: (0, (count + slot) * part)} for slot in range(count)]
    total = middle(near_made[0], *shared, [*got, across], direct, (0, 2), levels, shards)
    node, total = lax.optimization_barrier((node, total))
    common = (acts, log, gains, near_made[3], all_stats[-1])
    node_across = moved(node, 2)
    own_done = last(total, *common, node, top, levels, (0,), shards, {})
    node_across, own_done, total = lax.optimization_barrier((node_across, own_done, total))
    node_beside = moved(jnp.concatenate([node, node_across]), 1)
    total = middle(total, *shared, [beside], relayed, (1, 3), levels, shards)
    across_done = last(total, *common, node_across, top, levels, (2,), shards, {})
    done = {0: own_done, 2: across_done}
    return last(total, *common, node_beside, top, levels, (1, 3), shards, done)


def solution(mesh):
    in_specs = (
        P(("groups", "seq"), None),
        P(),
        P(None, ("groups", "seq")),
        P(None, None, ("groups", "seq")),
        P(),
    )
    out_specs = P(("groups", "seq"), None)
    return jax.shard_map(
        on_device, mesh=mesh, in_specs=in_specs, out_specs=out_specs, check_vma=False
    )
```

```python
import functools

import jax
import jax.numpy as jnp
from jax import lax
from jax.experimental import pallas as pl
from jax.experimental.pallas import tpu as pltpu
from jax.sharding import PartitionSpec as P

F32 = jnp.float32
BF16 = jnp.bfloat16
LANES = 128
GROUP = 8
PARTS = 4
VMEM_LIMIT = 24 << 20
HBM_SPEC = pl.BlockSpec(memory_space=pltpu.HBM)
VMEM_SPEC = pl.BlockSpec(memory_space=pltpu.VMEM)


def in_vmem(*arrays):
    return [pltpu.with_memory_space_constraint(array, pltpu.VMEM) for array in arrays]


def in_hbm(*arrays):
    return [pltpu.with_memory_space_constraint(array, pltpu.HBM) for array in arrays]


def params():
    return pltpu.CompilerParams(vmem_limit_bytes=VMEM_LIMIT)


def small_cost():
    return pl.CostEstimate(flops=1024, bytes_accessed=1024, transcendentals=0)


def product(left, right):
    return jnp.dot(left, right, preferred_element_type=F32)


def write_spans(message_ref, first_row, spans):
    head_count = spans.shape[0]
    place = lax.broadcasted_iota(jnp.int32, spans.shape, 1) // (LANES // PARTS)
    packed = jnp.zeros(spans.shape, F32)
    for part in range(PARTS - 1):
        rounded = spans.astype(BF16).astype(F32)
        packed = jnp.where(place == part, rounded, packed)
        spans = spans - rounded
    message_ref[first_row : first_row + head_count, :] = packed.astype(BF16)


def read_spans(message_ref, first_row, head_count):
    total = message_ref[first_row : first_row + head_count, :].astype(F32)
    width = LANES // PARTS
    while width < LANES:
        total = total + pltpu.roll(total, width, 1)
        width *= 2
    return total


def running_sum(logs):
    head_count, rows = logs.shape
    tiles = rows // LANES
    row = lax.broadcasted_iota(jnp.int32, (LANES, LANES), 0)
    column = lax.broadcasted_iota(jnp.int32, (LANES, LANES), 1)
    upto = (row <= column).astype(BF16)
    left = jnp.concatenate(
        [logs[:, tile * LANES : (tile + 1) * LANES] for tile in range(tiles)], axis=0
    )
    pieces = []
    for _ in range(3):
        pieces.append(left.astype(BF16))
        left = left - pieces[-1].astype(F32)
    size = head_count * tiles
    added = product(jnp.concatenate(pieces, axis=0), upto)
    within = added[2 * size :] + added[size : 2 * size] + added[:size]
    sums = []
    offset = jnp.zeros((head_count, 1), F32)
    for tile in range(tiles):
        part = within[tile * head_count : (tile + 1) * head_count]
        sums.append(part + offset)
        offset = offset + part[:, LANES - 1 :]
    return jnp.concatenate(sums, axis=1)


def activated(values, edge, weights, padded):
    rows = values.shape[0]
    taps = weights.shape[0]
    padded[GROUP : GROUP + rows, :] = values
    if edge is not None:
        padded[GROUP - taps + 1 : GROUP, :] = edge
    total = None
    for tap in range(taps):
        first = GROUP - taps + 1 + tap
        shifted = values if tap == taps - 1 else padded[first : first + rows, :]
        term = shifted * weights[tap : tap + 1]
        total = term if total is None else total + term
    return (total * jax.nn.sigmoid(total)).astype(BF16)


def some_columns(xbc_ref, taps_ref, acts_ref, head_ref, padded, start):
    part = slice(start, start + LANES)
    values = xbc_ref[:, part].astype(F32)
    result = activated(values, None, taps_ref[:, part], padded)
    head_ref[:, part] = result[:LANES]
    turned = result[LANES:].T
    acts_ref[part, LANES:] = turned
    return result, turned


def head_columns(
    xbc_ref, taps_ref, log_ref, maps_ref, acts_ref, head_ref, state_ref, padded, heads
):
    rows, _ = xbc_ref.shape
    for head in heads:
        place = slice(head * LANES, (head + 1) * LANES)
        _, turned = some_columns(
            xbc_ref, taps_ref, acts_ref, head_ref, padded.at[head % 2], head * LANES
        )
        logs = log_ref[head : head + 1, :]
        tail = jnp.exp(logs[:, rows - 1 : rows] - logs[:, LANES:])
        decayed = (turned.astype(F32) * tail).astype(BF16)
        state_ref[place, :] = product(decayed, maps_ref[LANES:, :])


def load_kernel(
    xbc_hbm, taps_hbm, decay_hbm, xbc_ref, taps_ref, log_ref, edge_ref, acts_ref, head_ref,
    maps_ref, state_ref, decay_buf, padded, sems, early
):
    rows, width = xbc_ref.shape
    pieces = sems.shape[0] - 2
    maps_width = 2 * maps_ref.shape[1]
    inner = width - maps_width
    rest = (inner - early * LANES) // (pieces - 2)
    cuts = [0] + [early * LANES + piece * rest for piece in range(pieces - 1)]
    spans = [(inner, maps_width)] + [(x, y - x) for x, y in zip(cuts, cuts[1:])]
    copies = [
        pltpu.make_async_copy(decay_hbm, decay_buf, sems.at[pieces]),
        pltpu.make_async_copy(taps_hbm, taps_ref, sems.at[pieces + 1]),
    ]
    for piece, (start, size) in enumerate(spans):
        part = pl.ds(start, size)
        copies.append(
            pltpu.make_async_copy(xbc_hbm.at[:, part], xbc_ref.at[:, part], sems.at[piece])
        )
    for copy in copies[:4]:
        copy.start()
    for copy in copies[4:]:
        copy.start()
    copies[0].wait()
    log_ref[...] = running_sum(decay_buf[...])
    copies[1].wait()
    copies[2].wait()
    for slot, start in enumerate(range(width - LANES, inner - 1, -LANES)):
        result, _ = some_columns(
            xbc_ref, taps_ref, acts_ref, head_ref, padded.at[slot % 2], start
        )
    maps_ref[...] = result
    copies[3].wait()
    head_columns(
        xbc_ref, taps_ref, log_ref, maps_ref, acts_ref, head_ref, state_ref, padded, range(early)
    )
    for copy in copies[4:]:
        copy.wait()
    few = edge_ref.shape[0]
    tail = xbc_ref[rows - 2 * GROUP :, :].astype(F32)
    edge_ref[...] = tail[2 * GROUP - few :].astype(BF16)


def load(xbc, conv_weight, log_decay, early):
    rows, width = xbc.shape
    inner = log_decay.shape[0] * LANES
    state_size = (width - inner) // 2
    pieces = 3
    return pl.pallas_call(
        functools.partial(load_kernel, early=early),
        in_specs=[HBM_SPEC] * 3,
        out_specs=[VMEM_SPEC] * 8,
        out_shape=[
            pltpu.VMEM(xbc.shape, BF16),
            pltpu.VMEM(conv_weight.shape, F32),
            pltpu.VMEM(log_decay.shape, F32),
            pltpu.VMEM((conv_weight.shape[0] - 1, width), BF16),
            pltpu.VMEM((width, rows), BF16),
            pltpu.VMEM((LANES, width), BF16),
            pltpu.VMEM((rows, state_size), BF16),
            pltpu.VMEM((inner, state_size), F32),
        ],
        scratch_shapes=[
            pltpu.VMEM(log_decay.shape, F32),
            pltpu.VMEM((2, rows + GROUP, LANES), F32),
            pltpu.SemaphoreType.DMA((pieces + 2,)),
        ],
        compiler_params=params(),
        cost_estimate=small_cost(),
        name="load",
    )(*in_hbm(xbc, conv_weight, log_decay))


def front_kernel(
    xbc_ref, taps_ref, log_ref, maps_ref, acts_in, head_in, state_in, acts_ref, head_ref,
    state_ref, padded, early
):
    head_columns(
        xbc_ref, taps_ref, log_ref, maps_ref, acts_ref, head_ref, state_ref, padded,
        range(early, log_ref.shape[0]),
    )


def front(xbc, taps, log, maps, acts, head, state, early):
    rows, _ = xbc.shape
    operands = [xbc, taps, log, maps, acts, head, state]
    return pl.pallas_call(
        functools.partial(front_kernel, early=early),
        in_specs=[VMEM_SPEC] * len(operands),
        out_specs=[VMEM_SPEC] * 3,
        out_shape=[
            pltpu.VMEM(acts.shape, BF16),
            pltpu.VMEM(head.shape, BF16),
            pltpu.VMEM(state.shape, F32),
        ],
        input_output_aliases={4: 0, 5: 1, 6: 2},
        scratch_shapes=[pltpu.VMEM((2, rows + GROUP, LANES), F32)],
        compiler_params=params(),
        name="front",
    )(*in_vmem(*operands))


def edge_kernel(far_edge_ref, near_edge_ref, log_ref, taps_ref, xbc_ref, head_ref, *refs):
    acts_ref, maps_ref, state_ref, message_ref, padded = refs[-5:]
    head_count, rows = log_ref.shape
    width = head_ref.shape[1]
    inner = head_count * LANES
    few = 2 * GROUP
    index = lax.axis_index("seq")

    def first_tile(start, slot):
        part = slice(start, start + LANES)
        near_edge = near_edge_ref[:, part].astype(F32)
        far_edge = far_edge_ref[:, part].astype(F32)
        edge = jnp.where(index % 2 == 1, near_edge, jnp.where(index == 0, 0.0, far_edge))
        values = xbc_ref[:few, part].astype(F32)
        result = activated(values, edge, taps_ref[:, part], padded.at[slot])
        block = jnp.concatenate([result, head_ref[few:, part]], axis=0)
        turned = block.T
        acts_ref[part, :LANES] = turned
        return block, turned

    first_tile(width - LANES, 0)
    maps, _ = first_tile(width - 2 * LANES, 1)
    maps_ref[:LANES, :] = maps
    totals = jnp.broadcast_to(log_ref[:, rows - 1 : rows], (head_count, LANES))
    write_spans(message_ref, inner, totals)
    for head in range(head_count):
        part = slice(head * LANES, (head + 1) * LANES)
        _, turned = first_tile(head * LANES, head % padded.shape[0])
        logs = log_ref[head : head + 1, :]
        tail = jnp.exp(logs[:, rows - 1 : rows] - logs[:, :LANES])
        decayed = (turned.astype(F32) * tail).astype(BF16)
        state = state_ref[part, :] + product(decayed, maps)
        state_ref[part, :] = state
        message_ref[part, :] = state.astype(BF16)


def edge_rows(far_edge, near_edge, log, taps, xbc, head, acts, maps, state):
    head_count, _ = log.shape
    inner, state_size = state.shape
    operands = [far_edge, near_edge, log, taps, xbc, head, acts, maps, state]
    return pl.pallas_call(
        edge_kernel,
        in_specs=[VMEM_SPEC] * len(operands),
        out_specs=[VMEM_SPEC] * 4,
        out_shape=[
            pltpu.VMEM(acts.shape, BF16),
            pltpu.VMEM(maps.shape, BF16),
            pltpu.VMEM(state.shape, F32),
            pltpu.VMEM((inner + head_count, state_size), BF16),
        ],
        input_output_aliases={6: 0, 7: 1, 8: 2},
        scratch_shapes=[pltpu.VMEM((2, 3 * GROUP, LANES), F32)],
        compiler_params=params(),
        cost_estimate=small_cost(),
        name="edge",
    )(*in_vmem(*operands))


def pair_kernel(state_ref, log_ref, got_ref, own_ref, stats_ref, send_ref, rest_ref, shards):
    head_count, rows = log_ref.shape
    inner = state_ref.shape[0]
    index = lax.axis_index("seq")
    is_upper = index % 2 == 1
    mine = jnp.broadcast_to(log_ref[:, rows - 1 : rows], (head_count, LANES))
    theirs = read_spans(got_ref, inner, head_count)
    stats_ref[0] = mine + theirs
    stats_ref[1] = jnp.where(is_upper, theirs, 0.0)
    write_spans(send_ref, inner // shards, mine + theirs)
    write_spans(rest_ref, inner // shards, mine + theirs)
    stats_ref[2] = jnp.exp(mine)
    stats_ref[3] = jnp.exp(theirs)
    shard = index % shards
    share = head_count // shards

    def joined(head):
        at = pl.ds(pl.multiple_of(head * LANES, LANES), LANES)
        own = state_ref[at, :]
        got = got_ref[at, :].astype(F32)
        late = jnp.where(is_upper, own, got)
        early = jnp.where(is_upper, got, own)
        late_row = jnp.where(is_upper, 2, 3)
        return early * stats_ref[late_row, pl.ds(head, 1), :] + late

    for local in range(share):
        place = slice(local * LANES, (local + 1) * LANES)
        send_ref[place, :] = joined((shard ^ 2) * share + local).astype(BF16)
        kept = joined(shard * share + local)
        own_ref[place, :] = kept
        rest_ref[place, :] = kept.astype(BF16)


def pair(state, log, got, shards):
    head_count, _ = log.shape
    inner, state_size = state.shape
    part = inner // shards
    return pl.pallas_call(
        functools.partial(pair_kernel, shards=shards),
        in_specs=[VMEM_SPEC] * 3,
        out_specs=[VMEM_SPEC] * 4,
        out_shape=[
            pltpu.VMEM((part, state_size), F32),
            pltpu.VMEM((4, head_count, LANES), F32),
            pltpu.VMEM((part + head_count, state_size), BF16),
            pltpu.VMEM((part + head_count, state_size), BF16),
        ],
        compiler_params=params(),
        cost_estimate=small_cost(),
        name="pair",
    )(*in_vmem(state, log, got))


def join_kernel(own_ref, stats_ref, got_ref, _, *refs, bit, shards, gathered):
    sources = refs[:gathered]
    if gathered:
        next_stats_ref, send_ref, across_ref = refs[gathered:]
    else:
        next_stats_ref, send_ref, next_ref = refs
    part = own_ref.shape[0]
    head_count = stats_ref.shape[1]
    share = head_count // shards
    index = lax.axis_index("seq")
    is_upper = (index >> bit) % 2 == 1
    mine = stats_ref[0]
    theirs = read_spans(got_ref, part, head_count)
    next_stats_ref[0] = mine + theirs
    next_stats_ref[1] = stats_ref[1] + jnp.where(is_upper, theirs, 0.0)
    next_stats_ref[2] = jnp.exp(jnp.where(is_upper, mine, theirs))
    next_stats_ref[3] = jnp.zeros_like(mine)
    if not gathered:
        write_spans(send_ref, part, mine + theirs)
    for local in range(share):
        place = slice(local * LANES, (local + 1) * LANES)
        head = (index % shards) * share + local
        own = own_ref[place, :]
        got = got_ref[place, :].astype(F32)
        late = jnp.where(is_upper, own, got)
        early = jnp.where(is_upper, got, own)
        total = early * next_stats_ref[2, pl.ds(head, 1), :] + late
        send_ref[place, :] = total.astype(BF16)
        if not gathered:
            next_ref[place, :] = total
    for slot in range(gathered):
        across_ref[slot * part : (slot + 1) * part, :] = sources[slot][:part, :]


def join(own, stats, got, after, bit, shards, sources):
    operands = [own, stats, got, after, *sources]
    message = own.shape if sources else got.shape
    out_shape = [pltpu.VMEM(stats.shape, F32), pltpu.VMEM(message, BF16)]
    if sources:
        out_shape.append(pltpu.VMEM((len(sources) * own.shape[0], own.shape[1]), BF16))
    else:
        out_shape.append(pltpu.VMEM(own.shape, F32))
    return pl.pallas_call(
        functools.partial(join_kernel, bit=bit, shards=shards, gathered=len(sources)),
        in_specs=[VMEM_SPEC] * len(operands),
        out_specs=[VMEM_SPEC] * 3,
        out_shape=out_shape,
        compiler_params=params(),
        cost_estimate=small_cost(),
        name="join",
    )(*in_vmem(*operands))


def bit_length(numbers, limit):
    counted = jnp.zeros(numbers.shape, jnp.int32)
    for power in range(limit):
        counted = counted + (numbers >= 1 << power).astype(jnp.int32)
    return counted


def near_kernel(*refs, first, wide, heads):
    if first:
        acts_ref, maps_ref, log_ref, gains_ref, node_ref, _, gain_ref = refs[:7]
        near_ref, scores, tails, columns_ref, turned, weights = refs[7:]
    else:
        acts_ref, maps_ref, log_ref, gains_ref, node_ref, _, scores, tails, _ = refs[:9]
        near_ref, turned, weights = refs[9:]
    head_count, rows = log_ref.shape
    inner = head_count * LANES
    state_size = maps_ref.shape[1]
    tiles = rows // LANES
    tile_bits = tiles.bit_length() - 1
    groups = LANES // GROUP
    low_bits = GROUP.bit_length() - 1
    tile_levels = LANES.bit_length() - 1
    queries = acts_ref[inner + state_size :, :]
    middle = LANES // 2 - 1
    if first:
        for start in range(0, rows, wide):
            upto = start + wide
            scores[:upto, start:upto] = product(maps_ref[:upto, :], queries[:, start:upto])
        turned[head_count:, :] = jnp.zeros((LANES - head_count, rows), F32)
        turned[:head_count, :LANES] = gain_ref[...]
        columns_ref[...] = turned[:, :LANES].T
        turned[:head_count, :] = log_ref[...]
        columns = [turned[:, tile * LANES : (tile + 1) * LANES].T for tile in range(tiles)]
        for tile in range(tiles):
            place = slice(tile * LANES, (tile + 1) * LANES)
            tails[0, place, :] = jnp.exp(columns[tile][middle : middle + 1] - columns[tile])
            for bit in range(tile_bits):
                if tile >> bit & 1 == 0:
                    edge = ((tile >> bit) + 1 << bit) - 1
                    tails[1 + bit, place, :] = jnp.exp(columns[edge][LANES - 1 :] - columns[tile])
    for late in range(tiles):
        for early in range(tiles):
            if early > late:
                weights[
                    :, early * LANES : (early + 1) * LANES, late * LANES : (late + 1) * LANES
                ] = jnp.zeros((weights.shape[0], LANES, LANES), BF16)
    lane = lax.broadcasted_iota(jnp.int32, (GROUP, LANES), 1)
    row = lax.broadcasted_iota(jnp.int32, (GROUP, LANES), 0)
    inside = bit_length((lane % GROUP) ^ row, low_bits)
    ahead = row <= lane % GROUP
    lane_group = lax.broadcasted_iota(jnp.int32, (groups, LANES), 1) // GROUP
    row_group = lax.broadcasted_iota(jnp.int32, (groups, LANES), 0)
    between = bit_length(lane_group ^ row_group, groups.bit_length() - 1)
    before = row_group < lane_group
    same = (
        lax.broadcasted_iota(jnp.int32, (groups, 1, LANES), 2) // GROUP
        == lax.broadcasted_iota(jnp.int32, (groups, 1, LANES), 0)
    )
    is_upper = lax.axis_index("seq") % 2 == 1

    def spread(kind, place, head):
        chosen = jnp.full((LANES, LANES), head, jnp.int32)
        return jnp.take_along_axis(
            tails[kind, place, :], chosen, axis=1, mode="promise_in_bounds"
        )

    def one_head(head, slot):
        logs = log_ref[pl.ds(head, 1), :]
        gain_rows = [
            gains_ref[pl.ds(level * head_count + head, 1), :]
            for level in range(tile_levels + tile_bits + 2)
        ]
        for late in range(tiles):
            span = slice(late * LANES, (late + 1) * LANES)
            own = logs[:, span]
            start = late * LANES + middle
            grown = jnp.exp(own - logs[:, start : start + 1])
            corner = jnp.zeros((GROUP, LANES), F32)
            for level in range(low_bits + 1):
                gain = gain_rows[level][:, span] * grown
                corner = jnp.where(ahead & (inside == level), gain, corner)
            rest = jnp.zeros((groups, LANES), F32)
            for level in range(low_bits + 1, tile_levels + 1):
                gain = gain_rows[level][:, span] * grown
                rest = jnp.where(before & (between == level - low_bits), gain, rest)
            chosen = jnp.where(same, corner[None], rest[:, None, :]).reshape(LANES, LANES)
            weight = chosen * spread(0, span, head) * scores[span, span]
            weights[slot, span, span] = weight.astype(BF16)
            for bit in range(tile_bits):
                if late >> bit & 1 == 0:
                    continue
                edge = (late >> bit << bit) * LANES - 1
                level = tile_levels + 1 + bit
                factor = gain_rows[level][:, span] * jnp.exp(
                    own - logs[:, edge : edge + 1]
                )
                for early in range(((late >> bit) - 1) << bit, (late >> bit) << bit):
                    place = slice(early * LANES, (early + 1) * LANES)
                    weight = spread(1 + bit, place, head) * factor * scores[place, span]
                    weights[slot, place, span] = weight.astype(BF16)
        at = pl.ds(pl.multiple_of(head * LANES, LANES), LANES)
        level = tile_levels + tile_bits + 1
        factor = gain_rows[level] * jnp.exp(jnp.where(is_upper, logs, -1e30))
        far = product(node_ref[at, :], queries) * factor
        for start in range(0, rows, wide):
            upto = start + wide
            near_ref[at, start:upto] = far[:, start:upto] + product(
                acts_ref[at, :upto], weights[slot, :upto, start:upto]
            )

    def some_heads(step, carry):
        for slot in range(weights.shape[0]):
            one_head(step * weights.shape[0] + slot, slot)
        return carry

    lax.fori_loop(heads[0] // weights.shape[0], heads[1] // weights.shape[0], some_heads, 0)


def near(acts, maps, log, gains, node, after, gain, earlier, heads):
    head_count, rows = log.shape
    wide = min(rows, 2 * LANES)
    tile_bits = (rows // LANES).bit_length() - 1
    first = earlier is None
    out_shape = [pltpu.VMEM((head_count * LANES, rows), F32)]
    operands = [acts, maps, log, gains, node, after]
    aliases = {}
    if first:
        out_shape.append(pltpu.VMEM((rows, rows), F32))
        out_shape.append(pltpu.VMEM((1 + tile_bits, rows, LANES), F32))
        out_shape.append(pltpu.VMEM((LANES, LANES), F32))
        operands.append(gain.reshape(head_count, LANES))
    else:
        near_term, scores, tails, _ = earlier
        operands += [scores, tails, near_term]
        aliases = {len(operands) - 1: 0}
    made = pl.pallas_call(
        functools.partial(near_kernel, first=first, wide=wide, heads=heads),
        in_specs=[VMEM_SPEC] * len(operands),
        out_specs=[VMEM_SPEC] * len(out_shape),
        out_shape=out_shape,
        input_output_aliases=aliases,
        scratch_shapes=[
            pltpu.VMEM((LANES, rows), F32),
            pltpu.VMEM((2, rows, rows), BF16),
        ],
        compiler_params=params(),
        cost_estimate=pl.CostEstimate(
            flops=2 * head_count * rows * rows * LANES, bytes_accessed=10 << 20, transcendentals=0
        ),
        name="near",
    )(*in_vmem(*operands))
    return made if first else [made[0], *earlier[1:]]


def far_product(node_ref, first_row, count, queries):
    return product(node_ref[first_row : first_row + count, :], queries)


def far_factor(gains_ref, log_ref, stats_ref, head, level, base):
    is_upper = (lax.axis_index("seq") >> level) % 2 == 1
    shift = stats_ref[1, pl.ds(head, 1), :][:, :1]
    exponent = jnp.where(is_upper, log_ref[pl.ds(head, 1), :] + shift, -1e30)
    row = (base + level) * log_ref.shape[0] + head
    return gains_ref[pl.ds(row, 1), :] * jnp.exp(exponent)


def middle_kernel(*refs, places, relatives, levels, shards):
    count = len(places)
    acts_ref, log_ref, gains_ref = refs[:3]
    stats = refs[3 : 3 + count]
    sources = refs[3 + count : -2]
    total_ref = refs[-1]
    head_count, _ = log_ref.shape
    part = head_count // shards * LANES
    inner = head_count * LANES
    state_size = acts_ref.shape[0] - inner >> 1
    shard = lax.axis_index("seq") % shards
    base = gains_ref.shape[0] // head_count - levels
    queries = acts_ref[inner + state_size :, :]
    for relative in relatives:
        terms = []
        for slot in range(count):
            source, start = places[slot][relative]
            terms.append(far_product(sources[source], start, part, queries))
        for local in range(head_count // shards):
            head = (relative ^ shard) * (head_count // shards) + local
            at = pl.ds(pl.multiple_of(head * LANES, LANES), LANES)
            total = total_ref[at, :]
            for slot in range(count):
                factor = far_factor(gains_ref, log_ref, stats[slot], head, slot + 1, base)
                total = total + terms[slot][local * LANES : (local + 1) * LANES] * factor
            total_ref[at, :] = total


def middle(
    near_term, acts, log, gains, stats, sources, places, relatives, levels, shards
):
    operands = [acts, log, gains, *stats, *sources, near_term]
    return pl.pallas_call(
        functools.partial(
            middle_kernel, places=places, relatives=relatives, levels=levels, shards=shards
        ),
        in_specs=[VMEM_SPEC] * len(operands),
        out_specs=VMEM_SPEC,
        out_shape=pltpu.VMEM(near_term.shape, F32),
        input_output_aliases={len(operands) - 1: 0},
        compiler_params=params(),
        cost_estimate=small_cost(),
        name="middle",
    )(*in_vmem(*operands))


def last_kernel(
    total_ref, acts_ref, log_ref, gains_ref, columns_ref, stats_ref, node_ref, *refs,
    level, relatives, done, shards, base
):
    head_count, rows = log_ref.shape
    share = head_count // shards
    part = share * LANES
    inner = head_count * LANES
    state_size = acts_ref.shape[0] - inner >> 1
    shard = lax.axis_index("seq") % shards
    queries = acts_ref[inner + state_size :, :]
    copies = []
    if done:
        out_hbm, mixed_ref, sems = refs[-3:]

    def send(source_ref, place, relative, first, count):
        start = pl.multiple_of((relative ^ shard) * part, part)
        copies.append(
            pltpu.make_async_copy(
                source_ref.at[place, pl.ds(first, count), :],
                out_hbm.at[pl.ds(first, count), pl.ds(start, part)],
                sems.at[len(copies)],
            )
        )
        copies[-1].start()

    if done:
        for relative, source_ref in zip(done, refs):
            send(source_ref, 0, relative, 0, rows)
    else:
        (mixed_ref,) = refs
    for place, relative in enumerate(relatives):
        term = far_product(node_ref, place * part, part, queries)
        heads = [(relative ^ shard) * share + local for local in range(share)]
        places = [pl.ds(pl.multiple_of(head * LANES, LANES), LANES) for head in heads]
        factors = [
            far_factor(gains_ref, log_ref, stats_ref, head, level, base) for head in heads
        ]
        gain_columns = [
            jnp.take_along_axis(
                columns_ref[...],
                jnp.full((LANES, LANES), head, jnp.int32),
                axis=1,
                mode="promise_in_bounds",
            )
            for head in heads
        ]
        for first in range(0, rows, LANES):
            span = slice(first, first + LANES)
            for local in range(share):
                own = term[local * LANES : (local + 1) * LANES, span]
                total = total_ref[places[local], span] + own * factors[local][:, span]
                mean = jnp.mean(total * total, axis=0, keepdims=True)
                scale = lax.rsqrt(mean + 1e-05)
                mixed = (total * scale * gain_columns[local]).astype(BF16).T
                mixed_ref[place, span, local * LANES : (local + 1) * LANES] = mixed
            if done:
                send(mixed_ref, place, relative, first, LANES)
    for copy in copies:
        copy.wait()


def last(total, acts, log, gains, columns, stats, node, level, levels, relatives, shards, done):
    head_count, rows = log.shape
    share = head_count // shards
    operands = [total, acts, log, gains, columns, stats, node, *done.values()]
    mixed = pltpu.VMEM((len(relatives), rows, share * LANES), BF16)
    copies = len(done) + len(relatives) * rows // LANES
    whole = jax.ShapeDtypeStruct((rows, head_count * LANES), BF16)
    return pl.pallas_call(
        functools.partial(
            last_kernel, level=level, relatives=relatives, done=tuple(done), shards=shards,
            base=gains.shape[0] // head_count - levels,
        ),
        in_specs=[VMEM_SPEC] * len(operands),
        out_specs=HBM_SPEC if done else VMEM_SPEC,
        out_shape=whole if done else mixed,
        scratch_shapes=[mixed, pltpu.SemaphoreType.DMA((copies,))] if done else [],
        compiler_params=params(),
        cost_estimate=small_cost(),
        name="last",
    )(*in_vmem(*operands))


def moved(value, apart):
    return lax.ppermute(value, "seq", [(i, i ^ apart) for i in range(lax.axis_size("seq"))])


def onward(devices):
    route = {index: index + 1 for index in range(devices)}
    planes = devices // 4
    target = 0
    for plane in range(1, planes - 1):
        route[4 * plane + 2] = target
        target = 4 * plane + 3
    route[devices - 1] = target
    return list(route.items())


def on_device(xbc, conv_weight, log_decay, level_weights, gain):
    rows = xbc.shape[0]
    head_count = log_decay.shape[0]
    devices = lax.axis_size("seq")
    levels = devices.bit_length() - 1
    shards = 4
    part = head_count * LANES // shards
    gains = level_weights.transpose(1, 0, 2).reshape(-1, rows)
    beyond = onward(devices)
    early = head_count // 4
    values, taps, log, edge, acts, head, maps, state = load(xbc, conv_weight, log_decay, early)
    far_edge = lax.ppermute(edge, "seq", beyond)
    near_edge = moved(edge, 1)
    acts, head, state = front(values, taps, log, maps, acts, head, state, early)
    acts, maps, state, message = edge_rows(
        far_edge, near_edge, log, taps, values, head, acts, maps, state
    )
    first_node = moved(message, 1)
    own, stats, send, rest = pair(state, log, first_node, shards)
    near_made = None
    all_stats = [stats]
    got = []
    for bit in range(1, levels - 1):
        got.append(moved(send, 1 << bit))
        if bit <= 2:
            half = head_count // 2
            heads = (half * (bit - 1), half * bit)
            near_made = near(
                acts, maps, log, gains, first_node, stats, gain, near_made, heads
            )
        sources = [rest, *got[1:]] if bit == levels - 2 else []
        stats, send, own = join(own, stats, got[-1], near_made[0], bit, shards, sources)
        all_stats.append(stats)
    top = levels - 1

    across = moved(own, 2)
    node = moved(send, 1 << top)
    count = len(got)
    shared = (acts, log, gains, all_stats[:count])
    direct = [{0: (slot, 0), 2: (count, slot * part)} for slot in range(count)]
    relayed = [{1: (slot, 0), 3: (count + slot, 0)} for slot in range(count)]
    total = middle(near_made[0], *shared, [*got, across], direct, (0, 2), levels, shards)
    node, total = lax.optimization_barrier((node, total))
    common = (acts, log, gains, near_made[3], all_stats[-1])
    node_across = moved(node, 2)
    own_done = last(total, *common, node, top, levels, (0,), shards, {})
    shares = [kept[:part] for kept in got]
    shares += [across[slot * part : (slot + 1) * part] for slot in range(count)]
    own_done, shares = lax.optimization_barrier((own_done, shares))
    beside = [moved(kept, 1) for kept in shares]
    node_across, beside, total = lax.optimization_barrier((node_across, beside, total))
    node_beside = moved(jnp.concatenate([node, node_across]), 1)
    total = middle(total, *shared, beside, relayed, (1, 3), levels, shards)
    across_done = last(total, *common, node_across, top, levels, (2,), shards, {})
    done = {0: own_done, 2: across_done}
    return last(total, *common, node_beside, top, levels, (1, 3), shards, done)


def solution(mesh):
    in_specs = (
        P(("groups", "seq"), None),
        P(),
        P(None, ("groups", "seq")),
        P(None, None, ("groups", "seq")),
        P(),
    )
    out_specs = P(("groups", "seq"), None)
    return jax.shard_map(
        on_device, mesh=mesh, in_specs=in_specs, out_specs=out_specs, check_vma=False
    )
```

```python
import functools

import jax
import jax.numpy as jnp
from jax import lax
from jax.experimental import pallas as pl
from jax.experimental.pallas import tpu as pltpu
from jax.sharding import PartitionSpec as P

F32 = jnp.float32
BF16 = jnp.bfloat16
LANES = 128
GROUP = 8
PARTS = 4
VMEM_LIMIT = 24 << 20
HBM_SPEC = pl.BlockSpec(memory_space=pltpu.HBM)
VMEM_SPEC = pl.BlockSpec(memory_space=pltpu.VMEM)


def in_vmem(*arrays):
    return [pltpu.with_memory_space_constraint(array, pltpu.VMEM) for array in arrays]


def in_hbm(*arrays):
    return [pltpu.with_memory_space_constraint(array, pltpu.HBM) for array in arrays]


def params():
    return pltpu.CompilerParams(vmem_limit_bytes=VMEM_LIMIT)


def small_cost():
    return pl.CostEstimate(flops=1024, bytes_accessed=1024, transcendentals=0)


def product(left, right):
    return jnp.dot(left, right, preferred_element_type=F32)


def write_spans(message_ref, first_row, spans):
    head_count = spans.shape[0]
    place = lax.broadcasted_iota(jnp.int32, spans.shape, 1) // (LANES // PARTS)
    packed = jnp.zeros(spans.shape, F32)
    for part in range(PARTS - 1):
        rounded = spans.astype(BF16).astype(F32)
        packed = jnp.where(place == part, rounded, packed)
        spans = spans - rounded
    message_ref[first_row : first_row + head_count, :] = packed.astype(BF16)


def read_spans(message_ref, first_row, head_count):
    total = message_ref[first_row : first_row + head_count, :].astype(F32)
    width = LANES // PARTS
    while width < LANES:
        total = total + pltpu.roll(total, width, 1)
        width *= 2
    return total


def running_sum(logs):
    head_count, rows = logs.shape
    tiles = rows // LANES
    row = lax.broadcasted_iota(jnp.int32, (LANES, LANES), 0)
    column = lax.broadcasted_iota(jnp.int32, (LANES, LANES), 1)
    upto = (row <= column).astype(BF16)
    left = jnp.concatenate(
        [logs[:, tile * LANES : (tile + 1) * LANES] for tile in range(tiles)], axis=0
    )
    pieces = []
    for _ in range(3):
        pieces.append(left.astype(BF16))
        left = left - pieces[-1].astype(F32)
    size = head_count * tiles
    added = product(jnp.concatenate(pieces, axis=0), upto)
    within = added[2 * size :] + added[size : 2 * size] + added[:size]
    sums = []
    offset = jnp.zeros((head_count, 1), F32)
    for tile in range(tiles):
        part = within[tile * head_count : (tile + 1) * head_count]
        sums.append(part + offset)
        offset = offset + part[:, LANES - 1 :]
    return jnp.concatenate(sums, axis=1)


def activated(values, edge, weights, padded):
    rows = values.shape[0]
    taps = weights.shape[0]
    padded[GROUP : GROUP + rows, :] = values
    if edge is not None:
        padded[GROUP - taps + 1 : GROUP, :] = edge
    total = None
    for tap in range(taps):
        first = GROUP - taps + 1 + tap
        shifted = values if tap == taps - 1 else padded[first : first + rows, :]
        term = shifted * weights[tap : tap + 1]
        total = term if total is None else total + term
    return (total * jax.nn.sigmoid(total)).astype(BF16)


def some_columns(xbc_ref, taps_ref, acts_ref, head_ref, padded, start):
    part = slice(start, start + LANES)
    values = xbc_ref[:, part].astype(F32)
    result = activated(values, None, taps_ref[:, part], padded)
    head_ref[:, part] = result[:LANES]
    turned = result[LANES:].T
    acts_ref[part, LANES:] = turned
    return result, turned


def head_columns(
    xbc_ref, taps_ref, log_ref, maps_ref, acts_ref, head_ref, state_ref, padded, heads
):
    rows, _ = xbc_ref.shape
    for head in heads:
        place = slice(head * LANES, (head + 1) * LANES)
        _, turned = some_columns(
            xbc_ref, taps_ref, acts_ref, head_ref, padded.at[head % 2], head * LANES
        )
        logs = log_ref[head : head + 1, :]
        tail = jnp.exp(logs[:, rows - 1 : rows] - logs[:, LANES:])
        decayed = (turned.astype(F32) * tail).astype(BF16)
        state_ref[place, :] = product(decayed, maps_ref[LANES:, :])


def load_kernel(
    xbc_hbm, taps_hbm, decay_hbm, xbc_ref, taps_ref, log_ref, edge_ref, acts_ref, head_ref,
    maps_ref, state_ref, decay_buf, padded, sems, early
):
    rows, width = xbc_ref.shape
    pieces = sems.shape[0] - 2
    maps_width = 2 * maps_ref.shape[1]
    inner = width - maps_width
    rest = (inner - early * LANES) // (pieces - 2)
    cuts = [0] + [early * LANES + piece * rest for piece in range(pieces - 1)]
    spans = [(inner, maps_width)] + [(x, y - x) for x, y in zip(cuts, cuts[1:])]
    copies = [
        pltpu.make_async_copy(decay_hbm, decay_buf, sems.at[pieces]),
        pltpu.make_async_copy(taps_hbm, taps_ref, sems.at[pieces + 1]),
    ]
    for piece, (start, size) in enumerate(spans):
        part = pl.ds(start, size)
        copies.append(
            pltpu.make_async_copy(xbc_hbm.at[:, part], xbc_ref.at[:, part], sems.at[piece])
        )
    for copy in copies[:4]:
        copy.start()
    for copy in copies[4:]:
        copy.start()
    copies[0].wait()
    log_ref[...] = running_sum(decay_buf[...])
    copies[1].wait()
    copies[2].wait()
    for slot, start in enumerate(range(width - LANES, inner - 1, -LANES)):
        result, _ = some_columns(
            xbc_ref, taps_ref, acts_ref, head_ref, padded.at[slot % 2], start
        )
    maps_ref[...] = result
    copies[3].wait()
    head_columns(
        xbc_ref, taps_ref, log_ref, maps_ref, acts_ref, head_ref, state_ref, padded, range(early)
    )
    for copy in copies[4:]:
        copy.wait()
    few = edge_ref.shape[0]
    tail = xbc_ref[rows - 2 * GROUP :, :].astype(F32)
    edge_ref[...] = tail[2 * GROUP - few :].astype(BF16)


def load(xbc, conv_weight, log_decay, early):
    rows, width = xbc.shape
    inner = log_decay.shape[0] * LANES
    state_size = (width - inner) // 2
    pieces = 3
    return pl.pallas_call(
        functools.partial(load_kernel, early=early),
        in_specs=[HBM_SPEC] * 3,
        out_specs=[VMEM_SPEC] * 8,
        out_shape=[
            pltpu.VMEM(xbc.shape, BF16),
            pltpu.VMEM(conv_weight.shape, F32),
            pltpu.VMEM(log_decay.shape, F32),
            pltpu.VMEM((conv_weight.shape[0] - 1, width), BF16),
            pltpu.VMEM((width, rows), BF16),
            pltpu.VMEM((LANES, width), BF16),
            pltpu.VMEM((rows, state_size), BF16),
            pltpu.VMEM((inner, state_size), F32),
        ],
        scratch_shapes=[
            pltpu.VMEM(log_decay.shape, F32),
            pltpu.VMEM((2, rows + GROUP, LANES), F32),
            pltpu.SemaphoreType.DMA((pieces + 2,)),
        ],
        compiler_params=params(),
        cost_estimate=small_cost(),
        name="load",
    )(*in_hbm(xbc, conv_weight, log_decay))


def front_kernel(
    xbc_ref, taps_ref, log_ref, maps_ref, acts_in, head_in, state_in, acts_ref, head_ref,
    state_ref, padded, early
):
    head_columns(
        xbc_ref, taps_ref, log_ref, maps_ref, acts_ref, head_ref, state_ref, padded,
        range(early, log_ref.shape[0]),
    )


def front(xbc, taps, log, maps, acts, head, state, early):
    rows, _ = xbc.shape
    operands = [xbc, taps, log, maps, acts, head, state]
    return pl.pallas_call(
        functools.partial(front_kernel, early=early),
        in_specs=[VMEM_SPEC] * len(operands),
        out_specs=[VMEM_SPEC] * 3,
        out_shape=[
            pltpu.VMEM(acts.shape, BF16),
            pltpu.VMEM(head.shape, BF16),
            pltpu.VMEM(state.shape, F32),
        ],
        input_output_aliases={4: 0, 5: 1, 6: 2},
        scratch_shapes=[pltpu.VMEM((2, rows + GROUP, LANES), F32)],
        compiler_params=params(),
        name="front",
    )(*in_vmem(*operands))


def edge_kernel(
    far_edge_ref, near_edge_ref, log_ref, taps_ref, xbc_ref, head_ref, *refs, shards
):
    acts_ref, maps_ref, state_ref, away_ref, home_ref, padded = refs[-6:]
    head_count, rows = log_ref.shape
    width = head_ref.shape[1]
    inner = head_count * LANES
    few = 2 * GROUP
    index = lax.axis_index("seq")

    def first_tile(start, slot):
        part = slice(start, start + LANES)
        near_edge = near_edge_ref[:, part].astype(F32)
        far_edge = far_edge_ref[:, part].astype(F32)
        edge = jnp.where(index % 2 == 1, near_edge, jnp.where(index == 0, 0.0, far_edge))
        values = xbc_ref[:few, part].astype(F32)
        result = activated(values, edge, taps_ref[:, part], padded.at[slot])
        block = jnp.concatenate([result, head_ref[few:, part]], axis=0)
        turned = block.T
        acts_ref[part, :LANES] = turned
        return block, turned

    first_tile(width - LANES, 0)
    maps, _ = first_tile(width - 2 * LANES, 1)
    maps_ref[:LANES, :] = maps
    totals = jnp.broadcast_to(log_ref[:, rows - 1 : rows], (head_count, LANES))
    write_spans(away_ref, inner // 2, totals)
    parity = index % 2
    for head in range(head_count):
        part = slice(head * LANES, (head + 1) * LANES)
        _, turned = first_tile(head * LANES, head % padded.shape[0])
        logs = log_ref[head : head + 1, :]
        tail = jnp.exp(logs[:, rows - 1 : rows] - logs[:, :LANES])
        decayed = (turned.astype(F32) * tail).astype(BF16)
        state = state_ref[part, :] + product(decayed, maps)
        state_ref[part, :] = state
    part = inner // shards
    for slot in range(shards // 2):
        place = slice(slot * part, (slot + 1) * part)
        kept = pl.multiple_of((2 * slot + parity) * part, part)
        given = pl.multiple_of((2 * slot + 1 - parity) * part, part)
        away_ref[place, :] = state_ref[pl.ds(given, part), :].astype(BF16)
        home_ref[place, :] = state_ref[pl.ds(kept, part), :].astype(BF16)


def edge_rows(far_edge, near_edge, log, taps, xbc, head, acts, maps, state, shards):
    head_count, _ = log.shape
    inner, state_size = state.shape
    operands = [far_edge, near_edge, log, taps, xbc, head, acts, maps, state]
    return pl.pallas_call(
        functools.partial(edge_kernel, shards=shards),
        in_specs=[VMEM_SPEC] * len(operands),
        out_specs=[VMEM_SPEC] * 5,
        out_shape=[
            pltpu.VMEM(acts.shape, BF16),
            pltpu.VMEM(maps.shape, BF16),
            pltpu.VMEM(state.shape, F32),
            pltpu.VMEM((inner // 2 + head_count, state_size), BF16),
            pltpu.VMEM((inner // 2, state_size), BF16),
        ],
        input_output_aliases={6: 0, 7: 1, 8: 2},
        scratch_shapes=[pltpu.VMEM((2, 3 * GROUP, LANES), F32)],
        compiler_params=params(),
        cost_estimate=small_cost(),
        name="edge",
    )(*in_vmem(*operands))


def pair_kernel(state_ref, log_ref, got_ref, own_ref, stats_ref, send_ref, rest_ref, shards):
    head_count, rows = log_ref.shape
    inner = state_ref.shape[0]
    index = lax.axis_index("seq")
    is_upper = index % 2 == 1
    mine = jnp.broadcast_to(log_ref[:, rows - 1 : rows], (head_count, LANES))
    theirs = read_spans(got_ref, inner // 2, head_count)
    stats_ref[0] = mine + theirs
    stats_ref[1] = jnp.where(is_upper, theirs, 0.0)
    write_spans(send_ref, inner // shards, mine + theirs)
    stats_ref[2] = jnp.exp(mine)
    stats_ref[3] = jnp.exp(theirs)
    shard = index % shards
    share = head_count // shards

    def joined(owner, local):
        head = owner * share + local
        at = pl.ds(pl.multiple_of(head * LANES, LANES), LANES)
        own = state_ref[at, :]
        start = pl.multiple_of((owner // 2 * share + local) * LANES, LANES)
        got = got_ref[pl.ds(start, LANES), :].astype(F32)
        late = jnp.where(is_upper, own, got)
        early = jnp.where(is_upper, got, own)
        late_row = jnp.where(is_upper, 2, 3)
        return early * stats_ref[late_row, pl.ds(head, 1), :] + late

    for local in range(share):
        place = slice(local * LANES, (local + 1) * LANES)
        send_ref[place, :] = joined(shard ^ 2, local).astype(BF16)
        kept = joined(shard, local)
        own_ref[place, :] = kept
        rest_ref[place, :] = kept.astype(BF16)


def pair(state, log, got, shards):
    head_count, _ = log.shape
    inner, state_size = state.shape
    part = inner // shards
    return pl.pallas_call(
        functools.partial(pair_kernel, shards=shards),
        in_specs=[VMEM_SPEC] * 3,
        out_specs=[VMEM_SPEC] * 4,
        out_shape=[
            pltpu.VMEM((part, state_size), F32),
            pltpu.VMEM((4, head_count, LANES), F32),
            pltpu.VMEM((part + head_count, state_size), BF16),
            pltpu.VMEM((part, state_size), BF16),
        ],
        compiler_params=params(),
        cost_estimate=small_cost(),
        name="pair",
    )(*in_vmem(state, log, got))


def join_kernel(own_ref, stats_ref, got_ref, _, *refs, bit, shards, gathered):
    sources = refs[:gathered]
    if gathered:
        next_stats_ref, send_ref, across_ref = refs[gathered:]
    else:
        next_stats_ref, send_ref, next_ref = refs
    part = own_ref.shape[0]
    head_count = stats_ref.shape[1]
    share = head_count // shards
    index = lax.axis_index("seq")
    is_upper = (index >> bit) % 2 == 1
    mine = stats_ref[0]
    theirs = read_spans(got_ref, part, head_count)
    next_stats_ref[0] = mine + theirs
    next_stats_ref[1] = stats_ref[1] + jnp.where(is_upper, theirs, 0.0)
    next_stats_ref[2] = jnp.exp(jnp.where(is_upper, mine, theirs))
    next_stats_ref[3] = jnp.zeros_like(mine)
    if not gathered:
        write_spans(send_ref, part, mine + theirs)
    for local in range(share):
        place = slice(local * LANES, (local + 1) * LANES)
        head = (index % shards) * share + local
        own = own_ref[place, :]
        got = got_ref[place, :].astype(F32)
        late = jnp.where(is_upper, own, got)
        early = jnp.where(is_upper, got, own)
        total = early * next_stats_ref[2, pl.ds(head, 1), :] + late
        send_ref[place, :] = total.astype(BF16)
        if not gathered:
            next_ref[place, :] = total
    for slot in range(gathered):
        across_ref[slot * part : (slot + 1) * part, :] = sources[slot][:part, :]


def join(own, stats, got, after, bit, shards, sources):
    operands = [own, stats, got, after, *sources]
    message = own.shape if sources else got.shape
    out_shape = [pltpu.VMEM(stats.shape, F32), pltpu.VMEM(message, BF16)]
    if sources:
        out_shape.append(pltpu.VMEM((len(sources) * own.shape[0], own.shape[1]), BF16))
    else:
        out_shape.append(pltpu.VMEM(own.shape, F32))
    return pl.pallas_call(
        functools.partial(join_kernel, bit=bit, shards=shards, gathered=len(sources)),
        in_specs=[VMEM_SPEC] * len(operands),
        out_specs=[VMEM_SPEC] * 3,
        out_shape=out_shape,
        compiler_params=params(),
        cost_estimate=small_cost(),
        name="join",
    )(*in_vmem(*operands))


def bit_length(numbers, limit):
    counted = jnp.zeros(numbers.shape, jnp.int32)
    for power in range(limit):
        counted = counted + (numbers >= 1 << power).astype(jnp.int32)
    return counted


def near_kernel(*refs, first, wide, heads, shards):
    if first:
        acts_ref, maps_ref, log_ref, gains_ref, node_ref, _, gain_ref = refs[:7]
        near_ref, scores, tails, columns_ref, turned, weights = refs[7:]
    else:
        acts_ref, maps_ref, log_ref, gains_ref, node_ref, _, scores, tails, _ = refs[:9]
        near_ref, turned, weights = refs[9:]
    head_count, rows = log_ref.shape
    inner = head_count * LANES
    state_size = maps_ref.shape[1]
    tiles = rows // LANES
    tile_bits = tiles.bit_length() - 1
    groups = LANES // GROUP
    low_bits = GROUP.bit_length() - 1
    tile_levels = LANES.bit_length() - 1
    queries = acts_ref[inner + state_size :, :]
    middle = LANES // 2 - 1
    if first:
        for start in range(0, rows, wide):
            upto = start + wide
            scores[:upto, start:upto] = product(maps_ref[:upto, :], queries[:, start:upto])
        turned[head_count:, :] = jnp.zeros((LANES - head_count, rows), F32)
        turned[:head_count, :LANES] = gain_ref[...]
        columns_ref[...] = turned[:, :LANES].T
        turned[:head_count, :] = log_ref[...]
        columns = [turned[:, tile * LANES : (tile + 1) * LANES].T for tile in range(tiles)]
        for tile in range(tiles):
            place = slice(tile * LANES, (tile + 1) * LANES)
            tails[0, place, :] = jnp.exp(columns[tile][middle : middle + 1] - columns[tile])
            for bit in range(tile_bits):
                if tile >> bit & 1 == 0:
                    edge = ((tile >> bit) + 1 << bit) - 1
                    tails[1 + bit, place, :] = jnp.exp(columns[edge][LANES - 1 :] - columns[tile])
    for late in range(tiles):
        for early in range(tiles):
            if early > late:
                weights[
                    :, early * LANES : (early + 1) * LANES, late * LANES : (late + 1) * LANES
                ] = jnp.zeros((weights.shape[0], LANES, LANES), BF16)
    lane = lax.broadcasted_iota(jnp.int32, (GROUP, LANES), 1)
    row = lax.broadcasted_iota(jnp.int32, (GROUP, LANES), 0)
    inside = bit_length((lane % GROUP) ^ row, low_bits)
    ahead = row <= lane % GROUP
    lane_group = lax.broadcasted_iota(jnp.int32, (groups, LANES), 1) // GROUP
    row_group = lax.broadcasted_iota(jnp.int32, (groups, LANES), 0)
    between = bit_length(lane_group ^ row_group, groups.bit_length() - 1)
    before = row_group < lane_group
    same = (
        lax.broadcasted_iota(jnp.int32, (groups, 1, LANES), 2) // GROUP
        == lax.broadcasted_iota(jnp.int32, (groups, 1, LANES), 0)
    )
    index = lax.axis_index("seq")
    is_upper = index % 2 == 1
    share = head_count // shards

    def spread(kind, place, head):
        chosen = jnp.full((LANES, LANES), head, jnp.int32)
        return jnp.take_along_axis(
            tails[kind, place, :], chosen, axis=1, mode="promise_in_bounds"
        )

    def one_head(head, slot):
        logs = log_ref[pl.ds(head, 1), :]
        gain_rows = [
            gains_ref[pl.ds(level * head_count + head, 1), :]
            for level in range(tile_levels + tile_bits + 2)
        ]
        for late in range(tiles):
            span = slice(late * LANES, (late + 1) * LANES)
            own = logs[:, span]
            start = late * LANES + middle
            grown = jnp.exp(own - logs[:, start : start + 1])
            corner = jnp.zeros((GROUP, LANES), F32)
            for level in range(low_bits + 1):
                gain = gain_rows[level][:, span] * grown
                corner = jnp.where(ahead & (inside == level), gain, corner)
            rest = jnp.zeros((groups, LANES), F32)
            for level in range(low_bits + 1, tile_levels + 1):
                gain = gain_rows[level][:, span] * grown
                rest = jnp.where(before & (between == level - low_bits), gain, rest)
            chosen = jnp.where(same, corner[None], rest[:, None, :]).reshape(LANES, LANES)
            weight = chosen * spread(0, span, head) * scores[span, span]
            weights[slot, span, span] = weight.astype(BF16)
            for bit in range(tile_bits):
                if late >> bit & 1 == 0:
                    continue
                edge = (late >> bit << bit) * LANES - 1
                level = tile_levels + 1 + bit
                factor = gain_rows[level][:, span] * jnp.exp(
                    own - logs[:, edge : edge + 1]
                )
                for early in range(((late >> bit) - 1) << bit, (late >> bit) << bit):
                    place = slice(early * LANES, (early + 1) * LANES)
                    weight = spread(1 + bit, place, head) * factor * scores[place, span]
                    weights[slot, place, span] = weight.astype(BF16)
        at = pl.ds(pl.multiple_of(head * LANES, LANES), LANES)
        level = tile_levels + tile_bits + 1
        factor = gain_rows[level] * jnp.exp(jnp.where(is_upper, logs, -1e30))
        owner, local = head // share, head % share
        start = jnp.where(owner % 2 == index % 2, 0, inner // 2)
        start = start + (owner // 2 * share + local) * LANES
        node = node_ref[pl.ds(pl.multiple_of(start, LANES), LANES), :]
        far = product(node, queries) * factor
        for start in range(0, rows, wide):
            upto = start + wide
            near_ref[at, start:upto] = far[:, start:upto] + product(
                acts_ref[at, :upto], weights[slot, :upto, start:upto]
            )

    def some_heads(step, carry):
        for slot in range(weights.shape[0]):
            one_head(step * weights.shape[0] + slot, slot)
        return carry

    lax.fori_loop(heads[0] // weights.shape[0], heads[1] // weights.shape[0], some_heads, 0)


def near(acts, maps, log, gains, node, after, gain, earlier, heads, shards):
    head_count, rows = log.shape
    wide = min(rows, 2 * LANES)
    tile_bits = (rows // LANES).bit_length() - 1
    first = earlier is None
    out_shape = [pltpu.VMEM((head_count * LANES, rows), F32)]
    operands = [acts, maps, log, gains, node, after]
    aliases = {}
    if first:
        out_shape.append(pltpu.VMEM((rows, rows), F32))
        out_shape.append(pltpu.VMEM((1 + tile_bits, rows, LANES), F32))
        out_shape.append(pltpu.VMEM((LANES, LANES), F32))
        operands.append(gain.reshape(head_count, LANES))
    else:
        near_term, scores, tails, _ = earlier
        operands += [scores, tails, near_term]
        aliases = {len(operands) - 1: 0}
    made = pl.pallas_call(
        functools.partial(near_kernel, first=first, wide=wide, heads=heads, shards=shards),
        in_specs=[VMEM_SPEC] * len(operands),
        out_specs=[VMEM_SPEC] * len(out_shape),
        out_shape=out_shape,
        input_output_aliases=aliases,
        scratch_shapes=[
            pltpu.VMEM((LANES, rows), F32),
            pltpu.VMEM((2, rows, rows), BF16),
        ],
        compiler_params=params(),
        cost_estimate=pl.CostEstimate(
            flops=2 * head_count * rows * rows * LANES, bytes_accessed=10 << 20, transcendentals=0
        ),
        name="near",
    )(*in_vmem(*operands))
    return made if first else [made[0], *earlier[1:]]


def far_product(node_ref, first_row, count, queries):
    return product(node_ref[first_row : first_row + count, :], queries)


def far_factor(gains_ref, log_ref, stats_ref, head, level, base):
    is_upper = (lax.axis_index("seq") >> level) % 2 == 1
    shift = stats_ref[1, pl.ds(head, 1), :][:, :1]
    exponent = jnp.where(is_upper, log_ref[pl.ds(head, 1), :] + shift, -1e30)
    row = (base + level) * log_ref.shape[0] + head
    return gains_ref[pl.ds(row, 1), :] * jnp.exp(exponent)


def middle_kernel(*refs, places, relatives, levels, shards):
    count = len(places)
    acts_ref, log_ref, gains_ref = refs[:3]
    stats = refs[3 : 3 + count]
    sources = refs[3 + count : -2]
    total_ref = refs[-1]
    head_count, _ = log_ref.shape
    part = head_count // shards * LANES
    inner = head_count * LANES
    state_size = acts_ref.shape[0] - inner >> 1
    shard = lax.axis_index("seq") % shards
    base = gains_ref.shape[0] // head_count - levels
    queries = acts_ref[inner + state_size :, :]
    for relative in relatives:
        terms = []
        for slot in range(count):
            source, start = places[slot][relative]
            terms.append(far_product(sources[source], start, part, queries))
        for local in range(head_count // shards):
            head = (relative ^ shard) * (head_count // shards) + local
            at = pl.ds(pl.multiple_of(head * LANES, LANES), LANES)
            total = total_ref[at, :]
            for slot in range(count):
                factor = far_factor(gains_ref, log_ref, stats[slot], head, slot + 1, base)
                total = total + terms[slot][local * LANES : (local + 1) * LANES] * factor
            total_ref[at, :] = total


def middle(
    near_term, acts, log, gains, stats, sources, places, relatives, levels, shards
):
    operands = [acts, log, gains, *stats, *sources, near_term]
    return pl.pallas_call(
        functools.partial(
            middle_kernel, places=places, relatives=relatives, levels=levels, shards=shards
        ),
        in_specs=[VMEM_SPEC] * len(operands),
        out_specs=VMEM_SPEC,
        out_shape=pltpu.VMEM(near_term.shape, F32),
        input_output_aliases={len(operands) - 1: 0},
        compiler_params=params(),
        cost_estimate=small_cost(),
        name="middle",
    )(*in_vmem(*operands))


def last_kernel(
    total_ref, acts_ref, log_ref, gains_ref, columns_ref, stats_ref, node_ref, *refs,
    level, relatives, done, shards, base
):
    head_count, rows = log_ref.shape
    share = head_count // shards
    part = share * LANES
    inner = head_count * LANES
    state_size = acts_ref.shape[0] - inner >> 1
    shard = lax.axis_index("seq") % shards
    queries = acts_ref[inner + state_size :, :]
    copies = []
    if done:
        out_hbm, mixed_ref, sems = refs[-3:]

    def send(source_ref, place, relative, first, count):
        start = pl.multiple_of((relative ^ shard) * part, part)
        copies.append(
            pltpu.make_async_copy(
                source_ref.at[place, pl.ds(first, count), :],
                out_hbm.at[pl.ds(first, count), pl.ds(start, part)],
                sems.at[len(copies)],
            )
        )
        copies[-1].start()

    if done:
        for relative, source_ref in zip(done, refs):
            send(source_ref, 0, relative, 0, rows)
    else:
        (mixed_ref,) = refs
    for place, relative in enumerate(relatives):
        term = far_product(node_ref, place * part, part, queries)
        heads = [(relative ^ shard) * share + local for local in range(share)]
        places = [pl.ds(pl.multiple_of(head * LANES, LANES), LANES) for head in heads]
        factors = [
            far_factor(gains_ref, log_ref, stats_ref, head, level, base) for head in heads
        ]
        gain_columns = [
            jnp.take_along_axis(
                columns_ref[...],
                jnp.full((LANES, LANES), head, jnp.int32),
                axis=1,
                mode="promise_in_bounds",
            )
            for head in heads
        ]
        for first in range(0, rows, LANES):
            span = slice(first, first + LANES)
            for local in range(share):
                own = term[local * LANES : (local + 1) * LANES, span]
                total = total_ref[places[local], span] + own * factors[local][:, span]
                mean = jnp.mean(total * total, axis=0, keepdims=True)
                scale = lax.rsqrt(mean + 1e-05)
                mixed = (total * scale * gain_columns[local]).astype(BF16).T
                mixed_ref[place, span, local * LANES : (local + 1) * LANES] = mixed
            if done:
                send(mixed_ref, place, relative, first, LANES)
    for copy in copies:
        copy.wait()


def last(total, acts, log, gains, columns, stats, node, level, levels, relatives, shards, done):
    head_count, rows = log.shape
    share = head_count // shards
    operands = [total, acts, log, gains, columns, stats, node, *done.values()]
    mixed = pltpu.VMEM((len(relatives), rows, share * LANES), BF16)
    copies = len(done) + len(relatives) * rows // LANES
    whole = jax.ShapeDtypeStruct((rows, head_count * LANES), BF16)
    return pl.pallas_call(
        functools.partial(
            last_kernel, level=level, relatives=relatives, done=tuple(done), shards=shards,
            base=gains.shape[0] // head_count - levels,
        ),
        in_specs=[VMEM_SPEC] * len(operands),
        out_specs=HBM_SPEC if done else VMEM_SPEC,
        out_shape=whole if done else mixed,
        scratch_shapes=[mixed, pltpu.SemaphoreType.DMA((copies,))] if done else [],
        compiler_params=params(),
        cost_estimate=small_cost(),
        name="last",
    )(*in_vmem(*operands))


def moved(value, apart):
    return lax.ppermute(value, "seq", [(i, i ^ apart) for i in range(lax.axis_size("seq"))])


def onward(devices):
    route = {index: index + 1 for index in range(devices)}
    planes = devices // 4
    target = 0
    for plane in range(1, planes - 1):
        route[4 * plane + 2] = target
        target = 4 * plane + 3
    route[devices - 1] = target
    return list(route.items())


def on_device(xbc, conv_weight, log_decay, level_weights, gain):
    rows = xbc.shape[0]
    head_count = log_decay.shape[0]
    devices = lax.axis_size("seq")
    levels = devices.bit_length() - 1
    shards = 4
    part = head_count * LANES // shards
    gains = level_weights.transpose(1, 0, 2).reshape(-1, rows)
    beyond = onward(devices)
    early = head_count // 4
    values, taps, log, edge, acts, head, maps, state = load(xbc, conv_weight, log_decay, early)
    far_edge = lax.ppermute(edge, "seq", beyond)
    near_edge = moved(edge, 1)
    acts, head, state = front(values, taps, log, maps, acts, head, state, early)
    acts, maps, state, away, home = edge_rows(
        far_edge, near_edge, log, taps, values, head, acts, maps, state, shards
    )
    joined = moved(away, 1)
    first_node = jnp.concatenate([joined[: home.shape[0]], moved(home, 1)])
    own, stats, send, rest = pair(state, log, joined, shards)
    near_made = None
    all_stats = [stats]
    got = []
    for bit in range(1, levels - 1):
        got.append(moved(send, 1 << bit))
        if bit <= 2:
            half = head_count // 2
            heads = (half * (bit - 1), half * bit)
            near_made = near(
                acts, maps, log, gains, first_node, stats, gain, near_made, heads, shards
            )
        sources = [rest, *got[1:]] if bit == levels - 2 else []
        stats, send, own = join(own, stats, got[-1], near_made[0], bit, shards, sources)
        all_stats.append(stats)
    top = levels - 1

    across = moved(own, 2)
    node = moved(send, 1 << top)
    count = len(got)
    shared = (acts, log, gains, all_stats[:count])
    direct = [{0: (slot, 0), 2: (count, slot * part)} for slot in range(count)]
    relayed = [{1: (slot, 0), 3: (count + slot, 0)} for slot in range(count)]
    total = middle(near_made[0], *shared, [*got, across], direct, (0, 2), levels, shards)
    node, total = lax.optimization_barrier((node, total))
    common = (acts, log, gains, near_made[3], all_stats[-1])
    node_across = moved(node, 2)
    own_done = last(total, *common, node, top, levels, (0,), shards, {})
    shares = [kept[:part] for kept in got]
    shares += [across[slot * part : (slot + 1) * part] for slot in range(count)]
    own_done, shares = lax.optimization_barrier((own_done, shares))
    beside = [moved(kept, 1) for kept in shares]
    node_across, beside, total = lax.optimization_barrier((node_across, beside, total))
    node_beside = moved(jnp.concatenate([node, node_across]), 1)
    total = middle(total, *shared, beside, relayed, (1, 3), levels, shards)
    across_done = last(total, *common, node_across, top, levels, (2,), shards, {})
    done = {0: own_done, 2: across_done}
    return last(total, *common, node_beside, top, levels, (1, 3), shards, done)


def solution(mesh):
    in_specs = (
        P(("groups", "seq"), None),
        P(),
        P(None, ("groups", "seq")),
        P(None, None, ("groups", "seq")),
        P(),
    )
    out_specs = P(("groups", "seq"), None)
    return jax.shard_map(
        on_device, mesh=mesh, in_specs=in_specs, out_specs=out_specs, check_vma=False
    )
```

```python
import functools

import jax
import jax.numpy as jnp
from jax import lax
from jax.experimental import pallas as pl
from jax.experimental.pallas import tpu as pltpu
from jax.sharding import PartitionSpec as P

F32 = jnp.float32
BF16 = jnp.bfloat16
LANES = 128
GROUP = 8
PARTS = 4
VMEM_LIMIT = 24 << 20
HBM_SPEC = pl.BlockSpec(memory_space=pltpu.HBM)
VMEM_SPEC = pl.BlockSpec(memory_space=pltpu.VMEM)


def in_vmem(*arrays):
    return [pltpu.with_memory_space_constraint(array, pltpu.VMEM) for array in arrays]


def in_hbm(*arrays):
    return [pltpu.with_memory_space_constraint(array, pltpu.HBM) for array in arrays]


def params():
    return pltpu.CompilerParams(vmem_limit_bytes=VMEM_LIMIT)


def small_cost():
    return pl.CostEstimate(flops=1024, bytes_accessed=1024, transcendentals=0)


def product(left, right):
    return jnp.dot(left, right, preferred_element_type=F32)


def write_spans(message_ref, first_row, spans):
    head_count = spans.shape[0]
    place = lax.broadcasted_iota(jnp.int32, spans.shape, 1) // (LANES // PARTS)
    packed = jnp.zeros(spans.shape, F32)
    for part in range(PARTS - 1):
        rounded = spans.astype(BF16).astype(F32)
        packed = jnp.where(place == part, rounded, packed)
        spans = spans - rounded
    message_ref[first_row : first_row + head_count, :] = packed.astype(BF16)


def read_spans(message_ref, first_row, head_count):
    total = message_ref[first_row : first_row + head_count, :].astype(F32)
    width = LANES // PARTS
    while width < LANES:
        total = total + pltpu.roll(total, width, 1)
        width *= 2
    return total


def running_sum(logs):
    head_count, rows = logs.shape
    tiles = rows // LANES
    row = lax.broadcasted_iota(jnp.int32, (LANES, LANES), 0)
    column = lax.broadcasted_iota(jnp.int32, (LANES, LANES), 1)
    upto = (row <= column).astype(BF16)
    left = jnp.concatenate(
        [logs[:, tile * LANES : (tile + 1) * LANES] for tile in range(tiles)], axis=0
    )
    pieces = []
    for _ in range(3):
        pieces.append(left.astype(BF16))
        left = left - pieces[-1].astype(F32)
    size = head_count * tiles
    added = product(jnp.concatenate(pieces, axis=0), upto)
    within = added[2 * size :] + added[size : 2 * size] + added[:size]
    sums = []
    offset = jnp.zeros((head_count, 1), F32)
    for tile in range(tiles):
        part = within[tile * head_count : (tile + 1) * head_count]
        sums.append(part + offset)
        offset = offset + part[:, LANES - 1 :]
    return jnp.concatenate(sums, axis=1)


def activated(values, edge, weights, padded):
    rows = values.shape[0]
    taps = weights.shape[0]
    padded[GROUP : GROUP + rows, :] = values
    if edge is not None:
        padded[GROUP - taps + 1 : GROUP, :] = edge
    total = None
    for tap in range(taps):
        first = GROUP - taps + 1 + tap
        shifted = values if tap == taps - 1 else padded[first : first + rows, :]
        term = shifted * weights[tap : tap + 1]
        total = term if total is None else total + term
    return (total * jax.nn.sigmoid(total)).astype(BF16)


def some_columns(xbc_ref, taps_ref, acts_ref, head_ref, padded, start):
    part = slice(start, start + LANES)
    values = xbc_ref[:, part].astype(F32)
    result = activated(values, None, taps_ref[:, part], padded)
    head_ref[:, part] = result[:LANES]
    turned = result[LANES:].T
    acts_ref[part, LANES:] = turned
    return result, turned


def head_columns(
    xbc_ref, taps_ref, log_ref, maps_ref, acts_ref, head_ref, state_ref, padded, heads
):
    rows, _ = xbc_ref.shape
    for head in heads:
        place = slice(head * LANES, (head + 1) * LANES)
        _, turned = some_columns(
            xbc_ref, taps_ref, acts_ref, head_ref, padded.at[head % 2], head * LANES
        )
        logs = log_ref[head : head + 1, :]
        tail = jnp.exp(logs[:, rows - 1 : rows] - logs[:, LANES:])
        decayed = (turned.astype(F32) * tail).astype(BF16)
        state_ref[place, :] = product(decayed, maps_ref[LANES:, :])


def load_kernel(
    xbc_hbm, taps_hbm, decay_hbm, xbc_ref, taps_ref, log_ref, edge_ref, acts_ref, head_ref,
    maps_ref, state_ref, decay_buf, padded, sems, early
):
    rows, width = xbc_ref.shape
    pieces = sems.shape[0] - 2
    maps_width = 2 * maps_ref.shape[1]
    inner = width - maps_width
    rest = (inner - early * LANES) // (pieces - 2)
    cuts = [0] + [early * LANES + piece * rest for piece in range(pieces - 1)]
    spans = [(inner, maps_width)] + [(x, y - x) for x, y in zip(cuts, cuts[1:])]
    copies = [
        pltpu.make_async_copy(decay_hbm, decay_buf, sems.at[pieces]),
        pltpu.make_async_copy(taps_hbm, taps_ref, sems.at[pieces + 1]),
    ]
    for piece, (start, size) in enumerate(spans):
        part = pl.ds(start, size)
        copies.append(
            pltpu.make_async_copy(xbc_hbm.at[:, part], xbc_ref.at[:, part], sems.at[piece])
        )
    for copy in copies[:4]:
        copy.start()
    for copy in copies[4:]:
        copy.start()
    copies[0].wait()
    log_ref[...] = running_sum(decay_buf[...])
    copies[1].wait()
    copies[2].wait()
    for slot, start in enumerate(range(width - LANES, inner - 1, -LANES)):
        result, _ = some_columns(
            xbc_ref, taps_ref, acts_ref, head_ref, padded.at[slot % 2], start
        )
    maps_ref[...] = result
    copies[3].wait()
    head_columns(
        xbc_ref, taps_ref, log_ref, maps_ref, acts_ref, head_ref, state_ref, padded, range(early)
    )
    for copy in copies[4:]:
        copy.wait()
    few = edge_ref.shape[0]
    tail = xbc_ref[rows - 2 * GROUP :, :].astype(F32)
    edge_ref[...] = tail[2 * GROUP - few :].astype(BF16)


def load(xbc, conv_weight, log_decay, early):
    rows, width = xbc.shape
    inner = log_decay.shape[0] * LANES
    state_size = (width - inner) // 2
    pieces = 3
    return pl.pallas_call(
        functools.partial(load_kernel, early=early),
        in_specs=[HBM_SPEC] * 3,
        out_specs=[VMEM_SPEC] * 8,
        out_shape=[
            pltpu.VMEM(xbc.shape, BF16),
            pltpu.VMEM(conv_weight.shape, F32),
            pltpu.VMEM(log_decay.shape, F32),
            pltpu.VMEM((conv_weight.shape[0] - 1, width), BF16),
            pltpu.VMEM((width, rows), BF16),
            pltpu.VMEM((LANES, width), BF16),
            pltpu.VMEM((rows, state_size), BF16),
            pltpu.VMEM((inner, state_size), F32),
        ],
        scratch_shapes=[
            pltpu.VMEM(log_decay.shape, F32),
            pltpu.VMEM((2, rows + GROUP, LANES), F32),
            pltpu.SemaphoreType.DMA((pieces + 2,)),
        ],
        compiler_params=params(),
        cost_estimate=small_cost(),
        name="load",
    )(*in_hbm(xbc, conv_weight, log_decay))


def front_kernel(
    xbc_ref, taps_ref, log_ref, maps_ref, acts_in, head_in, state_in, acts_ref, head_ref,
    state_ref, padded, early
):
    head_columns(
        xbc_ref, taps_ref, log_ref, maps_ref, acts_ref, head_ref, state_ref, padded,
        range(early, log_ref.shape[0]),
    )


def front(xbc, taps, log, maps, acts, head, state, early):
    rows, _ = xbc.shape
    operands = [xbc, taps, log, maps, acts, head, state]
    return pl.pallas_call(
        functools.partial(front_kernel, early=early),
        in_specs=[VMEM_SPEC] * len(operands),
        out_specs=[VMEM_SPEC] * 3,
        out_shape=[
            pltpu.VMEM(acts.shape, BF16),
            pltpu.VMEM(head.shape, BF16),
            pltpu.VMEM(state.shape, F32),
        ],
        input_output_aliases={4: 0, 5: 1, 6: 2},
        scratch_shapes=[pltpu.VMEM((2, rows + GROUP, LANES), F32)],
        compiler_params=params(),
        name="front",
    )(*in_vmem(*operands))


def edge_kernel(
    far_edge_ref, near_edge_ref, log_ref, taps_ref, xbc_ref, head_ref, *refs, shards
):
    acts_ref, maps_ref, state_ref, away_ref, home_ref, padded = refs[-6:]
    head_count, rows = log_ref.shape
    width = head_ref.shape[1]
    inner = head_count * LANES
    few = 2 * GROUP
    index = lax.axis_index("seq")

    def first_tile(start, slot):
        part = slice(start, start + LANES)
        near_edge = near_edge_ref[:, part].astype(F32)
        far_edge = far_edge_ref[:, part].astype(F32)
        edge = jnp.where(index % 2 == 1, near_edge, jnp.where(index == 0, 0.0, far_edge))
        values = xbc_ref[:few, part].astype(F32)
        result = activated(values, edge, taps_ref[:, part], padded.at[slot])
        block = jnp.concatenate([result, head_ref[few:, part]], axis=0)
        turned = block.T
        acts_ref[part, :LANES] = turned
        return block, turned

    first_tile(width - LANES, 0)
    maps, _ = first_tile(width - 2 * LANES, 1)
    maps_ref[:LANES, :] = maps
    totals = jnp.broadcast_to(log_ref[:, rows - 1 : rows], (head_count, LANES))
    write_spans(away_ref, inner // 2, totals)
    parity = index % 2
    for head in range(head_count):
        part = slice(head * LANES, (head + 1) * LANES)
        _, turned = first_tile(head * LANES, head % padded.shape[0])
        logs = log_ref[head : head + 1, :]
        tail = jnp.exp(logs[:, rows - 1 : rows] - logs[:, :LANES])
        decayed = (turned.astype(F32) * tail).astype(BF16)
        state = state_ref[part, :] + product(decayed, maps)
        state_ref[part, :] = state
    part = inner // shards
    for slot in range(shards // 2):
        place = slice(slot * part, (slot + 1) * part)
        kept = pl.multiple_of((2 * slot + parity) * part, part)
        given = pl.multiple_of((2 * slot + 1 - parity) * part, part)
        away_ref[place, :] = state_ref[pl.ds(given, part), :].astype(BF16)
        home_ref[place, :] = state_ref[pl.ds(kept, part), :].astype(BF16)


def edge_rows(far_edge, near_edge, log, taps, xbc, head, acts, maps, state, shards):
    head_count, _ = log.shape
    inner, state_size = state.shape
    operands = [far_edge, near_edge, log, taps, xbc, head, acts, maps, state]
    return pl.pallas_call(
        functools.partial(edge_kernel, shards=shards),
        in_specs=[VMEM_SPEC] * len(operands),
        out_specs=[VMEM_SPEC] * 5,
        out_shape=[
            pltpu.VMEM(acts.shape, BF16),
            pltpu.VMEM(maps.shape, BF16),
            pltpu.VMEM(state.shape, F32),
            pltpu.VMEM((inner // 2 + head_count, state_size), BF16),
            pltpu.VMEM((inner // 2, state_size), BF16),
        ],
        input_output_aliases={6: 0, 7: 1, 8: 2},
        scratch_shapes=[pltpu.VMEM((2, 3 * GROUP, LANES), F32)],
        compiler_params=params(),
        cost_estimate=small_cost(),
        name="edge",
    )(*in_vmem(*operands))


def pair_kernel(state_ref, log_ref, got_ref, own_ref, stats_ref, send_ref, rest_ref, shards):
    head_count, rows = log_ref.shape
    inner = state_ref.shape[0]
    index = lax.axis_index("seq")
    is_upper = index % 2 == 1
    mine = jnp.broadcast_to(log_ref[:, rows - 1 : rows], (head_count, LANES))
    theirs = read_spans(got_ref, inner // 2, head_count)
    stats_ref[0] = mine + theirs
    stats_ref[1] = jnp.where(is_upper, theirs, 0.0)
    write_spans(send_ref, inner // shards, mine + theirs)
    stats_ref[2] = jnp.exp(mine)
    stats_ref[3] = jnp.exp(theirs)
    shard = index % shards
    share = head_count // shards

    def joined(owner, local):
        head = owner * share + local
        at = pl.ds(pl.multiple_of(head * LANES, LANES), LANES)
        own = state_ref[at, :]
        start = pl.multiple_of((owner // 2 * share + local) * LANES, LANES)
        got = got_ref[pl.ds(start, LANES), :].astype(F32)
        late = jnp.where(is_upper, own, got)
        early = jnp.where(is_upper, got, own)
        late_row = jnp.where(is_upper, 2, 3)
        return early * stats_ref[late_row, pl.ds(head, 1), :] + late

    for local in range(share):
        place = slice(local * LANES, (local + 1) * LANES)
        send_ref[place, :] = joined(shard ^ 2, local).astype(BF16)
        kept = joined(shard, local)
        own_ref[place, :] = kept
        rest_ref[place, :] = kept.astype(BF16)


def pair(state, log, got, shards):
    head_count, _ = log.shape
    inner, state_size = state.shape
    part = inner // shards
    return pl.pallas_call(
        functools.partial(pair_kernel, shards=shards),
        in_specs=[VMEM_SPEC] * 3,
        out_specs=[VMEM_SPEC] * 4,
        out_shape=[
            pltpu.VMEM((part, state_size), F32),
            pltpu.VMEM((4, head_count, LANES), F32),
            pltpu.VMEM((part + head_count, state_size), BF16),
            pltpu.VMEM((part, state_size), BF16),
        ],
        compiler_params=params(),
        cost_estimate=small_cost(),
        name="pair",
    )(*in_vmem(state, log, got))


def join_kernel(own_ref, stats_ref, got_ref, _, *refs, bit, shards, gathered):
    sources = refs[:gathered]
    if gathered:
        next_stats_ref, send_ref, across_ref = refs[gathered:]
    else:
        next_stats_ref, send_ref, next_ref = refs
    part = own_ref.shape[0]
    head_count = stats_ref.shape[1]
    share = head_count // shards
    index = lax.axis_index("seq")
    is_upper = (index >> bit) % 2 == 1
    mine = stats_ref[0]
    theirs = read_spans(got_ref, part, head_count)
    next_stats_ref[0] = mine + theirs
    next_stats_ref[1] = stats_ref[1] + jnp.where(is_upper, theirs, 0.0)
    next_stats_ref[2] = jnp.exp(jnp.where(is_upper, mine, theirs))
    next_stats_ref[3] = jnp.zeros_like(mine)
    if not gathered:
        write_spans(send_ref, part, mine + theirs)
    for local in range(share):
        place = slice(local * LANES, (local + 1) * LANES)
        head = (index % shards) * share + local
        own = own_ref[place, :]
        got = got_ref[place, :].astype(F32)
        late = jnp.where(is_upper, own, got)
        early = jnp.where(is_upper, got, own)
        total = early * next_stats_ref[2, pl.ds(head, 1), :] + late
        send_ref[place, :] = total.astype(BF16)
        if not gathered:
            next_ref[place, :] = total
    for slot in range(gathered):
        across_ref[slot * part : (slot + 1) * part, :] = sources[slot][:part, :]


def join(own, stats, got, after, bit, shards, sources):
    operands = [own, stats, got, after, *sources]
    message = own.shape if sources else got.shape
    out_shape = [pltpu.VMEM(stats.shape, F32), pltpu.VMEM(message, BF16)]
    if sources:
        out_shape.append(pltpu.VMEM((len(sources) * own.shape[0], own.shape[1]), BF16))
    else:
        out_shape.append(pltpu.VMEM(own.shape, F32))
    return pl.pallas_call(
        functools.partial(join_kernel, bit=bit, shards=shards, gathered=len(sources)),
        in_specs=[VMEM_SPEC] * len(operands),
        out_specs=[VMEM_SPEC] * 3,
        out_shape=out_shape,
        compiler_params=params(),
        cost_estimate=small_cost(),
        name="join",
    )(*in_vmem(*operands))


def bit_length(numbers, limit):
    counted = jnp.zeros(numbers.shape, jnp.int32)
    for power in range(limit):
        counted = counted + (numbers >= 1 << power).astype(jnp.int32)
    return counted


def near_kernel(*refs, first, wide, heads, shards):
    if first:
        acts_ref, maps_ref, log_ref, gains_ref, node_ref, _, gain_ref = refs[:7]
        near_ref, scores, tails, columns_ref, turned, weights = refs[7:]
    else:
        acts_ref, maps_ref, log_ref, gains_ref, node_ref, _, scores, tails, _ = refs[:9]
        near_ref, turned, weights = refs[9:]
    head_count, rows = log_ref.shape
    inner = head_count * LANES
    state_size = maps_ref.shape[1]
    tiles = rows // LANES
    tile_bits = tiles.bit_length() - 1
    groups = LANES // GROUP
    low_bits = GROUP.bit_length() - 1
    tile_levels = LANES.bit_length() - 1
    queries = acts_ref[inner + state_size :, :]
    middle = LANES // 2 - 1
    if first:
        for start in range(0, rows, wide):
            upto = start + wide
            scores[:upto, start:upto] = product(maps_ref[:upto, :], queries[:, start:upto])
        turned[head_count:, :] = jnp.zeros((LANES - head_count, rows), F32)
        turned[:head_count, :LANES] = gain_ref[...]
        columns_ref[...] = turned[:, :LANES].T
        turned[:head_count, :] = log_ref[...]
        columns = [turned[:, tile * LANES : (tile + 1) * LANES].T for tile in range(tiles)]
        for tile in range(tiles):
            place = slice(tile * LANES, (tile + 1) * LANES)
            tails[0, place, :] = jnp.exp(columns[tile][middle : middle + 1] - columns[tile])
            for bit in range(tile_bits):
                if tile >> bit & 1 == 0:
                    edge = ((tile >> bit) + 1 << bit) - 1
                    tails[1 + bit, place, :] = jnp.exp(columns[edge][LANES - 1 :] - columns[tile])
    for late in range(tiles):
        for early in range(tiles):
            if early > late:
                weights[
                    :, early * LANES : (early + 1) * LANES, late * LANES : (late + 1) * LANES
                ] = jnp.zeros((weights.shape[0], LANES, LANES), BF16)
    lane = lax.broadcasted_iota(jnp.int32, (GROUP, LANES), 1)
    row = lax.broadcasted_iota(jnp.int32, (GROUP, LANES), 0)
    inside = bit_length((lane % GROUP) ^ row, low_bits)
    ahead = row <= lane % GROUP
    lane_group = lax.broadcasted_iota(jnp.int32, (groups, LANES), 1) // GROUP
    row_group = lax.broadcasted_iota(jnp.int32, (groups, LANES), 0)
    between = bit_length(lane_group ^ row_group, groups.bit_length() - 1)
    before = row_group < lane_group
    same = (
        lax.broadcasted_iota(jnp.int32, (groups, 1, LANES), 2) // GROUP
        == lax.broadcasted_iota(jnp.int32, (groups, 1, LANES), 0)
    )
    index = lax.axis_index("seq")
    is_upper = index % 2 == 1
    share = head_count // shards

    def spread(kind, place, head):
        chosen = jnp.full((LANES, LANES), head, jnp.int32)
        return jnp.take_along_axis(
            tails[kind, place, :], chosen, axis=1, mode="promise_in_bounds"
        )

    def one_head(head, slot):
        logs = log_ref[pl.ds(head, 1), :]
        gain_rows = [
            gains_ref[pl.ds(level * head_count + head, 1), :]
            for level in range(tile_levels + tile_bits + 2)
        ]
        for late in range(tiles):
            span = slice(late * LANES, (late + 1) * LANES)
            own = logs[:, span]
            start = late * LANES + middle
            grown = jnp.exp(own - logs[:, start : start + 1])
            corner = jnp.zeros((GROUP, LANES), F32)
            for level in range(low_bits + 1):
                gain = gain_rows[level][:, span] * grown
                corner = jnp.where(ahead & (inside == level), gain, corner)
            rest = jnp.zeros((groups, LANES), F32)
            for level in range(low_bits + 1, tile_levels + 1):
                gain = gain_rows[level][:, span] * grown
                rest = jnp.where(before & (between == level - low_bits), gain, rest)
            chosen = jnp.where(same, corner[None], rest[:, None, :]).reshape(LANES, LANES)
            weight = chosen * spread(0, span, head) * scores[span, span]
            weights[slot, span, span] = weight.astype(BF16)
            for bit in range(tile_bits):
                if late >> bit & 1 == 0:
                    continue
                edge = (late >> bit << bit) * LANES - 1
                level = tile_levels + 1 + bit
                factor = gain_rows[level][:, span] * jnp.exp(
                    own - logs[:, edge : edge + 1]
                )
                for early in range(((late >> bit) - 1) << bit, (late >> bit) << bit):
                    place = slice(early * LANES, (early + 1) * LANES)
                    weight = spread(1 + bit, place, head) * factor * scores[place, span]
                    weights[slot, place, span] = weight.astype(BF16)
        at = pl.ds(pl.multiple_of(head * LANES, LANES), LANES)
        level = tile_levels + tile_bits + 1
        factor = gain_rows[level] * jnp.exp(jnp.where(is_upper, logs, -1e30))
        owner, local = head // share, head % share
        start = jnp.where(owner % 2 == index % 2, 0, inner // 2)
        start = start + (owner // 2 * share + local) * LANES
        node = node_ref[pl.ds(pl.multiple_of(start, LANES), LANES), :]
        far = product(node, queries) * factor
        for start in range(0, rows, wide):
            upto = start + wide
            near_ref[at, start:upto] = far[:, start:upto] + product(
                acts_ref[at, :upto], weights[slot, :upto, start:upto]
            )

    def some_heads(step, carry):
        for slot in range(weights.shape[0]):
            one_head(step * weights.shape[0] + slot, slot)
        return carry

    lax.fori_loop(heads[0] // weights.shape[0], heads[1] // weights.shape[0], some_heads, 0)


def near(acts, maps, log, gains, node, after, gain, earlier, heads, shards):
    head_count, rows = log.shape
    wide = min(rows, 2 * LANES)
    tile_bits = (rows // LANES).bit_length() - 1
    first = earlier is None
    out_shape = [pltpu.VMEM((head_count * LANES, rows), F32)]
    operands = [acts, maps, log, gains, node, after]
    aliases = {}
    if first:
        out_shape.append(pltpu.VMEM((rows, rows), F32))
        out_shape.append(pltpu.VMEM((1 + tile_bits, rows, LANES), F32))
        out_shape.append(pltpu.VMEM((LANES, LANES), F32))
        operands.append(gain.reshape(head_count, LANES))
    else:
        near_term, scores, tails, _ = earlier
        operands += [scores, tails, near_term]
        aliases = {len(operands) - 1: 0}
    made = pl.pallas_call(
        functools.partial(near_kernel, first=first, wide=wide, heads=heads, shards=shards),
        in_specs=[VMEM_SPEC] * len(operands),
        out_specs=[VMEM_SPEC] * len(out_shape),
        out_shape=out_shape,
        input_output_aliases=aliases,
        scratch_shapes=[
            pltpu.VMEM((LANES, rows), F32),
            pltpu.VMEM((2, rows, rows), BF16),
        ],
        compiler_params=params(),
        cost_estimate=pl.CostEstimate(
            flops=2 * head_count * rows * rows * LANES, bytes_accessed=10 << 20, transcendentals=0
        ),
        name="near",
    )(*in_vmem(*operands))
    return made if first else [made[0], *earlier[1:]]


def far_product(node_ref, first_row, count, queries):
    return product(node_ref[first_row : first_row + count, :], queries)


def far_factor(gains_ref, log_ref, stats_ref, head, level, base):
    is_upper = (lax.axis_index("seq") >> level) % 2 == 1
    shift = stats_ref[1, pl.ds(head, 1), :][:, :1]
    exponent = jnp.where(is_upper, log_ref[pl.ds(head, 1), :] + shift, -1e30)
    row = (base + level) * log_ref.shape[0] + head
    return gains_ref[pl.ds(row, 1), :] * jnp.exp(exponent)


def middle_kernel(*refs, places, relatives, levels, shards):
    count = len(places)
    acts_ref, log_ref, gains_ref = refs[:3]
    stats = refs[3 : 3 + count]
    sources = refs[3 + count : -2]
    total_ref = refs[-1]
    head_count, _ = log_ref.shape
    part = head_count // shards * LANES
    inner = head_count * LANES
    state_size = acts_ref.shape[0] - inner >> 1
    shard = lax.axis_index("seq") % shards
    base = gains_ref.shape[0] // head_count - levels
    queries = acts_ref[inner + state_size :, :]
    for relative in relatives:
        terms = []
        for slot in range(count):
            source, start = places[slot][relative]
            terms.append(far_product(sources[source], start, part, queries))
        for local in range(head_count // shards):
            head = (relative ^ shard) * (head_count // shards) + local
            at = pl.ds(pl.multiple_of(head * LANES, LANES), LANES)
            total = total_ref[at, :]
            for slot in range(count):
                factor = far_factor(gains_ref, log_ref, stats[slot], head, slot + 1, base)
                total = total + terms[slot][local * LANES : (local + 1) * LANES] * factor
            total_ref[at, :] = total


def middle(
    near_term, acts, log, gains, stats, sources, places, relatives, levels, shards
):
    operands = [acts, log, gains, *stats, *sources, near_term]
    return pl.pallas_call(
        functools.partial(
            middle_kernel, places=places, relatives=relatives, levels=levels, shards=shards
        ),
        in_specs=[VMEM_SPEC] * len(operands),
        out_specs=VMEM_SPEC,
        out_shape=pltpu.VMEM(near_term.shape, F32),
        input_output_aliases={len(operands) - 1: 0},
        compiler_params=params(),
        cost_estimate=small_cost(),
        name="middle",
    )(*in_vmem(*operands))


def last_kernel(
    total_ref, acts_ref, log_ref, gains_ref, columns_ref, stats_ref, node_ref, *refs,
    level, relatives, done, shards, base
):
    head_count, rows = log_ref.shape
    share = head_count // shards
    part = share * LANES
    inner = head_count * LANES
    state_size = acts_ref.shape[0] - inner >> 1
    shard = lax.axis_index("seq") % shards
    queries = acts_ref[inner + state_size :, :]
    copies = []
    if done:
        out_hbm, mixed_ref, sems = refs[-3:]

    def send(source_ref, place, relative, first, count):
        start = pl.multiple_of((relative ^ shard) * part, part)
        copies.append(
            pltpu.make_async_copy(
                source_ref.at[place, pl.ds(first, count), :],
                out_hbm.at[pl.ds(first, count), pl.ds(start, part)],
                sems.at[len(copies)],
            )
        )
        copies[-1].start()

    if done:
        for relative, source_ref in zip(done, refs):
            send(source_ref, 0, relative, 0, rows)
    else:
        (mixed_ref,) = refs
    for place, relative in enumerate(relatives):
        term = far_product(node_ref, place * part, part, queries)
        heads = [(relative ^ shard) * share + local for local in range(share)]
        places = [pl.ds(pl.multiple_of(head * LANES, LANES), LANES) for head in heads]
        factors = [
            far_factor(gains_ref, log_ref, stats_ref, head, level, base) for head in heads
        ]
        gain_columns = [
            jnp.take_along_axis(
                columns_ref[...],
                jnp.full((LANES, LANES), head, jnp.int32),
                axis=1,
                mode="promise_in_bounds",
            )
            for head in heads
        ]
        for first in range(0, rows, LANES):
            span = slice(first, first + LANES)
            for local in range(share):
                own = term[local * LANES : (local + 1) * LANES, span]
                total = total_ref[places[local], span] + own * factors[local][:, span]
                mean = jnp.mean(total * total, axis=0, keepdims=True)
                scale = lax.rsqrt(mean + 1e-05)
                mixed = (total * scale * gain_columns[local]).astype(BF16).T
                mixed_ref[place, span, local * LANES : (local + 1) * LANES] = mixed
            if done:
                send(mixed_ref, place, relative, first, LANES)
    for copy in copies:
        copy.wait()


def last(total, acts, log, gains, columns, stats, node, level, levels, relatives, shards, done):
    head_count, rows = log.shape
    share = head_count // shards
    operands = [total, acts, log, gains, columns, stats, node, *done.values()]
    mixed = pltpu.VMEM((len(relatives), rows, share * LANES), BF16)
    copies = len(done) + len(relatives) * rows // LANES
    whole = jax.ShapeDtypeStruct((rows, head_count * LANES), BF16)
    return pl.pallas_call(
        functools.partial(
            last_kernel, level=level, relatives=relatives, done=tuple(done), shards=shards,
            base=gains.shape[0] // head_count - levels,
        ),
        in_specs=[VMEM_SPEC] * len(operands),
        out_specs=HBM_SPEC if done else VMEM_SPEC,
        out_shape=whole if done else mixed,
        scratch_shapes=[mixed, pltpu.SemaphoreType.DMA((copies,))] if done else [],
        compiler_params=params(),
        cost_estimate=small_cost(),
        name="last",
    )(*in_vmem(*operands))


def moved(value, apart):
    return lax.ppermute(value, "seq", [(i, i ^ apart) for i in range(lax.axis_size("seq"))])


def onward(devices):
    route = {index: index + 1 for index in range(devices)}
    planes = devices // 4
    target = 0
    for plane in range(1, planes - 1):
        route[4 * plane + 2] = target
        target = 4 * plane + 3
    route[devices - 1] = target
    return list(route.items())


def on_device(xbc, conv_weight, log_decay, level_weights, gain):
    rows = xbc.shape[0]
    head_count = log_decay.shape[0]
    devices = lax.axis_size("seq")
    levels = devices.bit_length() - 1
    shards = 4
    part = head_count * LANES // shards
    gains = level_weights.transpose(1, 0, 2).reshape(-1, rows)
    beyond = onward(devices)
    early = head_count // 4
    values, taps, log, edge, acts, head, maps, state = load(xbc, conv_weight, log_decay, early)
    far_edge = lax.ppermute(edge, "seq", beyond)
    near_edge = moved(edge, 1)
    acts, head, state = front(values, taps, log, maps, acts, head, state, early)
    acts, maps, state, away, home = edge_rows(
        far_edge, near_edge, log, taps, values, head, acts, maps, state, shards
    )
    joined = moved(away, 1)
    first_node = jnp.concatenate([joined[: home.shape[0]], moved(home, 1)])
    own, stats, send, rest = pair(state, log, joined, shards)
    near_made = None
    all_stats = [stats]
    got = []
    for bit in range(1, levels - 1):
        got.append(moved(send, 1 << bit))
        if bit <= 2:
            half = head_count // 2
            heads = (half * (bit - 1), half * bit)
            near_made = near(
                acts, maps, log, gains, first_node, stats, gain, near_made, heads, shards
            )
        sources = [rest, *got[1:]] if bit == levels - 2 else []
        stats, send, own = join(own, stats, got[-1], near_made[0], bit, shards, sources)
        all_stats.append(stats)
    top = levels - 1

    node = moved(send, 1 << top)
    count = len(got)
    across = moved(own, 2)
    shared = (acts, log, gains, all_stats[:count])
    direct = [{0: (slot, 0)} for slot in range(count)]
    crossed = [{2: (0, slot * part)} for slot in range(count)]
    relayed = [{1: (slot, 0), 3: (count + slot, 0)} for slot in range(count)]
    total = middle(near_made[0], *shared, got, direct, (0,), levels, shards)
    node, total = lax.optimization_barrier((node, total))
    common = (acts, log, gains, near_made[3], all_stats[-1])
    node_across = moved(node, 2)
    own_done = last(total, *common, node, top, levels, (0,), shards, {})
    shares = [kept[:part] for kept in got]
    shares += [across[slot * part : (slot + 1) * part] for slot in range(count)]
    own_done, shares, total = lax.optimization_barrier((own_done, shares, total))
    beside = [moved(kept, 1) for kept in shares]
    total = middle(total, *shared, [across], crossed, (2,), levels, shards)
    node_across, beside, total = lax.optimization_barrier((node_across, beside, total))
    node_beside = moved(jnp.concatenate([node, node_across]), 1)
    total = middle(total, *shared, beside, relayed, (1, 3), levels, shards)
    across_done = last(total, *common, node_across, top, levels, (2,), shards, {})
    done = {0: own_done, 2: across_done}
    return last(total, *common, node_beside, top, levels, (1, 3), shards, done)


def solution(mesh):
    in_specs = (
        P(("groups", "seq"), None),
        P(),
        P(None, ("groups", "seq")),
        P(None, None, ("groups", "seq")),
        P(),
    )
    out_specs = P(("groups", "seq"), None)
    return jax.shard_map(
        on_device, mesh=mesh, in_specs=in_specs, out_specs=out_specs, check_vma=False
    )
```

```python
import functools

import jax
import jax.numpy as jnp
from jax import lax
from jax.experimental import pallas as pl
from jax.experimental.pallas import tpu as pltpu
from jax.sharding import PartitionSpec as P

F32 = jnp.float32
BF16 = jnp.bfloat16
LANES = 128
GROUP = 8
PARTS = 3
VMEM_LIMIT = 24 << 20
HBM_SPEC = pl.BlockSpec(memory_space=pltpu.HBM)
VMEM_SPEC = pl.BlockSpec(memory_space=pltpu.VMEM)


def in_vmem(*arrays):
    return [pltpu.with_memory_space_constraint(array, pltpu.VMEM) for array in arrays]


def in_hbm(*arrays):
    return [pltpu.with_memory_space_constraint(array, pltpu.HBM) for array in arrays]


def params():
    return pltpu.CompilerParams(vmem_limit_bytes=VMEM_LIMIT)


def small_cost():
    return pl.CostEstimate(flops=1024, bytes_accessed=1024, transcendentals=0)


def product(left, right):
    return jnp.dot(left, right, preferred_element_type=F32)


def write_spans(message_ref, first_row, spans):
    head_count = spans.shape[0]
    for part in range(PARTS):
        rounded = spans.astype(BF16)
        start = first_row + part * head_count
        message_ref[start : start + head_count, :] = rounded
        spans = spans - rounded.astype(F32)


def read_spans(message_ref, first_row, head_count):
    total = None
    for part in range(PARTS):
        start = first_row + part * head_count
        piece = message_ref[start : start + head_count, :].astype(F32)
        total = piece if total is None else total + piece
    return total


def running_sum(logs):
    head_count, rows = logs.shape
    tiles = rows // LANES
    row = lax.broadcasted_iota(jnp.int32, (LANES, LANES), 0)
    column = lax.broadcasted_iota(jnp.int32, (LANES, LANES), 1)
    upto = (row <= column).astype(BF16)
    left = jnp.concatenate(
        [logs[:, tile * LANES : (tile + 1) * LANES] for tile in range(tiles)], axis=0
    )
    pieces = []
    for _ in range(3):
        pieces.append(left.astype(BF16))
        left = left - pieces[-1].astype(F32)
    size = head_count * tiles
    added = product(jnp.concatenate(pieces, axis=0), upto)
    within = added[2 * size :] + added[size : 2 * size] + added[:size]
    sums = []
    offset = jnp.zeros((head_count, 1), F32)
    for tile in range(tiles):
        part = within[tile * head_count : (tile + 1) * head_count]
        sums.append(part + offset)
        offset = offset + part[:, LANES - 1 :]
    return jnp.concatenate(sums, axis=1)


def activated(values, edge, weights, padded):
    rows = values.shape[0]
    taps = weights.shape[0]
    padded[GROUP : GROUP + rows, :] = values
    if edge is not None:
        padded[GROUP - taps + 1 : GROUP, :] = edge
    total = None
    for tap in range(taps):
        first = GROUP - taps + 1 + tap
        shifted = values if tap == taps - 1 else padded[first : first + rows, :]
        term = shifted * weights[tap : tap + 1]
        total = term if total is None else total + term
    return (total * jax.nn.sigmoid(total)).astype(BF16)


def some_columns(xbc_ref, taps_ref, acts_ref, head_ref, padded, start):
    part = slice(start, start + LANES)
    values = xbc_ref[:, part].astype(F32)
    result = activated(values, None, taps_ref[:, part], padded)
    head_ref[:, part] = result[:LANES]
    turned = result[LANES:].T
    acts_ref[part, LANES:] = turned
    return result, turned


def head_columns(
    xbc_ref, taps_ref, log_ref, maps_ref, acts_ref, head_ref, state_ref, padded, heads
):
    rows, _ = xbc_ref.shape
    for head in heads:
        place = slice(head * LANES, (head + 1) * LANES)
        _, turned = some_columns(
            xbc_ref, taps_ref, acts_ref, head_ref, padded.at[head % 2], head * LANES
        )
        logs = log_ref[head : head + 1, :]
        tail = jnp.exp(logs[:, rows - 1 : rows] - logs[:, LANES:])
        decayed = (turned.astype(F32) * tail).astype(BF16)
        state_ref[place, :] = product(decayed, maps_ref[LANES:, :])


def load_kernel(
    xbc_hbm, taps_hbm, decay_hbm, xbc_ref, taps_ref, log_ref, edge_ref, acts_ref, head_ref,
    maps_ref, state_ref, decay_buf, padded, sems, early
):
    rows, width = xbc_ref.shape
    pieces = sems.shape[0] - 2
    maps_width = 2 * maps_ref.shape[1]
    inner = width - maps_width
    rest = (inner - early * LANES) // (pieces - 2)
    cuts = [0] + [early * LANES + piece * rest for piece in range(pieces - 1)]
    spans = [(inner, maps_width)] + [(x, y - x) for x, y in zip(cuts, cuts[1:])]
    copies = [
        pltpu.make_async_copy(decay_hbm, decay_buf, sems.at[pieces]),
        pltpu.make_async_copy(taps_hbm, taps_ref, sems.at[pieces + 1]),
    ]
    for piece, (start, size) in enumerate(spans):
        part = pl.ds(start, size)
        copies.append(
            pltpu.make_async_copy(xbc_hbm.at[:, part], xbc_ref.at[:, part], sems.at[piece])
        )
    for copy in copies[:4]:
        copy.start()
    for copy in copies[4:]:
        copy.start()
    copies[0].wait()
    log_ref[...] = running_sum(decay_buf[...])
    copies[1].wait()
    copies[2].wait()
    for slot, start in enumerate(range(width - LANES, inner - 1, -LANES)):
        result, _ = some_columns(
            xbc_ref, taps_ref, acts_ref, head_ref, padded.at[slot % 2], start
        )
    maps_ref[...] = result
    copies[3].wait()
    head_columns(
        xbc_ref, taps_ref, log_ref, maps_ref, acts_ref, head_ref, state_ref, padded, range(early)
    )
    for copy in copies[4:]:
        copy.wait()
    few = edge_ref.shape[0]
    tail = xbc_ref[rows - 2 * GROUP :, :].astype(F32)
    edge_ref[...] = tail[2 * GROUP - few :].astype(BF16)


def load(xbc, conv_weight, log_decay, early):
    rows, width = xbc.shape
    inner = log_decay.shape[0] * LANES
    state_size = (width - inner) // 2
    pieces = 3
    return pl.pallas_call(
        functools.partial(load_kernel, early=early),
        in_specs=[HBM_SPEC] * 3,
        out_specs=[VMEM_SPEC] * 8,
        out_shape=[
            pltpu.VMEM(xbc.shape, BF16),
            pltpu.VMEM(conv_weight.shape, F32),
            pltpu.VMEM(log_decay.shape, F32),
            pltpu.VMEM((conv_weight.shape[0] - 1, width), BF16),
            pltpu.VMEM((width, rows), BF16),
            pltpu.VMEM((LANES, width), BF16),
            pltpu.VMEM((rows, state_size), BF16),
            pltpu.VMEM((inner, state_size), F32),
        ],
        scratch_shapes=[
            pltpu.VMEM(log_decay.shape, F32),
            pltpu.VMEM((2, rows + GROUP, LANES), F32),
            pltpu.SemaphoreType.DMA((pieces + 2,)),
        ],
        compiler_params=params(),
        cost_estimate=small_cost(),
        name="load",
    )(*in_hbm(xbc, conv_weight, log_decay))


def front_kernel(
    xbc_ref, taps_ref, log_ref, maps_ref, acts_in, head_in, state_in, acts_ref, head_ref,
    state_ref, padded, early
):
    head_columns(
        xbc_ref, taps_ref, log_ref, maps_ref, acts_ref, head_ref, state_ref, padded,
        range(early, log_ref.shape[0]),
    )


def front(xbc, taps, log, maps, acts, head, state, early):
    rows, _ = xbc.shape
    operands = [xbc, taps, log, maps, acts, head, state]
    return pl.pallas_call(
        functools.partial(front_kernel, early=early),
        in_specs=[VMEM_SPEC] * len(operands),
        out_specs=[VMEM_SPEC] * 3,
        out_shape=[
            pltpu.VMEM(acts.shape, BF16),
            pltpu.VMEM(head.shape, BF16),
            pltpu.VMEM(state.shape, F32),
        ],
        input_output_aliases={4: 0, 5: 1, 6: 2},
        scratch_shapes=[pltpu.VMEM((2, rows + GROUP, LANES), F32)],
        compiler_params=params(),
        name="front",
    )(*in_vmem(*operands))


def edge_kernel(
    far_edge_ref, near_edge_ref, log_ref, taps_ref, xbc_ref, head_ref, *refs, shards
):
    acts_ref, maps_ref, state_ref, away_ref, home_ref, padded = refs[-6:]
    head_count, rows = log_ref.shape
    width = head_ref.shape[1]
    inner = head_count * LANES
    few = 2 * GROUP
    index = lax.axis_index("seq")

    def first_tile(start, slot):
        part = slice(start, start + LANES)
        near_edge = near_edge_ref[:, part].astype(F32)
        far_edge = far_edge_ref[:, part].astype(F32)
        edge = jnp.where(index % 2 == 1, near_edge, jnp.where(index == 0, 0.0, far_edge))
        values = xbc_ref[:few, part].astype(F32)
        result = activated(values, edge, taps_ref[:, part], padded.at[slot])
        block = jnp.concatenate([result, head_ref[few:, part]], axis=0)
        turned = block.T
        acts_ref[part, :LANES] = turned
        return block, turned

    first_tile(width - LANES, 0)
    maps, _ = first_tile(width - 2 * LANES, 1)
    maps_ref[:LANES, :] = maps
    totals = jnp.broadcast_to(log_ref[:, rows - 1 : rows], (head_count, LANES))
    write_spans(away_ref, inner // 2, totals)
    parity = index % 2
    for head in range(head_count):
        part = slice(head * LANES, (head + 1) * LANES)
        _, turned = first_tile(head * LANES, head % padded.shape[0])
        logs = log_ref[head : head + 1, :]
        tail = jnp.exp(logs[:, rows - 1 : rows] - logs[:, :LANES])
        decayed = (turned.astype(F32) * tail).astype(BF16)
        state = state_ref[part, :] + product(decayed, maps)
        state_ref[part, :] = state
    part = inner // shards
    for slot in range(shards // 2):
        place = slice(slot * part, (slot + 1) * part)
        kept = pl.multiple_of((2 * slot + parity) * part, part)
        given = pl.multiple_of((2 * slot + 1 - parity) * part, part)
        away_ref[place, :] = state_ref[pl.ds(given, part), :].astype(BF16)
        home_ref[place, :] = state_ref[pl.ds(kept, part), :].astype(BF16)


def edge_rows(far_edge, near_edge, log, taps, xbc, head, acts, maps, state, shards):
    head_count, _ = log.shape
    inner, state_size = state.shape
    operands = [far_edge, near_edge, log, taps, xbc, head, acts, maps, state]
    return pl.pallas_call(
        functools.partial(edge_kernel, shards=shards),
        in_specs=[VMEM_SPEC] * len(operands),
        out_specs=[VMEM_SPEC] * 5,
        out_shape=[
            pltpu.VMEM(acts.shape, BF16),
            pltpu.VMEM(maps.shape, BF16),
            pltpu.VMEM(state.shape, F32),
            pltpu.VMEM((inner // 2 + PARTS * head_count, state_size), BF16),
            pltpu.VMEM((inner // 2, state_size), BF16),
        ],
        input_output_aliases={6: 0, 7: 1, 8: 2},
        scratch_shapes=[pltpu.VMEM((2, 3 * GROUP, LANES), F32)],
        compiler_params=params(),
        cost_estimate=small_cost(),
        name="edge",
    )(*in_vmem(*operands))


def pair_kernel(state_ref, log_ref, got_ref, own_ref, stats_ref, send_ref, rest_ref, shards):
    head_count, rows = log_ref.shape
    inner = state_ref.shape[0]
    index = lax.axis_index("seq")
    is_upper = index % 2 == 1
    mine = jnp.broadcast_to(log_ref[:, rows - 1 : rows], (head_count, LANES))
    theirs = read_spans(got_ref, inner // 2, head_count)
    stats_ref[0] = mine + theirs
    stats_ref[1] = jnp.where(is_upper, theirs, 0.0)
    write_spans(send_ref, inner // shards, mine + theirs)
    stats_ref[2] = jnp.exp(mine)
    stats_ref[3] = jnp.exp(theirs)
    shard = index % shards
    share = head_count // shards

    def joined(owner, local):
        head = owner * share + local
        at = pl.ds(pl.multiple_of(head * LANES, LANES), LANES)
        own = state_ref[at, :]
        start = pl.multiple_of((owner // 2 * share + local) * LANES, LANES)
        got = got_ref[pl.ds(start, LANES), :].astype(F32)
        late = jnp.where(is_upper, own, got)
        early = jnp.where(is_upper, got, own)
        late_row = jnp.where(is_upper, 2, 3)
        return early * stats_ref[late_row, pl.ds(head, 1), :] + late

    for local in range(share):
        place = slice(local * LANES, (local + 1) * LANES)
        send_ref[place, :] = joined(shard ^ 2, local).astype(BF16)
        kept = joined(shard, local)
        own_ref[place, :] = kept
        rest_ref[place, :] = kept.astype(BF16)


def pair(state, log, got, shards):
    head_count, _ = log.shape
    inner, state_size = state.shape
    part = inner // shards
    return pl.pallas_call(
        functools.partial(pair_kernel, shards=shards),
        in_specs=[VMEM_SPEC] * 3,
        out_specs=[VMEM_SPEC] * 4,
        out_shape=[
            pltpu.VMEM((part, state_size), F32),
            pltpu.VMEM((4, head_count, LANES), F32),
            pltpu.VMEM((part + PARTS * head_count, state_size), BF16),
            pltpu.VMEM((part, state_size), BF16),
        ],
        compiler_params=params(),
        cost_estimate=small_cost(),
        name="pair",
    )(*in_vmem(state, log, got))


def join_kernel(own_ref, stats_ref, got_ref, _, *refs, bit, shards, gathered):
    sources = refs[:gathered]
    if gathered:
        next_stats_ref, send_ref, across_ref = refs[gathered:]
    else:
        next_stats_ref, send_ref, next_ref = refs
    part = own_ref.shape[0]
    head_count = stats_ref.shape[1]
    share = head_count // shards
    index = lax.axis_index("seq")
    is_upper = (index >> bit) % 2 == 1
    mine = stats_ref[0]
    theirs = read_spans(got_ref, part, head_count)
    next_stats_ref[0] = mine + theirs
    next_stats_ref[1] = stats_ref[1] + jnp.where(is_upper, theirs, 0.0)
    next_stats_ref[2] = jnp.exp(jnp.where(is_upper, mine, theirs))
    next_stats_ref[3] = jnp.zeros_like(mine)
    if not gathered:
        write_spans(send_ref, part, mine + theirs)
    for local in range(share):
        place = slice(local * LANES, (local + 1) * LANES)
        head = (index % shards) * share + local
        own = own_ref[place, :]
        got = got_ref[place, :].astype(F32)
        late = jnp.where(is_upper, own, got)
        early = jnp.where(is_upper, got, own)
        total = early * next_stats_ref[2, pl.ds(head, 1), :] + late
        send_ref[place, :] = total.astype(BF16)
        if not gathered:
            next_ref[place, :] = total
    for slot in range(gathered):
        across_ref[slot * part : (slot + 1) * part, :] = sources[slot][:part, :]


def join(own, stats, got, after, bit, shards, sources):
    operands = [own, stats, got, after, *sources]
    message = own.shape if sources else got.shape
    out_shape = [pltpu.VMEM(stats.shape, F32), pltpu.VMEM(message, BF16)]
    if sources:
        out_shape.append(pltpu.VMEM((len(sources) * own.shape[0], own.shape[1]), BF16))
    else:
        out_shape.append(pltpu.VMEM(own.shape, F32))
    return pl.pallas_call(
        functools.partial(join_kernel, bit=bit, shards=shards, gathered=len(sources)),
        in_specs=[VMEM_SPEC] * len(operands),
        out_specs=[VMEM_SPEC] * 3,
        out_shape=out_shape,
        compiler_params=params(),
        cost_estimate=small_cost(),
        name="join",
    )(*in_vmem(*operands))


def bit_length(numbers, limit):
    counted = jnp.zeros(numbers.shape, jnp.int32)
    for power in range(limit):
        counted = counted + (numbers >= 1 << power).astype(jnp.int32)
    return counted


def near_kernel(*refs, first, wide, heads, shards):
    if first:
        acts_ref, maps_ref, log_ref, gains_ref, node_ref, _, gain_ref = refs[:7]
        near_ref, scores, tails, columns_ref, turned, weights = refs[7:]
    else:
        acts_ref, maps_ref, log_ref, gains_ref, node_ref, _, scores, tails, _ = refs[:9]
        near_ref, turned, weights = refs[9:]
    head_count, rows = log_ref.shape
    inner = head_count * LANES
    state_size = maps_ref.shape[1]
    tiles = rows // LANES
    tile_bits = tiles.bit_length() - 1
    groups = LANES // GROUP
    low_bits = GROUP.bit_length() - 1
    tile_levels = LANES.bit_length() - 1
    queries = acts_ref[inner + state_size :, :]
    middle = LANES // 2 - 1
    if first:
        for start in range(0, rows, wide):
            upto = start + wide
            scores[:upto, start:upto] = product(maps_ref[:upto, :], queries[:, start:upto])
        turned[head_count:, :] = jnp.zeros((LANES - head_count, rows), F32)
        turned[:head_count, :LANES] = gain_ref[...]
        columns_ref[...] = turned[:, :LANES].T
        turned[:head_count, :] = log_ref[...]
        columns = [turned[:, tile * LANES : (tile + 1) * LANES].T for tile in range(tiles)]
        for tile in range(tiles):
            place = slice(tile * LANES, (tile + 1) * LANES)
            tails[0, place, :] = jnp.exp(columns[tile][middle : middle + 1] - columns[tile])
            for bit in range(tile_bits):
                if tile >> bit & 1 == 0:
                    edge = ((tile >> bit) + 1 << bit) - 1
                    tails[1 + bit, place, :] = jnp.exp(columns[edge][LANES - 1 :] - columns[tile])
    for late in range(tiles):
        for early in range(tiles):
            if early > late:
                weights[
                    :, early * LANES : (early + 1) * LANES, late * LANES : (late + 1) * LANES
                ] = jnp.zeros((weights.shape[0], LANES, LANES), BF16)
    lane = lax.broadcasted_iota(jnp.int32, (GROUP, LANES), 1)
    row = lax.broadcasted_iota(jnp.int32, (GROUP, LANES), 0)
    inside = bit_length((lane % GROUP) ^ row, low_bits)
    ahead = row <= lane % GROUP
    lane_group = lax.broadcasted_iota(jnp.int32, (groups, LANES), 1) // GROUP
    row_group = lax.broadcasted_iota(jnp.int32, (groups, LANES), 0)
    between = bit_length(lane_group ^ row_group, groups.bit_length() - 1)
    before = row_group < lane_group
    same = (
        lax.broadcasted_iota(jnp.int32, (groups, 1, LANES), 2) // GROUP
        == lax.broadcasted_iota(jnp.int32, (groups, 1, LANES), 0)
    )
    index = lax.axis_index("seq")
    is_upper = index % 2 == 1
    share = head_count // shards

    def spread(kind, place, head):
        chosen = jnp.full((LANES, LANES), head, jnp.int32)
        return jnp.take_along_axis(
            tails[kind, place, :], chosen, axis=1, mode="promise_in_bounds"
        )

    def one_head(head, slot):
        logs = log_ref[pl.ds(head, 1), :]
        gain_rows = [
            gains_ref[pl.ds(level * head_count + head, 1), :]
            for level in range(tile_levels + tile_bits + 2)
        ]
        for late in range(tiles):
            span = slice(late * LANES, (late + 1) * LANES)
            own = logs[:, span]
            start = late * LANES + middle
            grown = jnp.exp(own - logs[:, start : start + 1])
            corner = jnp.zeros((GROUP, LANES), F32)
            for level in range(low_bits + 1):
                gain = gain_rows[level][:, span] * grown
                corner = jnp.where(ahead & (inside == level), gain, corner)
            rest = jnp.zeros((groups, LANES), F32)
            for level in range(low_bits + 1, tile_levels + 1):
                gain = gain_rows[level][:, span] * grown
                rest = jnp.where(before & (between == level - low_bits), gain, rest)
            chosen = jnp.where(same, corner[None], rest[:, None, :]).reshape(LANES, LANES)
            weight = chosen * spread(0, span, head) * scores[span, span]
            weights[slot, span, span] = weight.astype(BF16)
            for bit in range(tile_bits):
                if late >> bit & 1 == 0:
                    continue
                edge = (late >> bit << bit) * LANES - 1
                level = tile_levels + 1 + bit
                factor = gain_rows[level][:, span] * jnp.exp(
                    own - logs[:, edge : edge + 1]
                )
                for early in range(((late >> bit) - 1) << bit, (late >> bit) << bit):
                    place = slice(early * LANES, (early + 1) * LANES)
                    weight = spread(1 + bit, place, head) * factor * scores[place, span]
                    weights[slot, place, span] = weight.astype(BF16)
        at = pl.ds(pl.multiple_of(head * LANES, LANES), LANES)
        level = tile_levels + tile_bits + 1
        factor = gain_rows[level] * jnp.exp(jnp.where(is_upper, logs, -1e30))
        owner, local = head // share, head % share
        start = jnp.where(owner % 2 == index % 2, 0, inner // 2)
        start = start + (owner // 2 * share + local) * LANES
        node = node_ref[pl.ds(pl.multiple_of(start, LANES), LANES), :]
        far = product(node, queries) * factor
        for start in range(0, rows, wide):
            upto = start + wide
            near_ref[at, start:upto] = far[:, start:upto] + product(
                acts_ref[at, :upto], weights[slot, :upto, start:upto]
            )

    def some_heads(step, carry):
        for slot in range(weights.shape[0]):
            one_head(step * weights.shape[0] + slot, slot)
        return carry

    lax.fori_loop(heads[0] // weights.shape[0], heads[1] // weights.shape[0], some_heads, 0)


def near(acts, maps, log, gains, node, after, gain, earlier, heads, shards):
    head_count, rows = log.shape
    wide = min(rows, 2 * LANES)
    tile_bits = (rows // LANES).bit_length() - 1
    first = earlier is None
    out_shape = [pltpu.VMEM((head_count * LANES, rows), F32)]
    operands = [acts, maps, log, gains, node, after]
    aliases = {}
    if first:
        out_shape.append(pltpu.VMEM((rows, rows), F32))
        out_shape.append(pltpu.VMEM((1 + tile_bits, rows, LANES), F32))
        out_shape.append(pltpu.VMEM((LANES, LANES), F32))
        operands.append(gain.reshape(head_count, LANES))
    else:
        near_term, scores, tails, _ = earlier
        operands += [scores, tails, near_term]
        aliases = {len(operands) - 1: 0}
    made = pl.pallas_call(
        functools.partial(near_kernel, first=first, wide=wide, heads=heads, shards=shards),
        in_specs=[VMEM_SPEC] * len(operands),
        out_specs=[VMEM_SPEC] * len(out_shape),
        out_shape=out_shape,
        input_output_aliases=aliases,
        scratch_shapes=[
            pltpu.VMEM((LANES, rows), F32),
            pltpu.VMEM((2, rows, rows), BF16),
        ],
        compiler_params=params(),
        cost_estimate=pl.CostEstimate(
            flops=2 * head_count * rows * rows * LANES, bytes_accessed=10 << 20, transcendentals=0
        ),
        name="near",
    )(*in_vmem(*operands))
    return made if first else [made[0], *earlier[1:]]


def far_product(node_ref, first_row, count, queries):
    return product(node_ref[first_row : first_row + count, :], queries)


def far_factor(gains_ref, log_ref, stats_ref, head, level, base):
    is_upper = (lax.axis_index("seq") >> level) % 2 == 1
    shift = stats_ref[1, pl.ds(head, 1), :][:, :1]
    exponent = jnp.where(is_upper, log_ref[pl.ds(head, 1), :] + shift, -1e30)
    row = (base + level) * log_ref.shape[0] + head
    return gains_ref[pl.ds(row, 1), :] * jnp.exp(exponent)


def middle_kernel(*refs, places, relatives, levels, shards):
    count = len(places)
    acts_ref, log_ref, gains_ref = refs[:3]
    stats = refs[3 : 3 + count]
    sources = refs[3 + count : -2]
    total_ref = refs[-1]
    head_count, _ = log_ref.shape
    part = head_count // shards * LANES
    inner = head_count * LANES
    state_size = acts_ref.shape[0] - inner >> 1
    shard = lax.axis_index("seq") % shards
    base = gains_ref.shape[0] // head_count - levels
    queries = acts_ref[inner + state_size :, :]
    for relative in relatives:
        terms = []
        for slot in range(count):
            source, start = places[slot][relative]
            terms.append(far_product(sources[source], start, part, queries))
        for local in range(head_count // shards):
            head = (relative ^ shard) * (head_count // shards) + local
            at = pl.ds(pl.multiple_of(head * LANES, LANES), LANES)
            total = total_ref[at, :]
            for slot in range(count):
                factor = far_factor(gains_ref, log_ref, stats[slot], head, slot + 1, base)
                total = total + terms[slot][local * LANES : (local + 1) * LANES] * factor
            total_ref[at, :] = total


def middle(
    near_term, acts, log, gains, stats, sources, places, relatives, levels, shards
):
    operands = [acts, log, gains, *stats, *sources, near_term]
    return pl.pallas_call(
        functools.partial(
            middle_kernel, places=places, relatives=relatives, levels=levels, shards=shards
        ),
        in_specs=[VMEM_SPEC] * len(operands),
        out_specs=VMEM_SPEC,
        out_shape=pltpu.VMEM(near_term.shape, F32),
        input_output_aliases={len(operands) - 1: 0},
        compiler_params=params(),
        cost_estimate=small_cost(),
        name="middle",
    )(*in_vmem(*operands))


def last_kernel(
    total_ref, acts_ref, log_ref, gains_ref, columns_ref, stats_ref, node_ref, *refs,
    level, relatives, done, shards, base
):
    head_count, rows = log_ref.shape
    share = head_count // shards
    part = share * LANES
    inner = head_count * LANES
    state_size = acts_ref.shape[0] - inner >> 1
    shard = lax.axis_index("seq") % shards
    queries = acts_ref[inner + state_size :, :]
    copies = []
    if done:
        out_hbm, mixed_ref, sems = refs[-3:]

    def send(source_ref, place, relative, first, count):
        start = pl.multiple_of((relative ^ shard) * part, part)
        copies.append(
            pltpu.make_async_copy(
                source_ref.at[place, pl.ds(first, count), :],
                out_hbm.at[pl.ds(first, count), pl.ds(start, part)],
                sems.at[len(copies)],
            )
        )
        copies[-1].start()

    if done:
        for relative, source_ref in zip(done, refs):
            send(source_ref, 0, relative, 0, rows)
    else:
        (mixed_ref,) = refs
    for place, relative in enumerate(relatives):
        term = far_product(node_ref, place * part, part, queries)
        heads = [(relative ^ shard) * share + local for local in range(share)]
        places = [pl.ds(pl.multiple_of(head * LANES, LANES), LANES) for head in heads]
        factors = [
            far_factor(gains_ref, log_ref, stats_ref, head, level, base) for head in heads
        ]
        gain_columns = [
            jnp.take_along_axis(
                columns_ref[...],
                jnp.full((LANES, LANES), head, jnp.int32),
                axis=1,
                mode="promise_in_bounds",
            )
            for head in heads
        ]
        for first in range(0, rows, LANES):
            span = slice(first, first + LANES)
            for local in range(share):
                own = term[local * LANES : (local + 1) * LANES, span]
                total = total_ref[places[local], span] + own * factors[local][:, span]
                mean = jnp.mean(total * total, axis=0, keepdims=True)
                scale = lax.rsqrt(mean + 1e-05)
                mixed = (total * scale * gain_columns[local]).astype(BF16).T
                mixed_ref[place, span, local * LANES : (local + 1) * LANES] = mixed
            if done:
                send(mixed_ref, place, relative, first, LANES)
    for copy in copies:
        copy.wait()


def last(total, acts, log, gains, columns, stats, node, level, levels, relatives, shards, done):
    head_count, rows = log.shape
    share = head_count // shards
    operands = [total, acts, log, gains, columns, stats, node, *done.values()]
    mixed = pltpu.VMEM((len(relatives), rows, share * LANES), BF16)
    copies = len(done) + len(relatives) * rows // LANES
    whole = jax.ShapeDtypeStruct((rows, head_count * LANES), BF16)
    return pl.pallas_call(
        functools.partial(
            last_kernel, level=level, relatives=relatives, done=tuple(done), shards=shards,
            base=gains.shape[0] // head_count - levels,
        ),
        in_specs=[VMEM_SPEC] * len(operands),
        out_specs=HBM_SPEC if done else VMEM_SPEC,
        out_shape=whole if done else mixed,
        scratch_shapes=[mixed, pltpu.SemaphoreType.DMA((copies,))] if done else [],
        compiler_params=params(),
        cost_estimate=small_cost(),
        name="last",
    )(*in_vmem(*operands))


def moved(value, apart):
    return lax.ppermute(value, "seq", [(i, i ^ apart) for i in range(lax.axis_size("seq"))])


def onward(devices):
    route = {index: index + 1 for index in range(devices)}
    planes = devices // 4
    target = 0
    for plane in range(1, planes - 1):
        route[4 * plane + 2] = target
        target = 4 * plane + 3
    route[devices - 1] = target
    return list(route.items())


def on_device(xbc, conv_weight, log_decay, level_weights, gain):
    rows = xbc.shape[0]
    head_count = log_decay.shape[0]
    devices = lax.axis_size("seq")
    levels = devices.bit_length() - 1
    shards = 4
    part = head_count * LANES // shards
    gains = level_weights.transpose(1, 0, 2).reshape(-1, rows)
    beyond = onward(devices)
    early = head_count // 4
    values, taps, log, edge, acts, head, maps, state = load(xbc, conv_weight, log_decay, early)
    far_edge = lax.ppermute(edge, "seq", beyond)
    near_edge = moved(edge, 1)
    acts, head, state = front(values, taps, log, maps, acts, head, state, early)
    acts, maps, state, away, home = edge_rows(
        far_edge, near_edge, log, taps, values, head, acts, maps, state, shards
    )
    joined = moved(away, 1)
    first_node = jnp.concatenate([joined[: home.shape[0]], moved(home, 1)])
    own, stats, send, rest = pair(state, log, joined, shards)
    near_made = None
    all_stats = [stats]
    got = []
    for bit in range(1, levels - 1):
        got.append(moved(send, 1 << bit))
        if bit <= 2:
            half = head_count // 2
            heads = (half * (bit - 1), half * bit)
            near_made = near(
                acts, maps, log, gains, first_node, stats, gain, near_made, heads, shards
            )
        sources = [rest, *got[1:]] if bit == levels - 2 else []
        stats, send, own = join(own, stats, got[-1], near_made[0], bit, shards, sources)
        all_stats.append(stats)
    top = levels - 1

    node = moved(send, 1 << top)
    count = len(got)
    across = moved(own, 2)
    shared = (acts, log, gains, all_stats[:count])
    direct = [{0: (slot, 0)} for slot in range(count)]
    crossed = [{2: (0, slot * part)} for slot in range(count)]
    relayed = [{1: (slot, 0), 3: (count + slot, 0)} for slot in range(count)]
    total = middle(near_made[0], *shared, got, direct, (0,), levels, shards)
    node, total = lax.optimization_barrier((node, total))
    common = (acts, log, gains, near_made[3], all_stats[-1])
    node_across = moved(node, 2)
    own_done = last(total, *common, node, top, levels, (0,), shards, {})
    shares = [kept[:part] for kept in got]
    shares += [across[slot * part : (slot + 1) * part] for slot in range(count)]
    own_done, shares, total = lax.optimization_barrier((own_done, shares, total))
    beside = [moved(kept, 1) for kept in shares]
    total = middle(total, *shared, [across], crossed, (2,), levels, shards)
    node_across, beside, total = lax.optimization_barrier((node_across, beside, total))
    node_beside = moved(jnp.concatenate([node, node_across]), 1)
    total = middle(total, *shared, beside, relayed, (1, 3), levels, shards)
    across_done = last(total, *common, node_across, top, levels, (2,), shards, {})
    done = {0: own_done, 2: across_done}
    return last(total, *common, node_beside, top, levels, (1, 3), shards, done)


def solution(mesh):
    in_specs = (
        P(("groups", "seq"), None),
        P(),
        P(None, ("groups", "seq")),
        P(None, None, ("groups", "seq")),
        P(),
    )
    out_specs = P(("groups", "seq"), None)
    return jax.shard_map(
        on_device, mesh=mesh, in_specs=in_specs, out_specs=out_specs, check_vma=False
    )
```

```python
import functools

import jax
import jax.numpy as jnp
from jax import lax
from jax.experimental import pallas as pl
from jax.experimental.pallas import tpu as pltpu
from jax.sharding import PartitionSpec as P

F32 = jnp.float32
BF16 = jnp.bfloat16
LANES = 128
GROUP = 8
PARTS = 3
VMEM_LIMIT = 24 << 20
HBM_SPEC = pl.BlockSpec(memory_space=pltpu.HBM)
VMEM_SPEC = pl.BlockSpec(memory_space=pltpu.VMEM)


def in_vmem(*arrays):
    return [pltpu.with_memory_space_constraint(array, pltpu.VMEM) for array in arrays]


def in_hbm(*arrays):
    return [pltpu.with_memory_space_constraint(array, pltpu.HBM) for array in arrays]


def params():
    return pltpu.CompilerParams(vmem_limit_bytes=VMEM_LIMIT)


def small_cost():
    return pl.CostEstimate(flops=1024, bytes_accessed=1024, transcendentals=0)


def product(left, right):
    return jnp.dot(left, right, preferred_element_type=F32)


def write_spans(message_ref, first_row, spans):
    head_count = spans.shape[0]
    for part in range(PARTS):
        rounded = spans.astype(BF16)
        start = first_row + part * head_count
        message_ref[start : start + head_count, :] = rounded
        spans = spans - rounded.astype(F32)


def read_spans(message_ref, first_row, head_count):
    total = None
    for part in range(PARTS):
        start = first_row + part * head_count
        piece = message_ref[start : start + head_count, :].astype(F32)
        total = piece if total is None else total + piece
    return total


def running_sum(logs):
    head_count, rows = logs.shape
    tiles = rows // LANES
    row = lax.broadcasted_iota(jnp.int32, (LANES, LANES), 0)
    column = lax.broadcasted_iota(jnp.int32, (LANES, LANES), 1)
    upto = (row <= column).astype(BF16)
    left = jnp.concatenate(
        [logs[:, tile * LANES : (tile + 1) * LANES] for tile in range(tiles)], axis=0
    )
    pieces = []
    for _ in range(3):
        pieces.append(left.astype(BF16))
        left = left - pieces[-1].astype(F32)
    size = head_count * tiles
    added = product(jnp.concatenate(pieces, axis=0), upto)
    within = added[2 * size :] + added[size : 2 * size] + added[:size]
    sums = []
    offset = jnp.zeros((head_count, 1), F32)
    for tile in range(tiles):
        part = within[tile * head_count : (tile + 1) * head_count]
        sums.append(part + offset)
        offset = offset + part[:, LANES - 1 :]
    return jnp.concatenate(sums, axis=1)


def activated(values, edge, weights, padded):
    rows = values.shape[0]
    taps = weights.shape[0]
    padded[GROUP : GROUP + rows, :] = values
    if edge is not None:
        padded[GROUP - taps + 1 : GROUP, :] = edge
    total = None
    for tap in range(taps):
        first = GROUP - taps + 1 + tap
        shifted = values if tap == taps - 1 else padded[first : first + rows, :]
        term = shifted * weights[tap : tap + 1]
        total = term if total is None else total + term
    return (total * jax.nn.sigmoid(total)).astype(BF16)


def some_columns(xbc_ref, taps_ref, acts_ref, head_ref, padded, start):
    part = slice(start, start + LANES)
    values = xbc_ref[:, part].astype(F32)
    result = activated(values, None, taps_ref[:, part], padded)
    head_ref[:, part] = result[:LANES]
    turned = result[LANES:].T
    acts_ref[part, LANES:] = turned
    return result, turned


def head_columns(
    xbc_ref, taps_ref, log_ref, maps_ref, acts_ref, head_ref, state_ref, padded, heads
):
    rows, _ = xbc_ref.shape
    for head in heads:
        place = slice(head * LANES, (head + 1) * LANES)
        _, turned = some_columns(
            xbc_ref, taps_ref, acts_ref, head_ref, padded.at[head % 2], head * LANES
        )
        logs = log_ref[head : head + 1, :]
        tail = jnp.exp(logs[:, rows - 1 : rows] - logs[:, LANES:])
        decayed = (turned.astype(F32) * tail).astype(BF16)
        state_ref[place, :] = product(decayed, maps_ref[LANES:, :])


def load_kernel(
    xbc_hbm, taps_hbm, decay_hbm, xbc_ref, taps_ref, log_ref, edge_ref, acts_ref, head_ref,
    maps_ref, state_ref, decay_buf, padded, sems, early
):
    rows, width = xbc_ref.shape
    pieces = sems.shape[0] - 2
    maps_width = 2 * maps_ref.shape[1]
    inner = width - maps_width
    rest = (inner - early * LANES) // (pieces - 2)
    cuts = [0] + [early * LANES + piece * rest for piece in range(pieces - 1)]
    spans = [(inner, maps_width)] + [(x, y - x) for x, y in zip(cuts, cuts[1:])]
    copies = [
        pltpu.make_async_copy(decay_hbm, decay_buf, sems.at[pieces]),
        pltpu.make_async_copy(taps_hbm, taps_ref, sems.at[pieces + 1]),
    ]
    for piece, (start, size) in enumerate(spans):
        part = pl.ds(start, size)
        copies.append(
            pltpu.make_async_copy(xbc_hbm.at[:, part], xbc_ref.at[:, part], sems.at[piece])
        )
    for copy in copies[:4]:
        copy.start()
    for copy in copies[4:]:
        copy.start()
    copies[0].wait()
    log_ref[...] = running_sum(decay_buf[...])
    copies[1].wait()
    copies[2].wait()
    for slot, start in enumerate(range(width - LANES, inner - 1, -LANES)):
        result, _ = some_columns(
            xbc_ref, taps_ref, acts_ref, head_ref, padded.at[slot % 2], start
        )
    maps_ref[...] = result
    copies[3].wait()
    head_columns(
        xbc_ref, taps_ref, log_ref, maps_ref, acts_ref, head_ref, state_ref, padded, range(early)
    )
    for copy in copies[4:]:
        copy.wait()
    few = edge_ref.shape[0]
    tail = xbc_ref[rows - 2 * GROUP :, :].astype(F32)
    edge_ref[...] = tail[2 * GROUP - few :].astype(BF16)


def load(xbc, conv_weight, log_decay, early):
    rows, width = xbc.shape
    inner = log_decay.shape[0] * LANES
    state_size = (width - inner) // 2
    pieces = 3
    return pl.pallas_call(
        functools.partial(load_kernel, early=early),
        in_specs=[HBM_SPEC] * 3,
        out_specs=[VMEM_SPEC] * 8,
        out_shape=[
            pltpu.VMEM(xbc.shape, BF16),
            pltpu.VMEM(conv_weight.shape, F32),
            pltpu.VMEM(log_decay.shape, F32),
            pltpu.VMEM((conv_weight.shape[0] - 1, width), BF16),
            pltpu.VMEM((width, rows), BF16),
            pltpu.VMEM((LANES, width), BF16),
            pltpu.VMEM((rows, state_size), BF16),
            pltpu.VMEM((inner, state_size), F32),
        ],
        scratch_shapes=[
            pltpu.VMEM(log_decay.shape, F32),
            pltpu.VMEM((2, rows + GROUP, LANES), F32),
            pltpu.SemaphoreType.DMA((pieces + 2,)),
        ],
        compiler_params=params(),
        cost_estimate=small_cost(),
        name="load",
    )(*in_hbm(xbc, conv_weight, log_decay))


def front_kernel(
    xbc_ref, taps_ref, log_ref, maps_ref, acts_in, head_in, state_in, acts_ref, head_ref,
    state_ref, padded, early
):
    head_columns(
        xbc_ref, taps_ref, log_ref, maps_ref, acts_ref, head_ref, state_ref, padded,
        range(early, log_ref.shape[0]),
    )


def front(xbc, taps, log, maps, acts, head, state, early):
    rows, _ = xbc.shape
    operands = [xbc, taps, log, maps, acts, head, state]
    return pl.pallas_call(
        functools.partial(front_kernel, early=early),
        in_specs=[VMEM_SPEC] * len(operands),
        out_specs=[VMEM_SPEC] * 3,
        out_shape=[
            pltpu.VMEM(acts.shape, BF16),
            pltpu.VMEM(head.shape, BF16),
            pltpu.VMEM(state.shape, F32),
        ],
        input_output_aliases={4: 0, 5: 1, 6: 2},
        scratch_shapes=[pltpu.VMEM((2, rows + GROUP, LANES), F32)],
        compiler_params=params(),
        name="front",
    )(*in_vmem(*operands))


def edge_kernel(
    far_edge_ref, near_edge_ref, log_ref, taps_ref, xbc_ref, head_ref, *refs, shards
):
    acts_ref, maps_ref, state_ref, away_ref, home_ref, padded = refs[-6:]
    head_count, rows = log_ref.shape
    width = head_ref.shape[1]
    inner = head_count * LANES
    few = 2 * GROUP
    index = lax.axis_index("seq")

    def first_tile(start, slot):
        part = slice(start, start + LANES)
        near_edge = near_edge_ref[:, part].astype(F32)
        far_edge = far_edge_ref[:, part].astype(F32)
        edge = jnp.where(index % 2 == 1, near_edge, jnp.where(index == 0, 0.0, far_edge))
        values = xbc_ref[:few, part].astype(F32)
        result = activated(values, edge, taps_ref[:, part], padded.at[slot])
        block = jnp.concatenate([result, head_ref[few:, part]], axis=0)
        turned = block.T
        acts_ref[part, :LANES] = turned
        return block, turned

    first_tile(width - LANES, 0)
    maps, _ = first_tile(width - 2 * LANES, 1)
    maps_ref[:LANES, :] = maps
    totals = jnp.broadcast_to(log_ref[:, rows - 1 : rows], (head_count, LANES))
    write_spans(away_ref, inner // 2, totals)
    parity = index % 2
    for head in range(head_count):
        part = slice(head * LANES, (head + 1) * LANES)
        _, turned = first_tile(head * LANES, head % padded.shape[0])
        logs = log_ref[head : head + 1, :]
        tail = jnp.exp(logs[:, rows - 1 : rows] - logs[:, :LANES])
        decayed = (turned.astype(F32) * tail).astype(BF16)
        state = state_ref[part, :] + product(decayed, maps)
        state_ref[part, :] = state
    part = inner // shards
    for slot in range(shards // 2):
        place = slice(slot * part, (slot + 1) * part)
        kept = pl.multiple_of((2 * slot + parity) * part, part)
        given = pl.multiple_of((2 * slot + 1 - parity) * part, part)
        away_ref[place, :] = state_ref[pl.ds(given, part), :].astype(BF16)
        home_ref[place, :] = state_ref[pl.ds(kept, part), :].astype(BF16)


def edge_rows(far_edge, near_edge, log, taps, xbc, head, acts, maps, state, shards):
    head_count, _ = log.shape
    inner, state_size = state.shape
    operands = [far_edge, near_edge, log, taps, xbc, head, acts, maps, state]
    return pl.pallas_call(
        functools.partial(edge_kernel, shards=shards),
        in_specs=[VMEM_SPEC] * len(operands),
        out_specs=[VMEM_SPEC] * 5,
        out_shape=[
            pltpu.VMEM(acts.shape, BF16),
            pltpu.VMEM(maps.shape, BF16),
            pltpu.VMEM(state.shape, F32),
            pltpu.VMEM((inner // 2 + PARTS * head_count, state_size), BF16),
            pltpu.VMEM((inner // 2, state_size), BF16),
        ],
        input_output_aliases={6: 0, 7: 1, 8: 2},
        scratch_shapes=[pltpu.VMEM((2, 3 * GROUP, LANES), F32)],
        compiler_params=params(),
        cost_estimate=small_cost(),
        name="edge",
    )(*in_vmem(*operands))


def pair_kernel(state_ref, log_ref, got_ref, own_ref, stats_ref, send_ref, rest_ref, shards):
    head_count, rows = log_ref.shape
    inner = state_ref.shape[0]
    index = lax.axis_index("seq")
    is_upper = index % 2 == 1
    mine = jnp.broadcast_to(log_ref[:, rows - 1 : rows], (head_count, LANES))
    theirs = read_spans(got_ref, inner // 2, head_count)
    stats_ref[0] = mine + theirs
    stats_ref[1] = jnp.where(is_upper, theirs, 0.0)
    write_spans(send_ref, inner // shards, mine + theirs)
    stats_ref[2] = jnp.exp(mine)
    stats_ref[3] = jnp.exp(theirs)
    shard = index % shards
    share = head_count // shards

    def joined(owner, local):
        head = owner * share + local
        at = pl.ds(pl.multiple_of(head * LANES, LANES), LANES)
        own = state_ref[at, :]
        start = pl.multiple_of((owner // 2 * share + local) * LANES, LANES)
        got = got_ref[pl.ds(start, LANES), :].astype(F32)
        late = jnp.where(is_upper, own, got)
        early = jnp.where(is_upper, got, own)
        late_row = jnp.where(is_upper, 2, 3)
        return early * stats_ref[late_row, pl.ds(head, 1), :] + late

    for local in range(share):
        place = slice(local * LANES, (local + 1) * LANES)
        send_ref[place, :] = joined(shard ^ 2, local).astype(BF16)
        kept = joined(shard, local)
        own_ref[place, :] = kept
        rest_ref[place, :] = kept.astype(BF16)


def pair(state, log, got, shards):
    head_count, _ = log.shape
    inner, state_size = state.shape
    part = inner // shards
    return pl.pallas_call(
        functools.partial(pair_kernel, shards=shards),
        in_specs=[VMEM_SPEC] * 3,
        out_specs=[VMEM_SPEC] * 4,
        out_shape=[
            pltpu.VMEM((part, state_size), F32),
            pltpu.VMEM((4, head_count, LANES), F32),
            pltpu.VMEM((part + PARTS * head_count, state_size), BF16),
            pltpu.VMEM((part, state_size), BF16),
        ],
        compiler_params=params(),
        cost_estimate=small_cost(),
        name="pair",
    )(*in_vmem(state, log, got))


def join_kernel(own_ref, stats_ref, got_ref, _, *refs, bit, shards, gathered):
    sources = refs[:gathered]
    if gathered:
        next_stats_ref, send_ref, across_ref = refs[gathered:]
    else:
        next_stats_ref, send_ref, next_ref = refs
    part = own_ref.shape[0]
    head_count = stats_ref.shape[1]
    share = head_count // shards
    index = lax.axis_index("seq")
    is_upper = (index >> bit) % 2 == 1
    mine = stats_ref[0]
    theirs = read_spans(got_ref, part, head_count)
    next_stats_ref[0] = mine + theirs
    next_stats_ref[1] = stats_ref[1] + jnp.where(is_upper, theirs, 0.0)
    next_stats_ref[2] = jnp.exp(jnp.where(is_upper, mine, theirs))
    next_stats_ref[3] = jnp.zeros_like(mine)
    if not gathered:
        write_spans(send_ref, part, mine + theirs)
    for local in range(share):
        place = slice(local * LANES, (local + 1) * LANES)
        head = (index % shards) * share + local
        own = own_ref[place, :]
        got = got_ref[place, :].astype(F32)
        late = jnp.where(is_upper, own, got)
        early = jnp.where(is_upper, got, own)
        total = early * next_stats_ref[2, pl.ds(head, 1), :] + late
        send_ref[place, :] = total.astype(BF16)
        if not gathered:
            next_ref[place, :] = total
    for slot in range(gathered):
        across_ref[slot * part : (slot + 1) * part, :] = sources[slot][:part, :]


def join(own, stats, got, after, bit, shards, sources):
    operands = [own, stats, got, after, *sources]
    message = own.shape if sources else got.shape
    out_shape = [pltpu.VMEM(stats.shape, F32), pltpu.VMEM(message, BF16)]
    if sources:
        out_shape.append(pltpu.VMEM((len(sources) * own.shape[0], own.shape[1]), BF16))
    else:
        out_shape.append(pltpu.VMEM(own.shape, F32))
    return pl.pallas_call(
        functools.partial(join_kernel, bit=bit, shards=shards, gathered=len(sources)),
        in_specs=[VMEM_SPEC] * len(operands),
        out_specs=[VMEM_SPEC] * 3,
        out_shape=out_shape,
        compiler_params=params(),
        cost_estimate=small_cost(),
        name="join",
    )(*in_vmem(*operands))


def bit_length(numbers, limit):
    counted = jnp.zeros(numbers.shape, jnp.int32)
    for power in range(limit):
        counted = counted + (numbers >= 1 << power).astype(jnp.int32)
    return counted


def near_kernel(*refs, first, wide, heads, shards):
    if first:
        acts_ref, maps_ref, log_ref, gains_ref, node_ref, _, gain_ref = refs[:7]
        near_ref, scores, tails, columns_ref, turned, weights = refs[7:]
    else:
        acts_ref, maps_ref, log_ref, gains_ref, node_ref, _, scores, tails, _ = refs[:9]
        near_ref, turned, weights = refs[9:]
    head_count, rows = log_ref.shape
    inner = head_count * LANES
    state_size = maps_ref.shape[1]
    tiles = rows // LANES
    tile_bits = tiles.bit_length() - 1
    groups = LANES // GROUP
    low_bits = GROUP.bit_length() - 1
    tile_levels = LANES.bit_length() - 1
    queries = acts_ref[inner + state_size :, :]
    middle = LANES // 2 - 1
    if first:
        for start in range(0, rows, wide):
            upto = start + wide
            scores[:upto, start:upto] = product(maps_ref[:upto, :], queries[:, start:upto])
        turned[head_count:, :] = jnp.zeros((LANES - head_count, rows), F32)
        turned[:head_count, :LANES] = gain_ref[...]
        columns_ref[...] = turned[:, :LANES].T
        turned[:head_count, :] = log_ref[...]
        columns = [turned[:, tile * LANES : (tile + 1) * LANES].T for tile in range(tiles)]
        for tile in range(tiles):
            place = slice(tile * LANES, (tile + 1) * LANES)
            tails[0, place, :] = jnp.exp(columns[tile][middle : middle + 1] - columns[tile])
            for bit in range(tile_bits):
                if tile >> bit & 1 == 0:
                    edge = ((tile >> bit) + 1 << bit) - 1
                    tails[1 + bit, place, :] = jnp.exp(columns[edge][LANES - 1 :] - columns[tile])
    for late in range(tiles):
        for early in range(tiles):
            if early > late:
                weights[
                    :, early * LANES : (early + 1) * LANES, late * LANES : (late + 1) * LANES
                ] = jnp.zeros((weights.shape[0], LANES, LANES), BF16)
    lane = lax.broadcasted_iota(jnp.int32, (GROUP, LANES), 1)
    row = lax.broadcasted_iota(jnp.int32, (GROUP, LANES), 0)
    inside = bit_length((lane % GROUP) ^ row, low_bits)
    ahead = row <= lane % GROUP
    lane_group = lax.broadcasted_iota(jnp.int32, (groups, LANES), 1) // GROUP
    row_group = lax.broadcasted_iota(jnp.int32, (groups, LANES), 0)
    between = bit_length(lane_group ^ row_group, groups.bit_length() - 1)
    before = row_group < lane_group
    same = (
        lax.broadcasted_iota(jnp.int32, (groups, 1, LANES), 2) // GROUP
        == lax.broadcasted_iota(jnp.int32, (groups, 1, LANES), 0)
    )
    index = lax.axis_index("seq")
    is_upper = index % 2 == 1
    share = head_count // shards

    def spread(kind, place, head):
        chosen = jnp.full((LANES, LANES), head, jnp.int32)
        return jnp.take_along_axis(
            tails[kind, place, :], chosen, axis=1, mode="promise_in_bounds"
        )

    def one_head(head, slot):
        logs = log_ref[pl.ds(head, 1), :]
        gain_rows = [
            gains_ref[pl.ds(level * head_count + head, 1), :]
            for level in range(tile_levels + tile_bits + 2)
        ]
        for late in range(tiles):
            span = slice(late * LANES, (late + 1) * LANES)
            own = logs[:, span]
            start = late * LANES + middle
            grown = jnp.exp(own - logs[:, start : start + 1])
            corner = jnp.zeros((GROUP, LANES), F32)
            for level in range(low_bits + 1):
                gain = gain_rows[level][:, span] * grown
                corner = jnp.where(ahead & (inside == level), gain, corner)
            rest = jnp.zeros((groups, LANES), F32)
            for level in range(low_bits + 1, tile_levels + 1):
                gain = gain_rows[level][:, span] * grown
                rest = jnp.where(before & (between == level - low_bits), gain, rest)
            chosen = jnp.where(same, corner[None], rest[:, None, :]).reshape(LANES, LANES)
            weight = chosen * spread(0, span, head) * scores[span, span]
            weights[slot, span, span] = weight.astype(BF16)
            for bit in range(tile_bits):
                if late >> bit & 1 == 0:
                    continue
                edge = (late >> bit << bit) * LANES - 1
                level = tile_levels + 1 + bit
                factor = gain_rows[level][:, span] * jnp.exp(
                    own - logs[:, edge : edge + 1]
                )
                for early in range(((late >> bit) - 1) << bit, (late >> bit) << bit):
                    place = slice(early * LANES, (early + 1) * LANES)
                    weight = spread(1 + bit, place, head) * factor * scores[place, span]
                    weights[slot, place, span] = weight.astype(BF16)
        at = pl.ds(pl.multiple_of(head * LANES, LANES), LANES)
        level = tile_levels + tile_bits + 1
        factor = gain_rows[level] * jnp.exp(jnp.where(is_upper, logs, -1e30))
        owner, local = head // share, head % share
        start = jnp.where(owner % 2 == index % 2, 0, inner // 2)
        start = start + (owner // 2 * share + local) * LANES
        node = node_ref[pl.ds(pl.multiple_of(start, LANES), LANES), :]
        far = product(node, queries) * factor
        for start in range(0, rows, wide):
            upto = start + wide
            near_ref[at, start:upto] = far[:, start:upto] + product(
                acts_ref[at, :upto], weights[slot, :upto, start:upto]
            )

    def some_heads(step, carry):
        for slot in range(weights.shape[0]):
            one_head(step * weights.shape[0] + slot, slot)
        return carry

    lax.fori_loop(heads[0] // weights.shape[0], heads[1] // weights.shape[0], some_heads, 0)


def near(acts, maps, log, gains, node, after, gain, earlier, heads, shards):
    head_count, rows = log.shape
    wide = min(rows, 2 * LANES)
    tile_bits = (rows // LANES).bit_length() - 1
    first = earlier is None
    out_shape = [pltpu.VMEM((head_count * LANES, rows), F32)]
    operands = [acts, maps, log, gains, node, after]
    aliases = {}
    if first:
        out_shape.append(pltpu.VMEM((rows, rows), F32))
        out_shape.append(pltpu.VMEM((1 + tile_bits, rows, LANES), F32))
        out_shape.append(pltpu.VMEM((LANES, LANES), F32))
        operands.append(gain.reshape(head_count, LANES))
    else:
        near_term, scores, tails, _ = earlier
        operands += [scores, tails, near_term]
        aliases = {len(operands) - 1: 0}
    made = pl.pallas_call(
        functools.partial(near_kernel, first=first, wide=wide, heads=heads, shards=shards),
        in_specs=[VMEM_SPEC] * len(operands),
        out_specs=[VMEM_SPEC] * len(out_shape),
        out_shape=out_shape,
        input_output_aliases=aliases,
        scratch_shapes=[
            pltpu.VMEM((LANES, rows), F32),
            pltpu.VMEM((2, rows, rows), BF16),
        ],
        compiler_params=params(),
        cost_estimate=pl.CostEstimate(
            flops=2 * head_count * rows * rows * LANES, bytes_accessed=10 << 20, transcendentals=0
        ),
        name="near",
    )(*in_vmem(*operands))
    return made if first else [made[0], *earlier[1:]]


def far_product(node_ref, first_row, count, queries):
    return product(node_ref[first_row : first_row + count, :], queries)


def far_factor(gains_ref, log_ref, stats_ref, head, level, base):
    is_upper = (lax.axis_index("seq") >> level) % 2 == 1
    shift = stats_ref[1, pl.ds(head, 1), :][:, :1]
    exponent = jnp.where(is_upper, log_ref[pl.ds(head, 1), :] + shift, -1e30)
    row = (base + level) * log_ref.shape[0] + head
    return gains_ref[pl.ds(row, 1), :] * jnp.exp(exponent)


def middle_kernel(*refs, places, relatives, levels, shards):
    count = len(places)
    acts_ref, log_ref, gains_ref = refs[:3]
    stats = refs[3 : 3 + count]
    sources = refs[3 + count : -2]
    total_ref = refs[-1]
    head_count, _ = log_ref.shape
    part = head_count // shards * LANES
    inner = head_count * LANES
    state_size = acts_ref.shape[0] - inner >> 1
    shard = lax.axis_index("seq") % shards
    base = gains_ref.shape[0] // head_count - levels
    queries = acts_ref[inner + state_size :, :]
    for relative in relatives:
        terms = []
        for slot in range(count):
            source, start = places[slot][relative]
            terms.append(far_product(sources[source], start, part, queries))
        for local in range(head_count // shards):
            head = (relative ^ shard) * (head_count // shards) + local
            at = pl.ds(pl.multiple_of(head * LANES, LANES), LANES)
            total = total_ref[at, :]
            for slot in range(count):
                factor = far_factor(gains_ref, log_ref, stats[slot], head, slot + 1, base)
                total = total + terms[slot][local * LANES : (local + 1) * LANES] * factor
            total_ref[at, :] = total


def middle(
    near_term, acts, log, gains, stats, sources, places, relatives, levels, shards
):
    operands = [acts, log, gains, *stats, *sources, near_term]
    return pl.pallas_call(
        functools.partial(
            middle_kernel, places=places, relatives=relatives, levels=levels, shards=shards
        ),
        in_specs=[VMEM_SPEC] * len(operands),
        out_specs=VMEM_SPEC,
        out_shape=pltpu.VMEM(near_term.shape, F32),
        input_output_aliases={len(operands) - 1: 0},
        compiler_params=params(),
        cost_estimate=small_cost(),
        name="middle",
    )(*in_vmem(*operands))


def last_kernel(
    total_ref, acts_ref, log_ref, gains_ref, columns_ref, stats_ref, node_ref, *refs,
    level, relatives, done, sends, shards, base
):
    head_count, rows = log_ref.shape
    share = head_count // shards
    part = share * LANES
    inner = head_count * LANES
    state_size = acts_ref.shape[0] - inner >> 1
    shard = lax.axis_index("seq") % shards
    queries = acts_ref[inner + state_size :, :]
    copies = []
    if sends:
        out_hbm, mixed_ref, sems = refs[-3:]

    def send(source_ref, place, relative, first, count):
        start = pl.multiple_of((relative ^ shard) * part, part)
        copies.append(
            pltpu.make_async_copy(
                source_ref.at[place, pl.ds(first, count), :],
                out_hbm.at[pl.ds(first, count), pl.ds(start, part)],
                sems.at[len(copies)],
            )
        )
        copies[-1].start()

    for relative, source_ref in zip(done, refs):
        send(source_ref, 0, relative, 0, rows)
    if not sends:
        (mixed_ref,) = refs
    for place, relative in enumerate(relatives):
        term = far_product(node_ref, place * part, part, queries)
        heads = [(relative ^ shard) * share + local for local in range(share)]
        places = [pl.ds(pl.multiple_of(head * LANES, LANES), LANES) for head in heads]
        factors = [
            far_factor(gains_ref, log_ref, stats_ref, head, level, base) for head in heads
        ]
        gain_columns = [
            jnp.take_along_axis(
                columns_ref[...],
                jnp.full((LANES, LANES), head, jnp.int32),
                axis=1,
                mode="promise_in_bounds",
            )
            for head in heads
        ]
        for first in range(0, rows, LANES):
            span = slice(first, first + LANES)
            for local in range(share):
                own = term[local * LANES : (local + 1) * LANES, span]
                total = total_ref[places[local], span] + own * factors[local][:, span]
                mean = jnp.mean(total * total, axis=0, keepdims=True)
                scale = lax.rsqrt(mean + 1e-05)
                mixed = (total * scale * gain_columns[local]).astype(BF16).T
                mixed_ref[place, span, local * LANES : (local + 1) * LANES] = mixed
            if sends:
                send(mixed_ref, place, relative, first, LANES)
    for copy in copies:
        copy.wait()


def last(
    total, acts, log, gains, columns, stats, node, level, levels, relatives, shards,
    done=None, whole=None, sends=True
):
    head_count, rows = log.shape
    share = head_count // shards
    done = done or {}
    operands = in_vmem(total, acts, log, gains, columns, stats, node, *done.values())
    specs = [VMEM_SPEC] * len(operands)
    aliases = {}
    if whole is not None:
        aliases = {len(operands): 0}
        operands += in_hbm(whole)
        specs.append(HBM_SPEC)
    mixed = pltpu.VMEM((len(relatives), rows, share * LANES), BF16)
    copies = len(done) + len(relatives) * rows // LANES
    out = jax.ShapeDtypeStruct((rows, head_count * LANES), BF16)
    return pl.pallas_call(
        functools.partial(
            last_kernel, level=level, relatives=relatives, done=tuple(done), sends=sends,
            shards=shards, base=gains.shape[0] // head_count - levels,
        ),
        in_specs=specs,
        out_specs=HBM_SPEC if sends else VMEM_SPEC,
        out_shape=out if sends else mixed,
        input_output_aliases=aliases,
        scratch_shapes=[mixed, pltpu.SemaphoreType.DMA((copies,))] if sends else [],
        compiler_params=params(),
        cost_estimate=small_cost(),
        name="last",
    )(*operands)


def moved(value, apart):
    return lax.ppermute(value, "seq", [(i, i ^ apart) for i in range(lax.axis_size("seq"))])


def onward(devices):
    route = {index: index + 1 for index in range(devices)}
    planes = devices // 4
    target = 0
    for plane in range(1, planes - 1):
        route[4 * plane + 2] = target
        target = 4 * plane + 3
    route[devices - 1] = target
    return list(route.items())


def on_device(xbc, conv_weight, log_decay, level_weights, gain):
    rows = xbc.shape[0]
    head_count = log_decay.shape[0]
    devices = lax.axis_size("seq")
    levels = devices.bit_length() - 1
    shards = 4
    part = head_count * LANES // shards
    gains = level_weights.transpose(1, 0, 2).reshape(-1, rows)
    beyond = onward(devices)
    early = head_count // 4
    values, taps, log, edge, acts, head, maps, state = load(xbc, conv_weight, log_decay, early)
    far_edge = lax.ppermute(edge, "seq", beyond)
    near_edge = moved(edge, 1)
    acts, head, state = front(values, taps, log, maps, acts, head, state, early)
    acts, maps, state, away, home = edge_rows(
        far_edge, near_edge, log, taps, values, head, acts, maps, state, shards
    )
    joined = moved(away, 1)
    first_node = jnp.concatenate([joined[: home.shape[0]], moved(home, 1)])
    own, stats, send, rest = pair(state, log, joined, shards)
    near_made = None
    all_stats = [stats]
    got = []
    for bit in range(1, levels - 1):
        got.append(moved(send, 1 << bit))
        if bit <= 2:
            half = head_count // 2
            heads = (half * (bit - 1), half * bit)
            near_made = near(
                acts, maps, log, gains, first_node, stats, gain, near_made, heads, shards
            )
        sources = [rest, *got[1:]] if bit == levels - 2 else []
        stats, send, own = join(own, stats, got[-1], near_made[0], bit, shards, sources)
        all_stats.append(stats)
    top = levels - 1

    node = moved(send, 1 << top)
    count = len(got)
    across = moved(own, 2)
    shared = (acts, log, gains, all_stats[:count])
    direct = [{0: (slot, 0)} for slot in range(count)]
    crossed = [{2: (0, slot * part)} for slot in range(count)]
    relayed = [{1: (slot, 0), 3: (count + slot, 0)} for slot in range(count)]
    total = middle(near_made[0], *shared, got, direct, (0,), levels, shards)
    node, total = lax.optimization_barrier((node, total))
    common = (acts, log, gains, near_made[3], all_stats[-1])
    node_across = moved(node, 2)
    mixed = last(total, *common, node, top, levels, (0,), shards)
    shares = [kept[:part] for kept in got]
    shares += [across[slot * part : (slot + 1) * part] for slot in range(count)]
    mixed, shares, total = lax.optimization_barrier((mixed, shares, total))
    beside = [moved(kept, 1) for kept in shares]
    total = middle(total, *shared, [across], crossed, (2,), levels, shards)
    node_across, beside, total = lax.optimization_barrier((node_across, beside, total))
    node_beside = moved(jnp.concatenate([node, node_across]), 1)
    total = middle(total, *shared, beside, relayed, (1, 3), levels, shards)
    done = {2: last(total, *common, node_across, top, levels, (2,), shards, sends=False)}
    return last(total, *common, node_beside, top, levels, (1, 3), shards, done, mixed)


def solution(mesh):
    in_specs = (
        P(("groups", "seq"), None),
        P(),
        P(None, ("groups", "seq")),
        P(None, None, ("groups", "seq")),
        P(),
    )
    out_specs = P(("groups", "seq"), None)
    return jax.shard_map(
        on_device, mesh=mesh, in_specs=in_specs, out_specs=out_specs, check_vma=False
    )
```
